128 devices in a mesh: azim: 16 (over x, y_hi, core), axial: 8 (over z, y_lo).
Axes of the slice: x: 4, y: 4 (y_hi: 2, y_lo: 2; y = y_hi * 2 + y_lo), z: 4, core: 2. Of those that a mesh axis runs over, the one named last changes fastest.
Arguments:
- populations: float32 [19, 128, 128, 256], P(None, 'azim', 'axial'), may hold values from 0.03 to 0.09
- fluid_flags: int32 [128, 128, 256], P('azim', 'axial'), may hold values 0 or 1
- wall_cell: int32 [65536], P(('azim', 'axial')), may hold values from 0 to 32767
- wall_drive: float32 [65536], P(('azim', 'axial')), may hold values from -6 to 6
- wall_owner: int32 [65536], P(('azim', 'axial')), may hold values from 0 to 127, as said below
- wall_slot: int32 [65536], P(('azim', 'axial')), may hold values from 0 to 7
- receive_cell: int32 [131072], P(('azim', 'axial')), may hold values from 0 to 65536, as said below
- materials: int32 [256, 128, 256], P('azim', 'axial'), may hold values from 0 to 3
- solid_temp: float32 [256, 128, 256], P('azim', 'axial'), may hold values from -6 to 6
Outputs:
- fluid_out: float32 [19, 128, 128, 256], P(None, 'azim', 'axial')
- solid_out: float32 [256, 128, 256], P('azim', 'axial')
The draws below stay inside these ranges and needn't reach their ends.
Inputs may be any that keep to these rules, and one draw needn't show every extreme that they name: `wall_cell`: index into the sending device's own fluid block, flattened with azimuth slowest and radius fastest. `wall_owner`: device index azim index * 8 + axial index. Rows of one device never share an (owner, slot) pair; some owner receives all 8 slots from every device. `receive_cell`: ordered by owner, then sender, then slot; equals 65536 exactly where the sender has no row for that owner and slot.
All inputs are finite; a program needn't handle non-finite values. No bound on the sum of `fluid_flags` on one device may be relied on, other than what follows from the above.
Results may differ from the reference program's by a relative error of at most 0.0003.
Values sent between devices are 32-bit elements; how exact they have to be, the bound alone decides.
No kernel may reach another device: no remote copies, remote signals or barrier semaphores. Data moves between devices by JAX's collectives and lax.ppermute only.
A program may use at most 128 MiB of HBM per device.

```python
import jax
import jax.numpy as jnp
from jax import lax

Q = 19
CA = 8
CZ = 16
NR = 256
STEPS = 2
SA = 16
SZ = 16
SR = 256
SWEEPS = 3
CAP = 8
NA = 128
NZ = 128
SNA = 256
SNZ = 128
W_DEV = 512
TOTAL_W = 65536
S_CELLS = 65536
N_AZIM = 16
N_AXIAL = 8


def routing(key):
    devices = N_AZIM * N_AXIAL
    positions = devices * CAP
    key_tier, key_full, key_noise = jax.random.split(key, 3)
    owner_ids = jnp.arange(devices, dtype=jnp.int32)
    tier = jax.random.randint(key_tier, (devices,), 0, 2, dtype=jnp.int32) * 8192
    full = jax.random.randint(key_full, (), 0, devices, dtype=jnp.int32)
    tier = jnp.where(owner_ids == devices - 1, 0, tier)
    tier = jnp.where(owner_ids == full, -16384, tier)
    noise = jax.random.randint(key_noise, (devices, positions), 0, 8192, dtype=jnp.int32)
    place = jnp.arange(positions, dtype=jnp.int32)
    score = (tier[place // CAP][None, :] + noise + 16384) * positions + place[None, :]
    order = jnp.argsort(score, axis=1)
    return order[:, :W_DEV].astype(jnp.int32)


def draw_wall_owner(key, part):
    chosen = routing(key)
    return (chosen // CAP).reshape(-1).astype(jnp.int32)


def draw_wall_slot(key, part):
    chosen = routing(key)
    return (chosen % CAP).reshape(-1).astype(jnp.int32)


def draw_receive_cell(key, part):
    chosen = routing(key)
    key = jax.random.fold_in(key, 7)
    devices = N_AZIM * N_AXIAL
    sender = jnp.broadcast_to(jnp.arange(devices, dtype=jnp.int32)[:, None], chosen.shape)
    live = jnp.zeros((devices, devices * CAP), jnp.int32).at[sender, chosen].set(1)
    live = jnp.transpose(live.reshape(devices, devices, CAP), (1, 0, 2))
    cells = jax.random.randint(key, (devices, devices, CAP), 0, S_CELLS, dtype=jnp.int32)
    return jnp.where(live > 0, cells, S_CELLS).reshape(-1).astype(jnp.int32)


def place_ends(array, key, smallest, top_value):
    longest = array.shape.index(max(array.shape))
    spots = []
    for shift in (0, 1):
        where = [jax.random.randint(jax.random.fold_in(key, axis), (), 0, length) for axis, length in enumerate(array.shape)]
        where[longest] = (where[longest] + shift) % array.shape[longest]
        spots.append(tuple(where))
    return array.at[spots[0]].set(smallest).at[spots[1]].set(top_value)


def shard_levels(key, shape, shards, least, largest):
    gain, own = 1.0, jax.random.fold_in(key, 6)
    for axis_at, parts in shards:
        steps = jnp.exp(jax.random.uniform(jax.random.fold_in(own, axis_at), (parts,), jnp.float32, least / len(shards), largest / len(shards)))
        gain = gain * jnp.repeat(steps, shape[axis_at] // parts).reshape([-1 if axis == axis_at else 1 for axis in range(len(shape))])
    return gain


def scatter_about(rng, dims, deviation, most, cuts=(), held_as=jnp.bfloat16):
    drawn = jax.random.normal(rng, dims, jnp.float32) * deviation
    if len(cuts) > 0:
        drawn = shard_levels(rng, dims, cuts, -0.22, 0.18) * drawn
    return jnp.clip(drawn, min=-most, max=most).astype(held_as)


def setup_inputs(seed: int = 0) -> dict:
    key_of = jax.random.split(jax.random.key(seed), 10)
    populations = jnp.clip(0.03 + 0.060000004 * jax.random.uniform(key_of[0], (Q, NA, NZ, NR), jnp.float32) ** shard_levels(key_of[0], (Q, NA, NZ, NR), ((1, 16), (2, 8)), -0.2, 0.2), 0.03, 0.09)
    fluid_flags = place_ends((jax.random.randint(key_of[1], (NA, NZ, NR), 0, 10) < 9).astype(jnp.int32), jax.random.fold_in(key_of[1], 1), 0, 1)
    wall_cell = place_ends(jax.random.randint(key_of[2], (TOTAL_W,), 0, CA * CZ * NR), jax.random.fold_in(key_of[2], 1), 0, (CA * CZ * NR) - 1).astype(jnp.int32)
    wall_drive = scatter_about(key_of[3], (TOTAL_W,), 1.0, 6.0, ((0, 128),), jnp.float32)
    wall_owner = draw_wall_owner(jax.random.fold_in(key_of[9], 71), 0)
    wall_slot = draw_wall_slot(jax.random.fold_in(key_of[9], 71), 0)
    receive_cell = draw_receive_cell(jax.random.fold_in(key_of[9], 71), 0)
    materials = place_ends(jax.random.randint(key_of[7], (SNA, SNZ, SR), 0, 4), jax.random.fold_in(key_of[7], 1), 0, 3).astype(jnp.int32)
    solid_temp = scatter_about(key_of[8], (SNA, SNZ, SR), 1.0, 6.0, ((0, 16), (1, 8)), jnp.float32)
    return dict(populations=populations, fluid_flags=fluid_flags, wall_cell=wall_cell, wall_drive=wall_drive, wall_owner=wall_owner, wall_slot=wall_slot, receive_cell=receive_cell, materials=materials, solid_temp=solid_temp)


WEIGHTS = [1.0 / 3.0] + [1.0 / 18.0] * 6 + [1.0 / 36.0] * 12
STEP_A = [0, 1, -1, 0, 0, 0, 0, 1, -1, 1, -1, 1, -1, 1, -1, 0, 0, 0, 0]
STEP_Z = [0, 0, 0, 1, -1, 0, 0, 1, -1, -1, 1, 0, 0, 0, 0, 1, -1, 1, -1]
STEP_R = [0, 0, 0, 0, 0, 1, -1, 0, 0, 0, 0, 1, -1, -1, 1, 1, -1, -1, 1]
OPPOSITE = [0, 2, 1, 4, 3, 6, 5, 8, 7, 10, 9, 12, 11, 14, 13, 16, 15, 18, 17]
RELAXATION = 1.25
SPEED_REF = 0.05
HEAT_CAPACITY = 6.5
CONDUCTIVITY = [1.0, 0.55, 0.2, 0.8]

def velocity_sum(popul, table):
    total = jnp.zeros(popul.shape[1:], popul.dtype)
    for which in range(19):
        if table[which] != 0:
            total = total + table[which] * popul[which]
    return total

def collide(popul, flags):
    density = lax.optimization_barrier(jnp.sum(popul, axis=0))
    fluid = flags > 0
    safe = jnp.where(fluid, density, 1.0)
    vel_a = velocity_sum(popul, STEP_A) / safe
    vel_z = velocity_sum(popul, STEP_Z) / safe
    vel_r = velocity_sum(popul, STEP_R) / safe
    square = vel_a * vel_a + vel_z * vel_z + vel_r * vel_r
    relaxed = []
    for which in range(19):
        proj = STEP_A[which] * vel_a + STEP_Z[which] * vel_z + STEP_R[which] * vel_r
        equil = WEIGHTS[which] * density * (1.0 + 3.0 * proj + 4.5 * proj * proj - 1.5 * square)
        relaxed.append(popul[which] + RELAXATION * (equil - popul[which]))
    return jnp.where(fluid[None], jnp.stack(relaxed), popul)

def propagate(post, flags):
    span_a = post.shape[1] - 2
    span_z = post.shape[2] - 2
    span_r = post.shape[3]
    padded = jnp.pad(post, ((0, 0), (0, 0), (0, 0), (1, 1)))
    padded_flags = jnp.pad(flags, ((0, 0), (0, 0), (1, 1)))
    moved = []
    for which in range(19):
        start_a = 1 - STEP_A[which]
        start_z = 1 - STEP_Z[which]
        start_r = 1 - STEP_R[which]
        source = padded[which, start_a:start_a + span_a, start_z:start_z + span_z, start_r:start_r + span_r]
        open_src = padded_flags[start_a:start_a + span_a, start_z:start_z + span_z, start_r:start_r + span_r]
        own = post[OPPOSITE[which], 1:-1, 1:-1, :]
        moved.append(jnp.where(open_src > 0, source, own))
    return jnp.stack(moved)

def wall_flux(rows, drive):
    density = lax.optimization_barrier(jnp.sum(rows, axis=0))
    vel_a = velocity_sum(rows, STEP_A) / density
    vel_z = velocity_sum(rows, STEP_Z) / density
    vel_r = velocity_sum(rows, STEP_R) / density
    speed = jnp.sqrt(vel_a * vel_a + vel_z * vel_z + vel_r * vel_r + 1e-06)
    return drive * (0.2 + speed / SPEED_REF)

def conductivity(materials):
    total = jnp.zeros(materials.shape, jnp.float32)
    for which in range(4):
        total = total + jnp.where(materials == which, CONDUCTIVITY[which], 0.0).astype(jnp.float32)
    return total

def face_conductance(first, second):
    joined = first + second
    return jnp.where(joined > 0, 2.0 * first * second / jnp.where(joined > 0, joined, 1.0), 0.0)

def window(arr, off_a, off_z, off_r):
    return arr[1 + off_a:arr.shape[0] - 1 + off_a, 1 + off_z:arr.shape[1] - 1 + off_z, 1 + off_r:arr.shape[2] - 1 + off_r]

def heat_divergence(temp, cond):
    temp_pad = jnp.pad(temp, ((0, 0), (0, 0), (1, 1)))
    cond_pad = jnp.pad(cond, ((0, 0), (0, 0), (1, 1)))
    center = window(temp_pad, 0, 0, 0)
    cond_mid = window(cond_pad, 0, 0, 0)
    total = jnp.zeros(center.shape, center.dtype)
    for offsets in ((1, 0, 0), (-1, 0, 0), (0, 1, 0), (0, -1, 0), (0, 0, 1), (0, 0, -1)):
        neigh = window(temp_pad, offsets[0], offsets[1], offsets[2])
        link = face_conductance(cond_mid, window(cond_pad, offsets[0], offsets[1], offsets[2]))
        total = total + link * (neigh - center)
    return total

def extend(arr, lead):
    wrap_pad = [(0, 0)] * arr.ndim
    wrap_pad[lead] = (1, 1)
    zero_pad = [(0, 0)] * arr.ndim
    zero_pad[lead + 1] = (1, 1)
    return jnp.pad(jnp.pad(arr, wrap_pad, mode='wrap'), zero_pad)

def reference(populations, fluid_flags, wall_cell, wall_drive, wall_owner, wall_slot, receive_cell, materials, solid_temp):
    devices = N_AZIM * N_AXIAL
    popul = populations
    flag_ext = extend(fluid_flags, 0)
    for step_index in range(STEPS):
        post = collide(popul, fluid_flags)
        popul = propagate(extend(post, 1), flag_ext)
    blocks = popul.reshape(Q, N_AZIM, CA, N_AXIAL, CZ, NR).transpose(1, 3, 0, 2, 4, 5).reshape(devices, Q, CA * CZ * NR)
    cells = jnp.broadcast_to(wall_cell.reshape(devices, 1, W_DEV), (devices, Q, W_DEV))
    rows = jnp.moveaxis(jnp.take_along_axis(blocks, cells, axis=2), 1, 0)
    flux = wall_flux(rows, wall_drive.reshape(devices, W_DEV))
    sender = jnp.broadcast_to(jnp.arange(devices, dtype=jnp.int32)[:, None], (devices, W_DEV))
    buffers = jnp.zeros((devices, devices, CAP), jnp.float32).at[sender, wall_owner.reshape(devices, W_DEV), wall_slot.reshape(devices, W_DEV)].set(flux)
    arrived = jnp.transpose(buffers, (1, 0, 2)).reshape(devices, devices * CAP)
    owner = jnp.broadcast_to(jnp.arange(devices, dtype=jnp.int32)[:, None], (devices, devices * CAP))
    deposit = jnp.zeros((devices, S_CELLS + 1), jnp.float32).at[owner, receive_cell.reshape(devices, devices * CAP)].add(arrived)
    deposit = deposit[:, :S_CELLS].reshape(N_AZIM, N_AXIAL, SA, SZ, SR).transpose(0, 2, 1, 3, 4).reshape(SNA, SNZ, SR)
    cond_ext = extend(conductivity(materials), 0)
    temp = solid_temp
    for sweep_index in range(SWEEPS):
        temp = temp + (heat_divergence(extend(temp, 0), cond_ext) + deposit) / HEAT_CAPACITY
    return (popul, temp)
```

```python
import functools
import itertools

import jax
import jax.numpy as jnp
from jax import lax
from jax.experimental import pallas as pl
from jax.experimental.pallas import tpu as pltpu
from jax.sharding import PartitionSpec as P

CAP = 8
STEP_A = [0, 1, -1, 0, 0, 0, 0, 1, -1, 1, -1, 1, -1, 1, -1, 0, 0, 0, 0]
STEP_Z = [0, 0, 0, 1, -1, 0, 0, 1, -1, -1, 1, 0, 0, 0, 0, 1, -1, 1, -1]
STEP_R = [0, 0, 0, 0, 0, 1, -1, 0, 0, 0, 0, 1, -1, -1, 1, 1, -1, -1, 1]
OPPOSITE = [0, 2, 1, 4, 3, 6, 5, 8, 7, 10, 9, 12, 11, 14, 13, 16, 15, 18, 17]
AZIM_UP = [i for i in range(19) if STEP_A[i] == 1]
AZIM_DOWN = [i for i in range(19) if STEP_A[i] == -1]
AXIAL_UP = [i for i in range(19) if STEP_Z[i] == 1]
AXIAL_DOWN = [i for i in range(19) if STEP_Z[i] == -1]
RELAXATION = 1.25
SPEED_REF = 0.05
HEAT_CAPACITY = 6.5

Q = 19
CA, CZ, NR = 8, 16, 256
SA, SZ = 16, 16
HALVES = (0, 1)
ROWS = 32

FLAG_PLANE = 24
TEMP_PLANE = 26
COND_PLANE = 29
CELL_ROW = 512
AZIM_ROWS = 520
PER_PLACE = 26
TEMP_ROW = 312
COND_ROW = 378
TAIL_ROW = 448
AXIAL_ROWS = 464

VMEM = pltpu.VMEM
f32 = jnp.float32
bf16 = jnp.bfloat16


def lanes(half):
    return pl.ds(128 * half, 128)


def moments(f):
    rho = f[0]
    for i in range(1, Q):
        rho = rho + f[i]
    d = [f[i] - f[i + 1] for i in range(1, Q, 2)]
    mom_a = d[0] + d[3] + d[4] + d[5] + d[6]
    mom_z = d[1] + d[3] - d[4] + d[7] + d[8]
    mom_r = d[2] + d[5] - d[6] + d[7] - d[8]
    return rho, mom_a, mom_z, mom_r


def collide(f, flag):
    rho, mom_a, mom_z, mom_r = moments(f)
    open_cell = flag > 0
    inv = 1.0 / jnp.where(open_cell, rho, 1.0)
    omega = jnp.where(open_cell, RELAXATION, 0.0)
    keep = 1.0 - omega
    ua, uz, ur = mom_a * inv, mom_z * inv, mom_r * inv
    base = 1.0 - 1.5 * (ua * ua + uz * uz + ur * ur)
    scale = omega * rho
    face, edge = scale * (1.0 / 18.0), scale * (1.0 / 36.0)
    post = [keep * f[0] + scale * (1.0 / 3.0) * base]
    for n, proj in enumerate(
        (ua, uz, ur, ua + uz, ua - uz, ua + ur, ua - ur, uz + ur, uz - ur)
    ):
        weight = face if n < 3 else edge
        even = weight * (base + 4.5 * proj * proj)
        odd = weight * (3.0 * proj)
        post.append(keep * f[2 * n + 1] + (even + odd))
        post.append(keep * f[2 * n + 2] + (even - odd))
    return post


def conductivity(material):
    return jnp.where(
        material == 0,
        1.0,
        jnp.where(material == 1, 0.55, jnp.where(material == 2, 0.2, 0.8)),
    ).astype(f32)


def by_parity(axis, body, near, far):
    odd = lax.rem(lax.axis_index(axis), 2) == 1

    @pl.when(odd)
    def _():
        body(near, far)

    @pl.when(jnp.logical_not(odd))
    def _():
        body(far, near)


def first_kernel(f, flags, temp, mat, cells, post, near, far, low, high):
    def layer(a, carry):
        for half in HALVES:
            for part in (0, 1):
                rows = pl.ds(8 * part, 8)
                flag = flags[a, rows, lanes(half)].astype(f32)
                out = collide([f[i, a, rows, lanes(half)] for i in range(Q)], flag)
                for i in range(Q):
                    post[i, a, rows, lanes(half)] = out[i]
                place = (a + 2) * PER_PLACE
                target, inner, edge, near_edge = (
                    (low, AXIAL_DOWN, 0, 1) if part == 0 else (high, AXIAL_UP, 7, 6)
                )
                for i in range(Q):
                    target[half, pl.ds(place + i, 1), :] = out[i][edge : edge + 1]
                for n, i in enumerate(inner):
                    target[half, pl.ds(place + Q + n, 1), :] = out[i][
                        near_edge : near_edge + 1
                    ]
                target[half, pl.ds(place + 24, 1), :] = flag[edge : edge + 1]
                target[half, pl.ds(place + 25, 1), :] = flag[
                    near_edge : near_edge + 1
                ]
        return carry

    lax.fori_loop(0, CA, layer, 0)

    def solid_layer(a, carry):
        for half in HALVES:
            for part, target in ((0, low), (1, high)):
                rows = pl.ds(8 * part, 8)
                t = temp[a, rows, lanes(half)]
                c = conductivity(mat[a, rows, lanes(half)])
                for depth in range(3):
                    at = depth if part == 0 else 7 - depth
                    target[half, pl.ds(TEMP_ROW + depth * 22 + 3 + a, 1), :] = t[
                        at : at + 1
                    ]
                    target[half, pl.ds(COND_ROW + depth * 22 + 3 + a, 1), :] = c[
                        at : at + 1
                    ]
        return carry

    lax.fori_loop(0, SA, solid_layer, 0)
    rc = cells[...].astype(f32)
    low[0, pl.ds(TAIL_ROW, 8), :] = rc
    high[0, pl.ds(TAIL_ROW, 8), :] = rc

    def fill(down, up):
        for target, outer, second, moving, solid in (
            (down, 0, 1, AZIM_DOWN, (0, 1, 2)),
            (up, 7, 6, AZIM_UP, (15, 14, 13)),
        ):
            for half in HALVES:
                for i in range(Q):
                    target[half, pl.ds(16 * i, 16), :] = post[i, outer, :, lanes(half)]
                for n, i in enumerate(moving):
                    target[half, pl.ds(16 * (Q + n), 16), :] = post[
                        i, second, :, lanes(half)
                    ]
                for n, a in enumerate((outer, second)):
                    target[half, pl.ds(16 * (FLAG_PLANE + n), 16), :] = flags[
                        a, :, lanes(half)
                    ].astype(f32)
                for depth, a in enumerate(solid):
                    target[half, pl.ds(16 * (TEMP_PLANE + depth), 16), :] = temp[
                        a, :, lanes(half)
                    ]
                    target[half, pl.ds(16 * (COND_PLANE + depth), 16), :] = (
                        conductivity(mat[a, :, lanes(half)])
                    )
            target[0, pl.ds(CELL_ROW, 8), :] = rc

    by_parity("azim", fill, near, far)


def axial_kernel(near_in, far_in, low_in, high_in, near, far):
    def pass_on(lower, upper):
        def fill(down, up):
            down[...] = low_in[...]
            up[...] = high_in[...]
            for half, (target, edge, near_edge, inner, solid) in itertools.product(
                HALVES,
                (
                    (down, 0, 1, AXIAL_DOWN, (0, 1, 2)),
                    (up, 15, 14, AXIAL_UP, (15, 14, 13)),
                ),
            ):
                for source, moving, first, second, layers in (
                    (lower, AZIM_UP, -1, -2, (-1, -2, -3)),
                    (upper, AZIM_DOWN, 8, 9, (16, 17, 18)),
                ):

                    def put(row, plane, z):
                        target[half, pl.ds(row, 1), :] = source[
                            half, pl.ds(16 * plane + z, 1), :
                        ]

                    place = (first + 2) * PER_PLACE
                    for i in range(Q):
                        put(place + i, i, edge)
                    for n, i in enumerate(inner):
                        put(place + Q + n, i, near_edge)
                    put(place + 24, FLAG_PLANE, edge)
                    put(place + 25, FLAG_PLANE, near_edge)
                    place = (second + 2) * PER_PLACE
                    for n, i in enumerate(moving):
                        put(place + i, Q + n, edge)
                        if i in inner:
                            put(place + Q + inner.index(i), Q + n, near_edge)
                    put(place + 24, FLAG_PLANE + 1, edge)
                    put(place + 25, FLAG_PLANE + 1, near_edge)
                    for n, a in enumerate(layers):
                        for depth, z in enumerate(solid):
                            put(TEMP_ROW + depth * 22 + 3 + a, TEMP_PLANE + n, z)
                            put(COND_ROW + depth * 22 + 3 + a, COND_PLANE + n, z)
            for target in (down, up):
                target[1, pl.ds(TAIL_ROW, 8), :] = lower[0, pl.ds(CELL_ROW, 8), :]
                target[0, pl.ds(TAIL_ROW + 8, 8), :] = upper[0, pl.ds(CELL_ROW, 8), :]

        by_parity("axial", fill, near, far)

    by_parity("azim", pass_on, near_in, far_in)


def ends(n_axial):
    z = lax.axis_index("axial")
    return (
        jnp.where(z > 0, 1.0, 0.0).astype(f32),
        jnp.where(z < n_axial - 1, 1.0, 0.0).astype(f32),
    )


def shifted(pair, step, lane):
    if step == 0:
        return pair
    turn = 1 if step == 1 else 127
    at = 0 if step == 1 else 127
    a, b = (pltpu.roll(x, turn, 1) for x in pair)
    return [jnp.where(lane == at, b, a), jnp.where(lane == at, a, b)]


def split3(x):
    one = x.astype(bf16)
    rest = x - one.astype(f32)
    two = rest.astype(bf16)
    return one, two, (rest - two.astype(f32)).astype(bf16)


def stream(source, opened, at_a, flag_a, row, lane):
    rows = pl.ds(row, 8)
    out = [[], []]
    for i in range(Q):
        own = OPPOSITE[i]
        moved = shifted(
            [
                source[i, at_a - STEP_A[i], half, pl.ds(row - STEP_Z[i], 8), :]
                for half in HALVES
            ],
            STEP_R[i],
            lane,
        )
        for half in HALVES:
            if i == 0:
                out[half].append(moved[half])
                continue
            mask = opened[
                STEP_R[i] % 3,
                flag_a - STEP_A[i],
                half,
                pl.ds(row - STEP_Z[i], 8),
                :,
            ]
            out[half].append(
                jnp.where(mask > 0, moved[half], source[own, at_a, half, rows, :])
            )
    return out


def fluid_kernel(
    n_azim,
    n_axial,
    post,
    flags,
    near_a,
    far_a,
    near_z,
    far_z,
    cell,
    drive,
    owner,
    slot,
    fluid_out,
    message,
    ext,
    opened,
    second,
    speeds,
):
    lane = lax.broadcasted_iota(jnp.int32, (8, 128), 1)

    def own_layer(a, carry):
        for half in HALVES:
            for part in (0, 1):
                rows = pl.ds(8 * part, 8)
                to = pl.ds(8 + 8 * part, 8)
                for i in range(Q):
                    ext[i, a + 2, half, to, :] = post[i, a, rows, lanes(half)]
                opened[0, a + 2, half, to, :] = flags[a, rows, lanes(half)].astype(f32)
        return carry

    lax.fori_loop(0, CA, own_layer, 0)

    def azim_rim(lower, upper):
        for half in HALVES:
            for source, first, last, moving in (
                (lower, 1, 0, AZIM_UP),
                (upper, 10, 11, AZIM_DOWN),
            ):
                to = pl.ds(8, 16)
                for i in range(Q):
                    ext[i, first, half, to, :] = source[half, pl.ds(16 * i, 16), :]
                for n, i in enumerate(moving):
                    ext[i, last, half, to, :] = source[half, pl.ds(16 * (Q + n), 16), :]
                opened[0, first, half, to, :] = source[half, pl.ds(16 * FLAG_PLANE, 16), :]
                opened[0, last, half, to, :] = source[half, pl.ds(16 * (FLAG_PLANE + 1), 16), :]

    by_parity("azim", azim_rim, near_a, far_a)
    below, above = ends(n_axial)

    def axial_rim(lower, upper):
        def layer(a, carry):
            place = a * PER_PLACE
            for half in HALVES:
                for source, first, last, moving, there in (
                    (lower, 7, 6, AXIAL_UP, below),
                    (upper, 24, 25, AXIAL_DOWN, above),
                ):
                    for i in range(Q):
                        ext[i, a, half, pl.ds(first, 1), :] = source[half, pl.ds(place + i, 1), :]
                    for n, i in enumerate(moving):
                        ext[i, a, half, pl.ds(last, 1), :] = source[half, pl.ds(place + Q + n, 1), :]
                    opened[0, a, half, pl.ds(first, 1), :] = (
                        source[half, pl.ds(place + 24, 1), :] * there
                    )
                    opened[0, a, half, pl.ds(last, 1), :] = (
                        source[half, pl.ds(place + 25, 1), :] * there
                    )
            return carry

        lax.fori_loop(0, CA + 4, layer, 0)

    by_parity("axial", axial_rim, near_z, far_z)

    def turn(a, carry):
        for part in range(4):
            rows = pl.ds(8 * part, 8)
            pair = [opened[0, a, half, rows, :] for half in HALVES]
            up = shifted(pair, 1, lane)
            down = shifted(pair, -1, lane)
            opened[1, a, 0, rows, :] = jnp.where(lane == 0, 0.0, up[0])
            opened[1, a, 1, rows, :] = up[1]
            opened[2, a, 0, rows, :] = down[0]
            opened[2, a, 1, rows, :] = jnp.where(lane == 127, 0.0, down[1])
        return carry

    lax.fori_loop(0, CA + 4, turn, 0)

    def first_step(a, carry):
        for row in (7, 15, 23):
            moved = stream(ext, opened, a + 1, a + 1, row, lane)
            for half in HALVES:
                out = collide(moved[half], opened[0, a + 1, half, pl.ds(row, 8), :])
                for i in range(Q):
                    second[i, a, half, pl.ds(row, 8), :] = out[i]
        return carry

    lax.fori_loop(0, CA + 2, first_step, 0)

    def second_step(a, carry):
        for part in (0, 1):
            moved = stream(second, opened, a + 1, a + 2, 8 + 8 * part, lane)
            for half in HALVES:
                for i in range(Q):
                    fluid_out[i, a, pl.ds(8 * part, 8), lanes(half)] = moved[half][i]
                rho, mom_a, mom_z, mom_r = moments(moved[half])
                inv = 1.0 / rho
                ua, uz, ur = mom_a * inv, mom_z * inv, mom_r * inv
                speeds[pl.ds(a * CZ + 8 * part, 8), lanes(half)] = jnp.sqrt(
                    ua * ua + uz * uz + ur * ur + 1e-06
                )
        return carry

    lax.fori_loop(0, CA, second_step, 0)

    rows_here = cell.shape[1]
    place = cell[...]
    row_hot = (
        lax.broadcasted_iota(jnp.int32, (CA * CZ, rows_here), 0) == place // NR
    ).astype(f32).astype(bf16)
    turned = jnp.transpose(speeds[...])
    picked = jnp.zeros((NR, rows_here), f32)
    for term in split3(turned):
        picked = picked + jnp.dot(term, row_hot, preferred_element_type=f32)
    column = lax.broadcasted_iota(jnp.int32, (NR, rows_here), 0) == place % NR
    speed = jnp.sum(jnp.where(column, picked, 0.0), axis=0, keepdims=True)
    flux = drive[...] * (0.2 + speed / SPEED_REF)
    devices = n_azim * n_axial
    owner_hot = (
        lax.broadcasted_iota(jnp.int32, (devices, rows_here), 0) == owner[...]
    ).astype(f32).astype(bf16)
    slotted = jnp.where(
        lax.broadcasted_iota(jnp.int32, (128, rows_here), 0) == slot[...], flux, 0.0
    )
    sent = jnp.zeros((devices, 128), f32)
    for term in split3(slotted):
        sent = sent + lax.dot_general(
            owner_hot, term, (((1,), (1,)), ((), ())), preferred_element_type=f32
        )
    total = jnp.zeros((devices, 128), f32)
    for da in (-1, 0, 1):
        for dz in (-1, 0, 1):
            which = (da + 1) * 3 + dz + 1
            back = (-(da * n_axial + dz)) % devices
            moved = pltpu.roll(sent, back, 0) if back else sent
            total = total + (pltpu.roll(moved, CAP * which, 1) if which else moved)
    for o in range(devices):
        message[o, :, :] = total[o : o + 1]


def link(first, second):
    joined = first + second
    good = joined > 0
    return jnp.where(
        good,
        (2.0 / HEAT_CAPACITY) * first * second / jnp.where(good, joined, 1.0),
        0.0,
    )


def sweep(source, link_a, link_z, link_r, keep, a, row, lane):
    rows = pl.ds(row, 8)
    pair = [source[a, half, rows, :] for half in HALVES]
    lr = [link_r[a, half, rows, :] for half in HALVES]
    up = shifted(pair, -1, lane)
    down = shifted([x * y for x, y in zip(pair, lr)], 1, lane)
    out = []
    for half in HALVES:
        total = keep[a, half, rows, :] * pair[half]
        total = total + link_a[a, half, rows, :] * source[a + 1, half, rows, :]
        total = total + link_a[a - 1, half, rows, :] * source[a - 1, half, rows, :]
        total = (
            total + link_z[a, half, rows, :] * source[a, half, pl.ds(row + 1, 8), :]
        )
        total = (
            total
            + link_z[a, half, pl.ds(row - 1, 8), :]
            * source[a, half, pl.ds(row - 1, 8), :]
        )
        out.append(total + lr[half] * up[half] + down[half])
    return out


def solid_kernel(
    n_axial,
    temp,
    mat,
    near_a,
    far_a,
    near_z,
    far_z,
    swept,
    link_a,
    link_z,
    link_r,
    keep,
    ext,
    cond,
    other,
):
    lane = lax.broadcasted_iota(jnp.int32, (8, 128), 1)

    def own_layer(a, carry):
        for half in HALVES:
            for part in (0, 1):
                rows = pl.ds(8 * part, 8)
                to = pl.ds(8 + 8 * part, 8)
                ext[a + 3, half, to, :] = temp[a, rows, lanes(half)]
                cond[a + 3, half, to, :] = conductivity(mat[a, rows, lanes(half)])
        return carry

    lax.fori_loop(0, SA, own_layer, 0)

    def azim_rim(lower, upper):
        for half in HALVES:
            for depth in range(3):
                for source, a in ((lower, 2 - depth), (upper, 19 + depth)):
                    ext[a, half, pl.ds(8, 16), :] = source[half, pl.ds(16 * (TEMP_PLANE + depth), 16), :]
                    cond[a, half, pl.ds(8, 16), :] = source[half, pl.ds(16 * (COND_PLANE + depth), 16), :]

    by_parity("azim", azim_rim, near_a, far_a)
    below, above = ends(n_axial)

    def axial_rim(lower, upper):
        def layer(a, carry):
            for half in HALVES:
                for depth in range(3):
                    for source, row, there in (
                        (lower, 7 - depth, below),
                        (upper, 24 + depth, above),
                    ):
                        ext[a, half, pl.ds(row, 1), :] = source[half, pl.ds(TEMP_ROW + depth * 22 + a, 1), :]
                        cond[a, half, pl.ds(row, 1), :] = (
                            source[half, pl.ds(COND_ROW + depth * 22 + a, 1), :]
                            * there
                        )
            return carry

        lax.fori_loop(0, SA + 6, layer, 0)

    by_parity("axial", axial_rim, near_z, far_z)

    def links(a, carry):
        for row in (5, 13, 21):
            rows = pl.ds(row, 8)
            pair = [cond[a, half, rows, :] for half in HALVES]
            up = shifted(pair, -1, lane)
            up = [up[0], jnp.where(lane == 127, 0.0, up[1])]
            for half in HALVES:
                link_a[a, half, rows, :] = link(pair[half], cond[a + 1, half, rows, :])
                link_z[a, half, rows, :] = link(
                    pair[half], cond[a, half, pl.ds(row + 1, 8), :]
                )
                link_r[a, half, rows, :] = link(pair[half], up[half])
        return carry

    lax.fori_loop(0, SA + 5, links, 0)

    def keeps(a, carry):
        for row in (6, 14, 22):
            rows = pl.ds(row, 8)
            pair = [link_r[a, half, rows, :] for half in HALVES]
            down = shifted(pair, 1, lane)
            for half in HALVES:
                keep[a, half, rows, :] = 1.0 - (
                    link_a[a, half, rows, :]
                    + link_a[a - 1, half, rows, :]
                    + link_z[a, half, rows, :]
                    + link_z[a, half, pl.ds(row - 1, 8), :]
                    + pair[half]
                    + down[half]
                )
        return carry

    lax.fori_loop(1, SA + 5, keeps, 0)

    def once(source, target, first, last, at):
        def layer(a, carry):
            for row in at:
                out = sweep(source, link_a, link_z, link_r, keep, a, row, lane)
                for half in HALVES:
                    target[a, half, pl.ds(row, 8), :] = out[half]
            return carry

        lax.fori_loop(first, last, layer, 0)

    once(ext, other, 1, SA + 5, (6, 14, 22))
    once(other, ext, 2, SA + 4, (7, 15, 23))

    def final(a, carry):
        for part in (0, 1):
            out = sweep(ext, link_a, link_z, link_r, keep, a + 3, 8 + 8 * part, lane)
            for half in HALVES:
                swept[a, pl.ds(8 * part, 8), lanes(half)] = out[half]
        return carry

    lax.fori_loop(0, SA, final, 0)


def deposit_kernel(
    n_axial,
    arrived,
    cells,
    near_a,
    far_a,
    near_z,
    far_z,
    swept,
    link_a,
    link_z,
    link_r,
    keep,
    solid_out,
    heat,
    other,
    rim_cells,
    came,
):
    lane = lax.broadcasted_iota(jnp.int32, (8, 128), 1)
    senders = arrived.shape[0]
    for s in range(senders):
        came[pl.ds(s, 1), :] = arrived[s]

    def clear(a, carry):
        for half in HALVES:
            heat[a, half] = jnp.zeros((ROWS, 128), f32)
        return carry

    lax.fori_loop(0, SA + 6, clear, 0)

    rim_cells[4] = cells[...]

    def azim_cells(lower, upper):
        rim_cells[1] = lower[0, pl.ds(CELL_ROW, 8), :].astype(jnp.int32)
        rim_cells[7] = upper[0, pl.ds(CELL_ROW, 8), :].astype(jnp.int32)

    by_parity("azim", azim_cells, near_a, far_a)
    below, above = ends(n_axial)

    def axial_cells(lower, upper):
        for source, dz, there in ((lower, 0, below), (upper, 2, above)):
            for which, row, half in (
                (3, TAIL_ROW, 0),
                (0, TAIL_ROW, 1),
                (6, TAIL_ROW + 8, 0),
            ):
                got = source[half, pl.ds(row, 8), :].astype(jnp.int32)
                rim_cells[which + dz] = jnp.where(there > 0, got, SA * SZ * NR)

    by_parity("axial", axial_cells, near_z, far_z)

    values = jnp.transpose(came[...]) * (1.0 / HEAT_CAPACITY)

    def place(which, rows, row_of):
        cell = rim_cells[which]
        value = values[CAP * which : CAP * (which + 1)]
        one, two, three = split3(value)
        at_row = row_of(lax.broadcasted_iota(jnp.int32, (rows, senders), 0))
        at_col = lax.broadcasted_iota(jnp.int32, (NR, senders), 0)
        left, right = [[], [], []], []
        for c in range(CAP):
            hit = at_row == (cell[c : c + 1] // NR)
            for to, term in zip(left, (one, two, three)):
                to.append(
                    jnp.where(hit, term[c : c + 1].astype(f32), 0.0).astype(bf16)
                )
            right.append((at_col == cell[c : c + 1] % NR).astype(f32).astype(bf16))
        right = jnp.concatenate(right, axis=1)
        total = None
        for to in left:
            part = lax.dot_general(
                jnp.concatenate(to, axis=1),
                right,
                (((1,), (1,)), ((), ())),
                preferred_element_type=f32,
            )
            total = part if total is None else total + part
        return total

    own = place(4, SA * SZ, lambda j: j)
    for a in range(SA):
        for half in HALVES:
            heat[a + 3, half, pl.ds(8, 16), :] = own[
                16 * a : 16 * a + 16, 128 * half : 128 * half + 128
            ]
    low = place(1, 32, lambda j: j + 14 * SZ)
    high = place(7, 32, lambda j: j)
    for n in range(2):
        for half in HALVES:
            cut = slice(128 * half, 128 * half + 128)
            heat[1 + n, half, pl.ds(8, 16), :] = low[16 * n : 16 * n + 16, cut]
            heat[19 + n, half, pl.ds(8, 16), :] = high[16 * n : 16 * n + 16, cut]
    low = place(3, 32, lambda j: (j // 2) * SZ + 14 + j % 2)
    high = place(5, 32, lambda j: (j // 2) * SZ + j % 2)
    for a in range(SA):
        for half in HALVES:
            cut = slice(128 * half, 128 * half + 128)
            heat[a + 3, half, pl.ds(6, 2), :] = low[2 * a : 2 * a + 2, cut]
            heat[a + 3, half, pl.ds(24, 2), :] = high[2 * a : 2 * a + 2, cut]
    for which, cell_row, a, row in (
        (0, 255, 2, 7),
        (2, 240, 2, 24),
        (6, 15, 19, 7),
        (8, 0, 19, 24),
    ):
        one = place(which, 8, lambda j: jnp.where(j == 0, cell_row, -1))
        for half in HALVES:
            heat[a, half, pl.ds(row, 1), :] = one[0:1, 128 * half : 128 * half + 128]

    def middle(a, carry):
        for row in (7, 15, 23):
            out = sweep(heat, link_a, link_z, link_r, keep, a, row, lane)
            for half in HALVES:
                other[a, half, pl.ds(row, 8), :] = (
                    out[half] + heat[a, half, pl.ds(row, 8), :]
                )
        return carry

    lax.fori_loop(2, SA + 4, middle, 0)

    def final(a, carry):
        for part in (0, 1):
            rows = pl.ds(8 * part, 8)
            out = sweep(other, link_a, link_z, link_r, keep, a + 3, 8 + 8 * part, lane)
            for half in HALVES:
                solid_out[a, rows, lanes(half)] = (
                    out[half]
                    + heat[a + 3, half, pl.ds(8 + 8 * part, 8), :]
                    + swept[a, rows, lanes(half)]
                )
        return carry

    lax.fori_loop(0, SA, final, 0)


def call(kernel, ins, outs, scratch=(), limit=48, flops=0, moved=0):
    return pl.pallas_call(
        kernel,
        out_shape=[jax.ShapeDtypeStruct(s, f32) for s in outs],
        in_specs=[pl.BlockSpec(memory_space=VMEM)] * ins,
        out_specs=[pl.BlockSpec(memory_space=VMEM)] * len(outs),
        scratch_shapes=list(scratch),
        compiler_params=pltpu.CompilerParams(vmem_limit_bytes=limit * 1024 * 1024),
        cost_estimate=pl.CostEstimate(
            flops=flops, bytes_accessed=moved, transcendentals=0
        ),
    )


def swap(values, axis, far):
    count = lax.axis_size(axis)
    pairs = [(i, (((i + 1) ^ 1) - 1) % count if far else i ^ 1) for i in range(count)]
    return lax.ppermute(values, axis, pairs)


def per_device(
    n_azim,
    n_axial,
    populations,
    fluid_flags,
    wall_cell,
    wall_drive,
    wall_owner,
    wall_slot,
    receive_cell,
    materials,
    solid_temp,
):
    devices = n_azim * n_axial
    cells = receive_cell.reshape(devices, CAP).T
    azim_msg = (2, AZIM_ROWS, 128)
    axial_msg = (2, AXIAL_ROWS, 128)
    post, near, far, low, high = call(
        first_kernel,
        5,
        [(Q, CA, CZ, NR), azim_msg, azim_msg, axial_msg, axial_msg],
        moved=8 << 20,
    )(populations, fluid_flags, solid_temp, materials, cells)
    far_a = swap(far, "azim", True)
    near_a = swap(near, "azim", False)
    near, far = call(axial_kernel, 4, [axial_msg, axial_msg], moved=4 << 20)(
        near_a, far_a, low, high
    )
    far_z = swap(far, "axial", True)
    near_z = swap(near, "axial", False)
    rows = wall_cell.shape[0]
    fluid_out, message = call(
        functools.partial(fluid_kernel, n_azim, n_axial),
        10,
        [(Q, CA, CZ, NR), (devices, 1, 128)],
        [
            VMEM((Q, CA + 4, 2, ROWS, 128), f32),
            VMEM((3, CA + 4, 2, ROWS, 128), f32),
            VMEM((Q, CA + 2, 2, ROWS, 128), f32),
            VMEM((CA * CZ, NR), f32),
        ],
        moved=16 << 20,
    )(
        post,
        fluid_flags,
        near_a,
        far_a,
        near_z,
        far_z,
        wall_cell.reshape(1, rows),
        wall_drive.reshape(1, rows),
        wall_owner.reshape(1, rows),
        wall_slot.reshape(1, rows),
    )
    arrived = lax.all_to_all(
        message, ("azim", "axial"), split_axis=0, concat_axis=0, tiled=True
    )
    solid_ext = (SA + 6, 2, ROWS, 128)
    swept, *links = call(
        functools.partial(solid_kernel, n_axial),
        6,
        [(SA, SZ, NR)] + [solid_ext] * 4,
        [VMEM(solid_ext, f32)] * 3,
        moved=8 << 20,
    )(solid_temp, materials, near_a, far_a, near_z, far_z)
    (solid_out,) = call(
        functools.partial(deposit_kernel, n_axial),
        11,
        [(SA, SZ, NR)],
        [
            VMEM(solid_ext, f32),
            VMEM(solid_ext, f32),
            VMEM((9, CAP, devices), jnp.int32),
            VMEM((devices, 128), f32),
        ],
        moved=8 << 20,
    )(arrived, cells, near_a, far_a, near_z, far_z, swept, *links)
    return fluid_out, solid_out


def solution(mesh):
    both = ("azim", "axial")
    in_specs = (
        P(None, "azim", "axial", None),
        P("azim", "axial", None),
        P(both),
        P(both),
        P(both),
        P(both),
        P(both),
        P("azim", "axial", None),
        P("azim", "axial", None),
    )
    out_specs = (P(None, "azim", "axial", None), P("azim", "axial", None))
    return jax.shard_map(
        functools.partial(per_device, mesh.shape["azim"], mesh.shape["axial"]),
        mesh=mesh,
        in_specs=in_specs,
        out_specs=out_specs,
        check_vma=False,
    )
```

```python
import functools

import jax
import jax.numpy as jnp
from jax import lax
from jax.experimental import pallas as pl
from jax.experimental.pallas import tpu as pltpu
from jax.sharding import PartitionSpec as P

CAP = 8
STEP_A = [0, 1, -1, 0, 0, 0, 0, 1, -1, 1, -1, 1, -1, 1, -1, 0, 0, 0, 0]
STEP_Z = [0, 0, 0, 1, -1, 0, 0, 1, -1, -1, 1, 0, 0, 0, 0, 1, -1, 1, -1]
STEP_R = [0, 0, 0, 0, 0, 1, -1, 0, 0, 0, 0, 1, -1, -1, 1, 1, -1, -1, 1]
OPPOSITE = [0, 2, 1, 4, 3, 6, 5, 8, 7, 10, 9, 12, 11, 14, 13, 16, 15, 18, 17]
AZIM_UP = [i for i in range(19) if STEP_A[i] == 1]
AZIM_DOWN = [i for i in range(19) if STEP_A[i] == -1]
AXIAL_UP = [i for i in range(19) if STEP_Z[i] == 1]
AXIAL_DOWN = [i for i in range(19) if STEP_Z[i] == -1]
RELAXATION = 1.25
SPEED_REF = 0.05
HEAT_CAPACITY = 6.5

Q = 19
CA, CZ, NR = 8, 16, 256
SA, SZ = 16, 16
HALVES = (0, 1)
ROWS = 32

PER_PLACE = 26
TEMP_ROW = 208
COND_ROW = 256
TAIL_ROW = 304
AXIAL_ROWS = 312
STREAMED_ROW = 100
SUMS_ROW = 190
FLAG_ROW = 244
SOLID_ROW = 264
SOLID_SKIP = (0, 20, 38, 54)
CELL_ROW = 376
AZIM_ROWS = 392

VMEM = pltpu.VMEM
f32 = jnp.float32
bf16 = jnp.bfloat16


def lanes(half):
    return pl.ds(128 * half, 128)


def moments(f):
    rho = f[0]
    for i in range(1, Q):
        rho = rho + f[i]
    d = [f[i] - f[i + 1] for i in range(1, Q, 2)]
    mom_a = d[0] + d[3] + d[4] + d[5] + d[6]
    mom_z = d[1] + d[3] - d[4] + d[7] + d[8]
    mom_r = d[2] + d[5] - d[6] + d[7] - d[8]
    return rho, mom_a, mom_z, mom_r


def collide_part(sums, f, flag, which):
    rho, mom_a, mom_z, mom_r = sums
    open_cell = flag > 0
    inv = 1.0 / jnp.where(open_cell, rho, 1.0)
    omega = jnp.where(open_cell, RELAXATION, 0.0)
    keep = 1.0 - omega
    ua, uz, ur = mom_a * inv, mom_z * inv, mom_r * inv
    base = 1.0 - 1.5 * (ua * ua + uz * uz + ur * ur)
    scale = omega * rho
    face, edge = scale * (1.0 / 18.0), scale * (1.0 / 36.0)
    post = {}
    if 0 in which:
        post[0] = keep * f[0] + scale * (1.0 / 3.0) * base
    for n, proj in enumerate(
        (ua, uz, ur, ua + uz, ua - uz, ua + ur, ua - ur, uz + ur, uz - ur)
    ):
        weight = face if n < 3 else edge
        one, two = 2 * n + 1, 2 * n + 2
        if one in which or two in which:
            even = weight * (base + 4.5 * proj * proj)
            odd = weight * (3.0 * proj)
        if one in which:
            post[one] = keep * f[one] + (even + odd)
        if two in which:
            post[two] = keep * f[two] + (even - odd)
    return post


def collide(f, flag):
    return collide_part(moments(f), f, flag, range(Q))


def conductivity(material):
    return jnp.where(
        material == 0,
        1.0,
        jnp.where(material == 1, 0.55, jnp.where(material == 2, 0.2, 0.8)),
    ).astype(f32)


def by_parity(axis, body, near, far):
    odd = lax.rem(lax.axis_index(axis), 2) == 1

    @pl.when(odd)
    def _():
        body(near, far)

    @pl.when(jnp.logical_not(odd))
    def _():
        body(far, near)


def first_kernel(
    f_far,
    flags_far,
    temp_far,
    mat_far,
    cells,
    post,
    near,
    far,
    f,
    flags,
    temp,
    mat,
    low,
    high,
    layers_in,
    others_in,
):
    others = [
        pltpu.make_async_copy(source, target, others_in.at[n])
        for n, (source, target) in enumerate(
            ((flags_far, flags), (temp_far, temp), (mat_far, mat))
        )
    ]

    def layer_copy(a):
        return pltpu.make_async_copy(f_far.at[:, a], f.at[:, a], layers_in.at[a])

    others[0].start()
    for a in range(CA):
        layer_copy(a).start()
    others[1].start()
    others[2].start()
    others[0].wait()

    def layer(a, carry):
        layer_copy(a).wait()
        for half in HALVES:
            for part in (0, 1):
                rows = pl.ds(8 * part, 8)
                flag = flags[a, rows, lanes(half)].astype(f32)
                out = collide([f[i, a, rows, lanes(half)] for i in range(Q)], flag)
                for i in range(Q):
                    post[i, a, rows, lanes(half)] = out[i]
                place = a * PER_PLACE
                target, inner, edge, near_edge = (
                    (low, AXIAL_DOWN, 0, 1) if part == 0 else (high, AXIAL_UP, 7, 6)
                )

                def put(row, value, at):
                    target[half, pl.ds(place + row, 1), :] = value[at : at + 1]

                for i in range(Q):
                    put(i, out[i], edge)
                for n, i in enumerate(inner):
                    put(Q + n, out[i], near_edge)
                put(24, flag, edge)
                put(25, flag, near_edge)
        return carry

    lax.fori_loop(0, CA, layer, 0)
    others[1].wait()
    others[2].wait()

    def solid_layer(a, carry):
        for half in HALVES:
            for part, target in ((0, low), (1, high)):
                rows = pl.ds(8 * part, 8)
                t = temp[a, rows, lanes(half)]
                c = conductivity(mat[a, rows, lanes(half)])
                for depth in range(3):
                    at = depth if part == 0 else 7 - depth
                    target[half, pl.ds(TEMP_ROW + depth * SA + a, 1), :] = t[
                        at : at + 1
                    ]
                    target[half, pl.ds(COND_ROW + depth * SA + a, 1), :] = c[
                        at : at + 1
                    ]
        return carry

    lax.fori_loop(0, SA, solid_layer, 0, unroll=4)
    rc = cells[...].astype(f32)
    low[0, pl.ds(TAIL_ROW, 8), :] = rc
    high[0, pl.ds(TAIL_ROW, 8), :] = rc

    def hand_over(down, up):
        down[...] = low[...]
        up[...] = high[...]

    by_parity("axial", hand_over, near, far)


def ends(n_axial):
    z = lax.axis_index("axial")
    return (
        jnp.where(z > 0, 1.0, 0.0).astype(f32),
        jnp.where(z < n_axial - 1, 1.0, 0.0).astype(f32),
    )


def shifted(pair, step, lane):
    if step == 0:
        return pair
    turn = 1 if step == 1 else 127
    at = 0 if step == 1 else 127
    a, b = (pltpu.roll(x, turn, 1) for x in pair)
    return [jnp.where(lane == at, b, a), jnp.where(lane == at, a, b)]


def split(x):
    one = x.astype(bf16)
    return one, (x - one.astype(f32)).astype(bf16)


def stream(
    source,
    opened,
    at_a,
    flag_a,
    row,
    lane,
    which=None,
    sides=None,
    rim=None,
    beyond=False,
):
    rows = pl.ds(row, 8)
    out = [[], []]
    for i in range(Q) if which is None else which:
        own = OPPOSITE[i]
        from_rows = pl.ds(row - STEP_Z[i], 8)

        def before(half):
            if rim and i in rim:
                return sides[rim[i][0], rim[i][1], half, from_rows, :]
            if beyond:
                return source[i, at_a, half, from_rows, :]
            return source[i, at_a - STEP_A[i], half, from_rows, :]

        def back(half):
            if beyond:
                return sides[rim[own][0], rim[own][1], half, rows, :]
            return source[own, at_a, half, rows, :]

        moved = shifted([before(half) for half in HALVES], STEP_R[i], lane)
        for half in HALVES:
            if i == 0:
                out[half].append(moved[half])
                continue
            from_a = flag_a if beyond else flag_a - STEP_A[i]
            mask = opened[STEP_R[i] % 3, from_a, half, from_rows, :]
            out[half].append(jnp.where(mask > 0, moved[half], back(half)))
    return out


def rim_kernel(
    n_axial,
    post,
    flags,
    temp,
    mat,
    cells,
    near_z,
    far_z,
    ext,
    opened,
    near,
    far,
    low,
    high,
):
    lane = lax.broadcasted_iota(jnp.int32, (8, 128), 1)
    below, above = ends(n_axial)

    def own_layer(a, carry):
        for half in HALVES:
            for part in (0, 1):
                rows = pl.ds(8 * part, 8)
                to = pl.ds(8 + 8 * part, 8)
                for i in range(Q):
                    ext[i, a, half, to, :] = post[i, a, rows, lanes(half)]
                opened[0, a, half, to, :] = flags[a, rows, lanes(half)].astype(f32)
        return carry

    lax.fori_loop(0, CA, own_layer, 0)

    def axial_rim(lower, upper):
        def layer(a, carry):
            place = a * PER_PLACE
            for half in HALVES:
                for source, first, last, moving, there in (
                    (lower, 7, 6, AXIAL_UP, below),
                    (upper, 24, 25, AXIAL_DOWN, above),
                ):

                    def get(row):
                        return source[half, pl.ds(place + row, 1), :]

                    for i in range(Q):
                        ext[i, a, half, pl.ds(first, 1), :] = get(i)
                    for n, i in enumerate(moving):
                        ext[i, a, half, pl.ds(last, 1), :] = get(Q + n)
                    opened[0, a, half, pl.ds(first, 1), :] = get(24) * there
                    opened[0, a, half, pl.ds(last, 1), :] = get(25) * there
            return carry

        lax.fori_loop(0, CA, layer, 0, unroll=2)
        own = cells[...].astype(f32)
        outside = jnp.full((CAP, 128), SA * SZ * NR, f32)
        for target, first, step in ((low, 0, 1), (high, SA - 1, -1)):
            for half in HALVES:
                for n in range(3):
                    a = first + step * n
                    at = SOLID_ROW + SOLID_SKIP[n]
                    target[half, pl.ds(at + 2 - n, 16), :] = temp[a, :, lanes(half)]
                    target[half, pl.ds(at + 56 - n, 16), :] = conductivity(
                        mat[a, :, lanes(half)]
                    )
                    for depth in range(2 - n):
                        for source, row, there in (
                            (lower, at + 1 - n - depth, below),
                            (upper, at + 18 - n + depth, above),
                        ):
                            target[half, pl.ds(row, 1), :] = source[
                                half, pl.ds(TEMP_ROW + depth * SA + a, 1), :
                            ]
                            target[half, pl.ds(row + 54, 1), :] = (
                                source[half, pl.ds(COND_ROW + depth * SA + a, 1), :]
                                * there
                            )
            target[0, pl.ds(CELL_ROW, 8), :] = own
            for half, row, source, there in (
                (1, CELL_ROW, lower, below),
                (0, CELL_ROW + 8, upper, above),
            ):
                target[half, pl.ds(row, 8), :] = jnp.where(
                    there > 0, source[0, pl.ds(TAIL_ROW, 8), :], outside
                )

    by_parity("axial", axial_rim, near_z, far_z)

    def turn(a, carry):
        turn_flags(opened, a, lane)
        return carry

    lax.fori_loop(0, CA, turn, 0, unroll=2)

    for target, layer, moving, step in (
        (low, 0, AZIM_DOWN, -1),
        (high, CA - 1, AZIM_UP, 1),
    ):
        for half in HALVES:
            for n, i in enumerate(moving):
                target[half, pl.ds(20 * n, 20), :] = ext[
                    i, layer, half, pl.ds(6, 20), :
                ]
            target[half, pl.ds(FLAG_ROW, 20), :] = opened[
                0, layer, half, pl.ds(6, 20), :
            ]
        which = [i for i in range(Q) if STEP_A[i] in (0, step)]
        for row in (7, 15, 17):
            moved = stream(ext, opened, layer, layer, row, lane, which)
            for half in HALVES:
                new = dict(zip(which, moved[half]))
                at = row - 7
                for n, i in enumerate(moving):
                    target[half, pl.ds(STREAMED_ROW + 18 * n + at, 8), :] = new[i]
                still = [i for i in which if STEP_A[i] == 0]
                for n, table in enumerate(([1] * Q, STEP_Z, STEP_R)):
                    total = None
                    for i in still:
                        if table[i]:
                            term = new[i] * table[i]
                            total = term if total is None else total + term
                    target[half, pl.ds(SUMS_ROW + 18 * n + at, 8), :] = total

    def hand_over(down, up):
        down[...] = low[...]
        up[...] = high[...]

    by_parity("azim", hand_over, near, far)


def turn_flags(opened, a, lane):
    for part in range(4):
        rows = pl.ds(8 * part, 8)
        pair = [opened[0, a, half, rows, :] for half in HALVES]
        up = shifted(pair, 1, lane)
        down = shifted(pair, -1, lane)
        opened[1, a, 0, rows, :] = jnp.where(lane == 0, 0.0, up[0])
        opened[1, a, 1, rows, :] = up[1]
        opened[2, a, 0, rows, :] = down[0]
        opened[2, a, 1, rows, :] = jnp.where(lane == 127, 0.0, down[1])


def fluid_kernel(
    n_azim,
    n_axial,
    ext,
    own_opened,
    near_a,
    far_a,
    cell,
    drive,
    owner,
    slot,
    fluid_far,
    message,
    opened,
    second,
    sides,
    speeds,
    fluid_out,
    layers_out,
):
    lane = lax.broadcasted_iota(jnp.int32, (8, 128), 1)

    def own_flags(a, carry):
        for k in range(3):
            for half in HALVES:
                opened[k, a + 1, half] = own_opened[k, a, half]
        return carry

    lax.fori_loop(0, CA, own_flags, 0, unroll=2)

    def azim_rim(lower, upper):
        for side, (source, a) in enumerate(((lower, 0), (upper, CA + 1))):
            for half in HALVES:
                for n in range(5):
                    sides[side, n, half, pl.ds(6, 20), :] = source[
                        half, pl.ds(20 * n, 20), :
                    ]
                for n in range(8):
                    sides[side, 5 + n, half, pl.ds(7, 18), :] = source[
                        half, pl.ds(STREAMED_ROW + 18 * n, 18), :
                    ]
                opened[0, a, half, pl.ds(6, 20), :] = source[
                    half, pl.ds(FLAG_ROW, 20), :
                ]

    by_parity("azim", azim_rim, near_a, far_a)
    turn_flags(opened, 0, lane)
    turn_flags(opened, CA + 1, lane)

    def finish(a, row, moved):
        for half in HALVES:
            out = collide(moved[half], opened[0, a + 1, half, pl.ds(row, 8), :])
            for i in range(Q):
                second[i, a + 1, half, pl.ds(row, 8), :] = out[i]

    def first_step(a, carry):
        for row in (7, 15, 23):
            finish(a, row, stream(ext, opened, a, a + 1, row, lane))
        return carry

    lax.fori_loop(1, CA - 1, first_step, 0)
    for side, (a, inward, outward) in enumerate(
        ((0, AZIM_UP, AZIM_DOWN), (CA - 1, AZIM_DOWN, AZIM_UP))
    ):
        rim = {i: (side, n) for n, i in enumerate(inward)}
        beyond = 0 if side == 0 else CA + 1

        def edge_step(n, carry):
            row = 7 + 8 * n
            finish(a, row, stream(ext, opened, a, a + 1, row, lane, None, sides, rim))
            far_in = stream(
                ext, opened, a, a + 1, row, lane, outward, sides, rim, beyond=True
            )
            for half in HALVES:
                rows = pl.ds(row, 8)

                def at(n):
                    return sides[side, n, half, rows, :]

                new = {i: at(5 + n) for n, i in enumerate(inward)}
                new.update(zip(outward, far_in[half]))
                sums = [at(10), None, at(11), at(12)]
                for k, table in enumerate(([1] * Q, STEP_A, STEP_Z, STEP_R)):
                    for i in inward + outward:
                        if table[i]:
                            term = new[i] * table[i]
                            sums[k] = term if sums[k] is None else sums[k] + term
                out = collide_part(
                    sums, new, opened[0, beyond, half, rows, :], inward
                )
                for i in inward:
                    second[i, beyond, half, rows, :] = out[i]
            return carry

        lax.fori_loop(0, 3, edge_step, 0)

    def second_step(a, carry):
        for part in (0, 1):
            moved = stream(second, opened, a + 1, a + 1, 8 + 8 * part, lane)
            for half in HALVES:
                for i in range(Q):
                    fluid_out[i, a, pl.ds(8 * part, 8), lanes(half)] = moved[half][i]
                rho, mom_a, mom_z, mom_r = moments(moved[half])
                inv = 1.0 / rho
                ua, uz, ur = mom_a * inv, mom_z * inv, mom_r * inv
                speeds[pl.ds(a * CZ + 8 * part, 8), lanes(half)] = jnp.sqrt(
                    ua * ua + uz * uz + ur * ur + 1e-06
                )
        layer_copy(a).start()
        return carry

    def layer_copy(a):
        return pltpu.make_async_copy(
            fluid_out.at[:, a], fluid_far.at[:, a], layers_out.at[a]
        )

    lax.fori_loop(0, CA, second_step, 0)

    rows_here = cell.shape[1]
    place = cell[...]
    row_hot = (
        lax.broadcasted_iota(jnp.int32, (CA * CZ, rows_here), 0) == place // NR
    ).astype(f32).astype(bf16)
    turned = jnp.transpose(speeds[...])
    picked = jnp.zeros((NR, rows_here), f32)
    for term in split(turned):
        picked = picked + jnp.dot(term, row_hot, preferred_element_type=f32)
    column = lax.broadcasted_iota(jnp.int32, (NR, rows_here), 0) == place % NR
    speed = jnp.sum(jnp.where(column, picked, 0.0), axis=0, keepdims=True)
    flux = drive[...] * (0.2 + speed / SPEED_REF)
    devices = n_azim * n_axial
    owner_hot = (
        lax.broadcasted_iota(jnp.int32, (devices, rows_here), 0) == owner[...]
    ).astype(f32).astype(bf16)
    slotted = jnp.where(
        lax.broadcasted_iota(jnp.int32, (128, rows_here), 0) == slot[...], flux, 0.0
    )
    sent = jnp.zeros((devices, 128), f32)
    for term in split(slotted):
        sent = sent + lax.dot_general(
            owner_hot, term, (((1,), (1,)), ((), ())), preferred_element_type=f32
        )
    total = jnp.zeros((devices, 128), f32)
    for da in (-1, 0, 1):
        for dz in (-1, 0, 1):
            which = (da + 1) * 3 + dz + 1
            back = (-(da * n_axial + dz)) % devices
            moved = pltpu.roll(sent, back, 0) if back else sent
            total = total + (pltpu.roll(moved, CAP * which, 1) if which else moved)
    for o in range(devices):
        message[o, :, :] = total[o : o + 1]
    for a in range(CA):
        layer_copy(a).wait()


def link(first, second):
    joined = first + second
    good = joined > 0
    return jnp.where(
        good,
        (2.0 / HEAT_CAPACITY) * first * second / jnp.where(good, joined, 1.0),
        0.0,
    )


def sweep(source, link_a, link_z, link_r, keep, a, row, lane):
    rows = pl.ds(row, 8)
    pair = [source[a, half, rows, :] for half in HALVES]
    lr = [link_r[a, half, rows, :] for half in HALVES]
    up = shifted(pair, -1, lane)
    down = shifted([x * y for x, y in zip(pair, lr)], 1, lane)
    out = []
    for half in HALVES:
        total = keep[a, half, rows, :] * pair[half]
        total = total + link_a[a, half, rows, :] * source[a + 1, half, rows, :]
        total = total + link_a[a - 1, half, rows, :] * source[a - 1, half, rows, :]
        total = (
            total + link_z[a, half, rows, :] * source[a, half, pl.ds(row + 1, 8), :]
        )
        total = (
            total
            + link_z[a, half, pl.ds(row - 1, 8), :]
            * source[a, half, pl.ds(row - 1, 8), :]
        )
        out.append(total + lr[half] * up[half] + down[half])
    return out


def solid_kernel(
    n_axial,
    temp,
    mat,
    near_a,
    far_a,
    near_z,
    far_z,
    cells,
    swept,
    link_a,
    link_z,
    link_r,
    keep,
    all_cells,
    ext,
    cond,
    other,
):
    lane = lax.broadcasted_iota(jnp.int32, (8, 128), 1)

    def own_layer(a, carry):
        for half in HALVES:
            for part in (0, 1):
                rows = pl.ds(8 * part, 8)
                to = pl.ds(8 + 8 * part, 8)
                ext[a + 3, half, to, :] = temp[a, rows, lanes(half)]
                cond[a + 3, half, to, :] = conductivity(mat[a, rows, lanes(half)])
        return carry

    lax.fori_loop(0, SA, own_layer, 0, unroll=4)

    def azim_rim(lower, upper):
        for half in HALVES:
            for n in range(3):
                for source, a in ((lower, 2 - n), (upper, 19 + n)):
                    at = SOLID_ROW + SOLID_SKIP[n]
                    rows = pl.ds(6 + n, 20 - 2 * n)
                    ext[a, half, rows, :] = source[half, pl.ds(at, 20 - 2 * n), :]
                    cond[a, half, rows, :] = source[half, pl.ds(at + 54, 20 - 2 * n), :]
        for source, which in ((lower, 0), (upper, 6)):
            all_cells[which + 1] = source[0, pl.ds(CELL_ROW, 8), :]
            all_cells[which] = source[1, pl.ds(CELL_ROW, 8), :]
            all_cells[which + 2] = source[0, pl.ds(CELL_ROW + 8, 8), :]

    by_parity("azim", azim_rim, near_a, far_a)
    below, above = ends(n_axial)

    def axial_rim(lower, upper):
        def layer(a, carry):
            for half in HALVES:
                for depth in range(3):
                    for source, row, there in (
                        (lower, 7 - depth, below),
                        (upper, 24 + depth, above),
                    ):
                        ext[a + 3, half, pl.ds(row, 1), :] = source[
                            half, pl.ds(TEMP_ROW + depth * SA + a, 1), :
                        ]
                        cond[a + 3, half, pl.ds(row, 1), :] = (
                            source[half, pl.ds(COND_ROW + depth * SA + a, 1), :] * there
                        )
            return carry

        lax.fori_loop(0, SA, layer, 0, unroll=4)
        outside = jnp.full((CAP, 128), SA * SZ * NR, f32)
        for source, which, there in ((lower, 3, below), (upper, 5, above)):
            all_cells[which] = jnp.where(
                there > 0, source[0, pl.ds(TAIL_ROW, 8), :], outside
            )

    by_parity("axial", axial_rim, near_z, far_z)
    all_cells[4] = cells[...].astype(f32)

    def links(a, carry):
        for row in (5, 13, 21):
            rows = pl.ds(row, 8)
            pair = [cond[a, half, rows, :] for half in HALVES]
            up = shifted(pair, -1, lane)
            up = [up[0], jnp.where(lane == 127, 0.0, up[1])]
            for half in HALVES:
                link_a[a, half, rows, :] = link(pair[half], cond[a + 1, half, rows, :])
                link_z[a, half, rows, :] = link(
                    pair[half], cond[a, half, pl.ds(row + 1, 8), :]
                )
                link_r[a, half, rows, :] = link(pair[half], up[half])
        return carry

    lax.fori_loop(0, SA + 5, links, 0, unroll=3)

    def keeps(a, carry):
        for row in (6, 14, 22):
            rows = pl.ds(row, 8)
            pair = [link_r[a, half, rows, :] for half in HALVES]
            down = shifted(pair, 1, lane)
            for half in HALVES:
                keep[a, half, rows, :] = 1.0 - (
                    link_a[a, half, rows, :]
                    + link_a[a - 1, half, rows, :]
                    + link_z[a, half, rows, :]
                    + link_z[a, half, pl.ds(row - 1, 8), :]
                    + pair[half]
                    + down[half]
                )
        return carry

    lax.fori_loop(1, SA + 5, keeps, 0, unroll=4)

    def once(source, target, first, last, at):
        def layer(a, carry):
            for row in at:
                out = sweep(source, link_a, link_z, link_r, keep, a, row, lane)
                for half in HALVES:
                    target[a, half, pl.ds(row, 8), :] = out[half]
            return carry

        lax.fori_loop(first, last, layer, 0, unroll=2)

    once(ext, other, 1, SA + 5, (6, 14, 22))
    once(other, ext, 2, SA + 4, (7, 15, 23))

    def final(a, carry):
        for part in (0, 1):
            out = sweep(ext, link_a, link_z, link_r, keep, a + 3, 8 + 8 * part, lane)
            for half in HALVES:
                swept[a, pl.ds(8 * part, 8), lanes(half)] = out[half]
        return carry

    lax.fori_loop(0, SA, final, 0, unroll=4)


def deposit_kernel(
    swept_far,
    link_a_far,
    link_z_far,
    link_r_far,
    keep_far,
    arrived,
    all_cells,
    solid_out,
    heat,
    other,
    came,
    swept,
    link_a,
    link_z,
    link_r,
    keep,
    brought,
):
    copies = [
        pltpu.make_async_copy(source, target, brought.at[n])
        for n, (source, target) in enumerate(
            (
                (swept_far, swept),
                (link_a_far, link_a),
                (link_z_far, link_z),
                (link_r_far, link_r),
                (keep_far, keep),
            )
        )
    ]
    for copy in copies:
        copy.start()
    lane = lax.broadcasted_iota(jnp.int32, (8, 128), 1)
    senders = arrived.shape[0]
    for s in range(senders):
        came[pl.ds(s, 1), :] = arrived[s]

    def clear(a, carry):
        for half in HALVES:
            heat[a, half] = jnp.zeros((ROWS, 128), f32)
        return carry

    lax.fori_loop(0, SA + 6, clear, 0, unroll=2)

    values = jnp.transpose(came[...]) * (1.0 / HEAT_CAPACITY)

    def place(which, rows, row_of):
        cell = all_cells[which].astype(jnp.int32)
        value = values[CAP * which : CAP * (which + 1)]
        one, two = split(value)
        at_row = row_of(lax.broadcasted_iota(jnp.int32, (rows, senders), 0))
        at_col = lax.broadcasted_iota(jnp.int32, (NR, senders), 0)
        left, right = [[], []], []
        for c in range(CAP):
            hit = at_row == (cell[c : c + 1] // NR)
            for to, term in zip(left, (one, two)):
                to.append(
                    jnp.where(hit, term[c : c + 1].astype(f32), 0.0).astype(bf16)
                )
            right.append((at_col == cell[c : c + 1] % NR).astype(f32).astype(bf16))
        right = jnp.concatenate(right, axis=1)
        total = None
        for to in left:
            part = lax.dot_general(
                jnp.concatenate(to, axis=1),
                right,
                (((1,), (1,)), ((), ())),
                preferred_element_type=f32,
            )
            total = part if total is None else total + part
        return total

    own = place(4, SA * SZ, lambda j: j)
    for a in range(SA):
        for half in HALVES:
            heat[a + 3, half, pl.ds(8, 16), :] = own[
                16 * a : 16 * a + 16, 128 * half : 128 * half + 128
            ]
    low = place(1, 32, lambda j: j + 14 * SZ)
    high = place(7, 32, lambda j: j)
    for n in range(2):
        for half in HALVES:
            cut = slice(128 * half, 128 * half + 128)
            heat[1 + n, half, pl.ds(8, 16), :] = low[16 * n : 16 * n + 16, cut]
            heat[19 + n, half, pl.ds(8, 16), :] = high[16 * n : 16 * n + 16, cut]
    low = place(3, 32, lambda j: (j // 2) * SZ + 14 + j % 2)
    high = place(5, 32, lambda j: (j // 2) * SZ + j % 2)
    for a in range(SA):
        for half in HALVES:
            cut = slice(128 * half, 128 * half + 128)
            heat[a + 3, half, pl.ds(6, 2), :] = low[2 * a : 2 * a + 2, cut]
            heat[a + 3, half, pl.ds(24, 2), :] = high[2 * a : 2 * a + 2, cut]
    for which, cell_row, a, row in (
        (0, 255, 2, 7),
        (2, 240, 2, 24),
        (6, 15, 19, 7),
        (8, 0, 19, 24),
    ):
        one = place(which, 8, lambda j: jnp.where(j == 0, cell_row, -1))
        for half in HALVES:
            heat[a, half, pl.ds(row, 1), :] = one[0:1, 128 * half : 128 * half + 128]

    for copy in copies:
        copy.wait()

    def middle(a, carry):
        for row in (7, 15, 23):
            out = sweep(heat, link_a, link_z, link_r, keep, a, row, lane)
            for half in HALVES:
                other[a, half, pl.ds(row, 8), :] = (
                    out[half] + heat[a, half, pl.ds(row, 8), :]
                )
        return carry

    lax.fori_loop(2, SA + 4, middle, 0, unroll=2)

    def final(a, carry):
        for part in (0, 1):
            rows = pl.ds(8 * part, 8)
            out = sweep(other, link_a, link_z, link_r, keep, a + 3, 8 + 8 * part, lane)
            for half in HALVES:
                solid_out[a, rows, lanes(half)] = (
                    out[half]
                    + heat[a + 3, half, pl.ds(8 + 8 * part, 8), :]
                    + swept[a, rows, lanes(half)]
                )
        return carry

    lax.fori_loop(0, SA, final, 0, unroll=4)


def call(kernel, ins, outs, scratch=(), limit=16, moved=0, far_ins=0, far_outs=0):
    here, there = (pl.BlockSpec(memory_space=m) for m in (VMEM, pltpu.HBM))
    kernel_call = pl.pallas_call(
        kernel,
        out_shape=[jax.ShapeDtypeStruct(s, f32) for s in outs],
        in_specs=[there] * far_ins + [here] * (ins - far_ins),
        out_specs=[there] * far_outs + [here] * (len(outs) - far_outs),
        scratch_shapes=list(scratch),
        compiler_params=pltpu.CompilerParams(vmem_limit_bytes=limit * 1024 * 1024),
        cost_estimate=pl.CostEstimate(
            flops=0, bytes_accessed=moved, transcendentals=0
        ),
    )

    def run(*args):
        far = [pltpu.with_memory_space_constraint(x, pltpu.HBM) for x in args[:far_ins]]
        return kernel_call(*far, *args[far_ins:])

    return run


def swap(values, axis, far):
    count = lax.axis_size(axis)
    pairs = [(i, (((i + 1) ^ 1) - 1) % count if far else i ^ 1) for i in range(count)]
    return lax.ppermute(values, axis, pairs)


def per_device(
    n_azim,
    n_axial,
    populations,
    fluid_flags,
    wall_cell,
    wall_drive,
    wall_owner,
    wall_slot,
    receive_cell,
    materials,
    solid_temp,
):
    devices = n_azim * n_axial
    cells = receive_cell.reshape(devices, CAP).T
    azim_msg = (2, AZIM_ROWS, 128)
    axial_msg = (2, AXIAL_ROWS, 128)
    fluid = (Q, CA, CZ, NR)
    solid = (SA, SZ, NR)
    fluid_ext = (Q, CA, 2, ROWS, 128)
    solid_ext = (SA + 6, 2, ROWS, 128)
    post, near_z, far_z = call(
        first_kernel,
        5,
        [fluid, axial_msg, axial_msg],
        [
            VMEM(fluid, f32),
            VMEM((CA, CZ, NR), jnp.int32),
            VMEM(solid, f32),
            VMEM(solid, jnp.int32),
            VMEM(axial_msg, f32),
            VMEM(axial_msg, f32),
            pltpu.SemaphoreType.DMA((CA,)),
            pltpu.SemaphoreType.DMA((3,)),
        ],
        moved=8 << 20,
        far_ins=4,
    )(populations, fluid_flags, solid_temp, materials, cells)
    near_z = swap(near_z, "axial", False)
    far_z = swap(far_z, "axial", True)
    ext, opened, near_a, far_a = call(
        functools.partial(rim_kernel, n_axial),
        7,
        [fluid_ext, (3, CA, 2, ROWS, 128), azim_msg, azim_msg],
        [VMEM(azim_msg, f32), VMEM(azim_msg, f32)],
        moved=8 << 20,
    )(post, fluid_flags, solid_temp, materials, cells, near_z, far_z)
    near_a = swap(near_a, "azim", False)
    far_a = swap(far_a, "azim", True)
    rows = wall_cell.shape[0]
    fluid_out, message = call(
        functools.partial(fluid_kernel, n_azim, n_axial),
        8,
        [fluid, (devices, 1, 128)],
        [
            VMEM((3, CA + 2, 2, ROWS, 128), f32),
            VMEM((Q, CA + 2, 2, ROWS, 128), f32),
            VMEM((2, 13, 2, ROWS, 128), f32),
            VMEM((CA * CZ, NR), f32),
            VMEM(fluid, f32),
            pltpu.SemaphoreType.DMA((CA,)),
        ],
        limit=28,
        moved=16 << 20,
        far_outs=1,
    )(
        ext,
        opened,
        near_a,
        far_a,
        wall_cell.reshape(1, rows),
        wall_drive.reshape(1, rows),
        wall_owner.reshape(1, rows),
        wall_slot.reshape(1, rows),
    )
    arrived = lax.all_to_all(
        message, ("azim", "axial"), split_axis=0, concat_axis=0, tiled=True
    )
    *swept, all_cells = call(
        functools.partial(solid_kernel, n_axial),
        7,
        [solid] + [solid_ext] * 4 + [(9, CAP, devices)],
        [VMEM(solid_ext, f32)] * 3,
        moved=8 << 20,
    )(solid_temp, materials, near_a, far_a, near_z, far_z, cells)
    (solid_out,) = call(
        deposit_kernel,
        7,
        [solid],
        [
            VMEM(solid_ext, f32),
            VMEM(solid_ext, f32),
            VMEM((devices, 128), f32),
            VMEM(solid, f32),
        ]
        + [VMEM(solid_ext, f32)] * 4
        + [pltpu.SemaphoreType.DMA((5,))],
        moved=8 << 20,
        far_ins=5,
    )(*swept, arrived, all_cells)
    return fluid_out, solid_out


def solution(mesh):
    both = ("azim", "axial")
    in_specs = (
        P(None, "azim", "axial", None),
        P("azim", "axial", None),
        P(both),
        P(both),
        P(both),
        P(both),
        P(both),
        P("azim", "axial", None),
        P("azim", "axial", None),
    )
    out_specs = (P(None, "azim", "axial", None), P("azim", "axial", None))
    return jax.shard_map(
        functools.partial(per_device, mesh.shape["azim"], mesh.shape["axial"]),
        mesh=mesh,
        in_specs=in_specs,
        out_specs=out_specs,
        check_vma=False,
    )
```

```python
import functools

import jax
import jax.numpy as jnp
from jax import lax
from jax.experimental import pallas as pl
from jax.experimental.pallas import tpu as pltpu
from jax.sharding import PartitionSpec as P

CAP = 8
STEP_A = [0, 1, -1, 0, 0, 0, 0, 1, -1, 1, -1, 1, -1, 1, -1, 0, 0, 0, 0]
STEP_Z = [0, 0, 0, 1, -1, 0, 0, 1, -1, -1, 1, 0, 0, 0, 0, 1, -1, 1, -1]
STEP_R = [0, 0, 0, 0, 0, 1, -1, 0, 0, 0, 0, 1, -1, -1, 1, 1, -1, -1, 1]
OPPOSITE = [0, 2, 1, 4, 3, 6, 5, 8, 7, 10, 9, 12, 11, 14, 13, 16, 15, 18, 17]
AZIM_UP = [i for i in range(19) if STEP_A[i] == 1]
AZIM_DOWN = [i for i in range(19) if STEP_A[i] == -1]
AXIAL_UP = [i for i in range(19) if STEP_Z[i] == 1]
AXIAL_DOWN = [i for i in range(19) if STEP_Z[i] == -1]
RELAXATION = 1.25
SPEED_REF = 0.05
HEAT_CAPACITY = 6.5

Q = 19
CA, CZ, NR = 8, 16, 256
SA, SZ = 16, 16
HALVES = (0, 1)
ROWS = 32

PER_PLACE = 26
AXIAL_ROWS = CA * PER_PLACE
STREAMED_ROW = 100
SUMS_ROW = 190
FLAG_ROW = 244
AZIM_ROWS = 264
SOLID_COND = 48
SOLID_CELLS = 96
SOLID_ROWS = 104
SKIP = (0, 20, 38)
END_COND = 54
END_CELLS = 112
END_ROWS = 128

VMEM = pltpu.VMEM
f32 = jnp.float32
bf16 = jnp.bfloat16


def lanes(half):
    return pl.ds(128 * half, 128)


def moments(f):
    rho = f[0]
    for i in range(1, Q):
        rho = rho + f[i]
    d = [f[i] - f[i + 1] for i in range(1, Q, 2)]
    mom_a = d[0] + d[3] + d[4] + d[5] + d[6]
    mom_z = d[1] + d[3] - d[4] + d[7] + d[8]
    mom_r = d[2] + d[5] - d[6] + d[7] - d[8]
    return rho, mom_a, mom_z, mom_r


def collide_part(sums, f, flag, which):
    rho, mom_a, mom_z, mom_r = sums
    open_cell = flag > 0
    inv = 1.0 / jnp.where(open_cell, rho, 1.0)
    omega = jnp.where(open_cell, RELAXATION, 0.0)
    keep = 1.0 - omega
    ua, uz, ur = mom_a * inv, mom_z * inv, mom_r * inv
    base = 1.0 - 1.5 * (ua * ua + uz * uz + ur * ur)
    scale = omega * rho
    face, edge = scale * (1.0 / 18.0), scale * (1.0 / 36.0)
    post = {}
    if 0 in which:
        post[0] = keep * f[0] + scale * (1.0 / 3.0) * base
    for n, proj in enumerate(
        (ua, uz, ur, ua + uz, ua - uz, ua + ur, ua - ur, uz + ur, uz - ur)
    ):
        weight = face if n < 3 else edge
        one, two = 2 * n + 1, 2 * n + 2
        if one in which or two in which:
            even = weight * (base + 4.5 * proj * proj)
            odd = weight * (3.0 * proj)
        if one in which:
            post[one] = keep * f[one] + (even + odd)
        if two in which:
            post[two] = keep * f[two] + (even - odd)
    return post


def collide(f, flag):
    return collide_part(moments(f), f, flag, range(Q))


def conductivity(material):
    return jnp.where(
        material == 0,
        1.0,
        jnp.where(material == 1, 0.55, jnp.where(material == 2, 0.2, 0.8)),
    ).astype(f32)


def by_parity(axis, body, near, far):
    odd = lax.rem(lax.axis_index(axis), 2) == 1

    @pl.when(odd)
    def _():
        body(near, far)

    @pl.when(jnp.logical_not(odd))
    def _():
        body(far, near)


def first_kernel(f_far, flags_far, post, near, far, token, f, flags, low, high, come):
    flags_copy = pltpu.make_async_copy(flags_far, flags, come.at[CA])

    def layer_copy(a):
        return pltpu.make_async_copy(f_far.at[:, a], f.at[:, a], come.at[a])

    flags_copy.start()
    for a in range(CA):
        layer_copy(a).start()
    token[...] = jnp.zeros((8, 128), f32)
    flags_copy.wait()

    def layer(a, carry):
        layer_copy(a).wait()
        for half in HALVES:
            for part in (0, 1):
                rows = pl.ds(8 * part, 8)
                flag = flags[a, rows, lanes(half)].astype(f32)
                out = collide([f[i, a, rows, lanes(half)] for i in range(Q)], flag)
                for i in range(Q):
                    post[i, a, rows, lanes(half)] = out[i]
                place = a * PER_PLACE
                target, inner, edge, near_edge = (
                    (low, AXIAL_DOWN, 0, 1) if part == 0 else (high, AXIAL_UP, 7, 6)
                )

                def put(row, value, at):
                    target[half, pl.ds(place + row, 1), :] = value[at : at + 1]

                for i in range(Q):
                    put(i, out[i], edge)
                for n, i in enumerate(inner):
                    put(Q + n, out[i], near_edge)
                put(24, flag, edge)
                put(25, flag, near_edge)
        return carry

    lax.fori_loop(0, CA, layer, 0)

    def hand_over(down, up):
        down[...] = low[...]
        up[...] = high[...]

    by_parity("axial", hand_over, near, far)


def solid_azim_kernel(temp_far, mat_far, cells, token, near, far, temp, mat, come):
    copies = []
    for n, layers in enumerate((pl.ds(0, 3), pl.ds(SA - 3, 3))):
        for k, (source, target) in enumerate(((temp_far, temp), (mat_far, mat))):
            copy = pltpu.make_async_copy(
                source.at[layers], target.at[n], come.at[2 * n + k]
            )
            copy.start()
            copies.append(copy)
    for copy in copies:
        copy.wait()

    def fill(down, up):
        for side, target in enumerate((down, up)):
            for half in HALVES:
                for n in range(3):
                    a = n if side == 0 else 2 - n
                    target[half, pl.ds(16 * n, 16), :] = temp[side, a, :, lanes(half)]
                    target[half, pl.ds(SOLID_COND + 16 * n, 16), :] = conductivity(
                        mat[side, a, :, lanes(half)]
                    )
            target[0, pl.ds(SOLID_CELLS, 8), :] = cells[...].astype(f32)

    by_parity("azim", fill, near, far)


def solid_axial_kernel(
    temp_far,
    mat_far,
    cells,
    near_s,
    far_s,
    token,
    near,
    far,
    temp,
    mat,
    low,
    high,
    come,
):
    copies = [
        pltpu.make_async_copy(source, target, come.at[n])
        for n, (source, target) in enumerate(((temp_far, temp), (mat_far, mat)))
    ]
    for copy in copies:
        copy.start()

    def azim_ends(lower, upper):
        for target, edge, step in ((low, 0, 1), (high, SZ - 1, -1)):
            for half in HALVES:
                for depth in range(2):
                    z = edge + step * depth
                    for n in range(2 - depth):
                        for source, at in (
                            (lower, 1 - depth - n),
                            (upper, 18 - depth + n),
                        ):
                            for kind, here in ((0, 0), (END_COND, SOLID_COND)):
                                target[half, pl.ds(kind + SKIP[depth] + at, 1), :] = (
                                    source[half, pl.ds(here + 16 * n + z, 1), :]
                                )
            target[0, pl.ds(END_CELLS, 8), :] = cells[...].astype(f32)
            target[1, pl.ds(END_CELLS, 8), :] = lower[0, pl.ds(SOLID_CELLS, 8), :]
            target[0, pl.ds(END_CELLS + 8, 8), :] = upper[0, pl.ds(SOLID_CELLS, 8), :]

    by_parity("azim", azim_ends, near_s, far_s)
    for copy in copies:
        copy.wait()

    def layer(a, carry):
        for half in HALVES:
            for part, target in ((0, low), (1, high)):
                rows = pl.ds(8 * part, 8)
                t = temp[a, rows, lanes(half)]
                c = conductivity(mat[a, rows, lanes(half)])
                for depth in range(3):
                    at = depth if part == 0 else 7 - depth
                    row = SKIP[depth] + 2 - depth + a
                    target[half, pl.ds(row, 1), :] = t[at : at + 1]
                    target[half, pl.ds(END_COND + row, 1), :] = c[at : at + 1]
        return carry

    lax.fori_loop(0, SA, layer, 0, unroll=4)

    def hand_over(down, up):
        down[...] = low[...]
        up[...] = high[...]

    by_parity("axial", hand_over, near, far)


def ends(n_axial):
    z = lax.axis_index("axial")
    return (
        jnp.where(z > 0, 1.0, 0.0).astype(f32),
        jnp.where(z < n_axial - 1, 1.0, 0.0).astype(f32),
    )


def shifted(pair, step, lane):
    if step == 0:
        return pair
    turn = 1 if step == 1 else 127
    at = 0 if step == 1 else 127
    a, b = (pltpu.roll(x, turn, 1) for x in pair)
    return [jnp.where(lane == at, b, a), jnp.where(lane == at, a, b)]


def split(x):
    one = x.astype(bf16)
    return one, (x - one.astype(f32)).astype(bf16)


def stream(
    source,
    opened,
    at_a,
    flag_a,
    row,
    lane,
    which=None,
    sides=None,
    rim=None,
    beyond=False,
):
    rows = pl.ds(row, 8)
    out = [[], []]
    for i in range(Q) if which is None else which:
        own = OPPOSITE[i]
        from_rows = pl.ds(row - STEP_Z[i], 8)

        def before(half):
            if rim and i in rim:
                return sides[rim[i][0], rim[i][1], half, from_rows, :]
            if beyond:
                return source[i, at_a, half, from_rows, :]
            return source[i, at_a - STEP_A[i], half, from_rows, :]

        def back(half):
            if beyond:
                return sides[rim[own][0], rim[own][1], half, rows, :]
            return source[own, at_a, half, rows, :]

        moved = shifted([before(half) for half in HALVES], STEP_R[i], lane)
        for half in HALVES:
            if i == 0:
                out[half].append(moved[half])
                continue
            from_a = flag_a if beyond else flag_a - STEP_A[i]
            mask = opened[STEP_R[i] % 3, from_a, half, from_rows, :]
            out[half].append(jnp.where(mask > 0, moved[half], back(half)))
    return out


def rim_kernel(
    n_axial,
    post,
    flags,
    near_z,
    far_z,
    ext,
    opened,
    near,
    far,
    token,
    low,
    high,
):
    token[...] = jnp.zeros((8, 128), f32)
    lane = lax.broadcasted_iota(jnp.int32, (8, 128), 1)
    below, above = ends(n_axial)

    def own_layer(a, carry):
        for half in HALVES:
            for part in (0, 1):
                rows = pl.ds(8 * part, 8)
                to = pl.ds(8 + 8 * part, 8)
                for i in range(Q):
                    ext[i, a, half, to, :] = post[i, a, rows, lanes(half)]
                opened[0, a, half, to, :] = flags[a, rows, lanes(half)].astype(f32)
        return carry

    lax.fori_loop(0, CA, own_layer, 0)

    def axial_rim(lower, upper):
        def layer(a, carry):
            place = a * PER_PLACE
            for half in HALVES:
                for source, first, last, moving, there in (
                    (lower, 7, 6, AXIAL_UP, below),
                    (upper, 24, 25, AXIAL_DOWN, above),
                ):

                    def get(row):
                        return source[half, pl.ds(place + row, 1), :]

                    for i in range(Q):
                        ext[i, a, half, pl.ds(first, 1), :] = get(i)
                    for n, i in enumerate(moving):
                        ext[i, a, half, pl.ds(last, 1), :] = get(Q + n)
                    opened[0, a, half, pl.ds(first, 1), :] = get(24) * there
                    opened[0, a, half, pl.ds(last, 1), :] = get(25) * there
            return carry

        lax.fori_loop(0, CA, layer, 0, unroll=2)
    by_parity("axial", axial_rim, near_z, far_z)

    def turn(a, carry):
        turn_flags(opened, a, lane)
        return carry

    lax.fori_loop(0, CA, turn, 0, unroll=2)

    for target, layer, moving, step in (
        (low, 0, AZIM_DOWN, -1),
        (high, CA - 1, AZIM_UP, 1),
    ):
        for half in HALVES:
            for n, i in enumerate(moving):
                target[half, pl.ds(20 * n, 20), :] = ext[
                    i, layer, half, pl.ds(6, 20), :
                ]
            target[half, pl.ds(FLAG_ROW, 20), :] = opened[
                0, layer, half, pl.ds(6, 20), :
            ]
        which = [i for i in range(Q) if STEP_A[i] in (0, step)]
        for row in (7, 15, 17):
            moved = stream(ext, opened, layer, layer, row, lane, which)
            for half in HALVES:
                new = dict(zip(which, moved[half]))
                at = row - 7
                for n, i in enumerate(moving):
                    target[half, pl.ds(STREAMED_ROW + 18 * n + at, 8), :] = new[i]
                still = [i for i in which if STEP_A[i] == 0]
                for n, table in enumerate(([1] * Q, STEP_Z, STEP_R)):
                    total = None
                    for i in still:
                        if table[i]:
                            term = new[i] * table[i]
                            total = term if total is None else total + term
                    target[half, pl.ds(SUMS_ROW + 18 * n + at, 8), :] = total

    def hand_over(down, up):
        down[...] = low[...]
        up[...] = high[...]

    by_parity("azim", hand_over, near, far)


def turn_flags(opened, a, lane):
    for part in range(4):
        rows = pl.ds(8 * part, 8)
        pair = [opened[0, a, half, rows, :] for half in HALVES]
        up = shifted(pair, 1, lane)
        down = shifted(pair, -1, lane)
        opened[1, a, 0, rows, :] = jnp.where(lane == 0, 0.0, up[0])
        opened[1, a, 1, rows, :] = up[1]
        opened[2, a, 0, rows, :] = down[0]
        opened[2, a, 1, rows, :] = jnp.where(lane == 127, 0.0, down[1])


def fluid_kernel(
    n_azim,
    n_axial,
    ext,
    own_opened,
    near_a,
    far_a,
    cell,
    drive,
    owner,
    slot,
    fluid_far,
    message,
    opened,
    second,
    sides,
    speeds,
    fluid_out,
    layers_out,
):
    lane = lax.broadcasted_iota(jnp.int32, (8, 128), 1)

    def own_flags(a, carry):
        for k in range(3):
            for half in HALVES:
                opened[k, a + 1, half] = own_opened[k, a, half]
        return carry

    lax.fori_loop(0, CA, own_flags, 0, unroll=2)

    def azim_rim(lower, upper):
        for side, (source, a) in enumerate(((lower, 0), (upper, CA + 1))):
            for half in HALVES:
                for n in range(5):
                    sides[side, n, half, pl.ds(6, 20), :] = source[
                        half, pl.ds(20 * n, 20), :
                    ]
                for n in range(8):
                    sides[side, 5 + n, half, pl.ds(7, 18), :] = source[
                        half, pl.ds(STREAMED_ROW + 18 * n, 18), :
                    ]
                opened[0, a, half, pl.ds(6, 20), :] = source[
                    half, pl.ds(FLAG_ROW, 20), :
                ]

    by_parity("azim", azim_rim, near_a, far_a)
    turn_flags(opened, 0, lane)
    turn_flags(opened, CA + 1, lane)

    def finish(a, row, moved):
        for half in HALVES:
            out = collide(moved[half], opened[0, a + 1, half, pl.ds(row, 8), :])
            for i in range(Q):
                second[i, a + 1, half, pl.ds(row, 8), :] = out[i]

    def first_step(a, carry):
        for row in (7, 15, 23):
            finish(a, row, stream(ext, opened, a, a + 1, row, lane))
        return carry

    lax.fori_loop(1, CA - 1, first_step, 0)
    for side, (a, inward, outward) in enumerate(
        ((0, AZIM_UP, AZIM_DOWN), (CA - 1, AZIM_DOWN, AZIM_UP))
    ):
        rim = {i: (side, n) for n, i in enumerate(inward)}
        beyond = 0 if side == 0 else CA + 1

        def edge_step(n, carry):
            row = 7 + 8 * n
            finish(a, row, stream(ext, opened, a, a + 1, row, lane, None, sides, rim))
            far_in = stream(
                ext, opened, a, a + 1, row, lane, outward, sides, rim, beyond=True
            )
            for half in HALVES:
                rows = pl.ds(row, 8)

                def at(n):
                    return sides[side, n, half, rows, :]

                new = {i: at(5 + n) for n, i in enumerate(inward)}
                new.update(zip(outward, far_in[half]))
                sums = [at(10), None, at(11), at(12)]
                for k, table in enumerate(([1] * Q, STEP_A, STEP_Z, STEP_R)):
                    for i in inward + outward:
                        if table[i]:
                            term = new[i] * table[i]
                            sums[k] = term if sums[k] is None else sums[k] + term
                out = collide_part(
                    sums, new, opened[0, beyond, half, rows, :], inward
                )
                for i in inward:
                    second[i, beyond, half, rows, :] = out[i]
            return carry

        lax.fori_loop(0, 3, edge_step, 0)

    def second_step(a, carry):
        for part in (0, 1):
            moved = stream(second, opened, a + 1, a + 1, 8 + 8 * part, lane)
            for half in HALVES:
                for i in range(Q):
                    fluid_out[i, a, pl.ds(8 * part, 8), lanes(half)] = moved[half][i]
                rho, mom_a, mom_z, mom_r = moments(moved[half])
                inv = 1.0 / rho
                ua, uz, ur = mom_a * inv, mom_z * inv, mom_r * inv
                speeds[pl.ds(a * CZ + 8 * part, 8), lanes(half)] = jnp.sqrt(
                    ua * ua + uz * uz + ur * ur + 1e-06
                )
        layer_copy(a).start()
        return carry

    def layer_copy(a):
        return pltpu.make_async_copy(
            fluid_out.at[:, a], fluid_far.at[:, a], layers_out.at[a]
        )

    lax.fori_loop(0, CA, second_step, 0)

    rows_here = cell.shape[1]
    place = cell[...]
    row_hot = (
        lax.broadcasted_iota(jnp.int32, (CA * CZ, rows_here), 0) == place // NR
    ).astype(f32).astype(bf16)
    turned = jnp.transpose(speeds[...])
    picked = jnp.zeros((NR, rows_here), f32)
    for term in split(turned):
        picked = picked + jnp.dot(term, row_hot, preferred_element_type=f32)
    column = lax.broadcasted_iota(jnp.int32, (NR, rows_here), 0) == place % NR
    speed = jnp.sum(jnp.where(column, picked, 0.0), axis=0, keepdims=True)
    flux = drive[...] * (0.2 + speed / SPEED_REF)
    devices = n_azim * n_axial
    owner_hot = (
        lax.broadcasted_iota(jnp.int32, (devices, rows_here), 0) == owner[...]
    ).astype(f32).astype(bf16)
    slotted = jnp.where(
        lax.broadcasted_iota(jnp.int32, (128, rows_here), 0) == slot[...], flux, 0.0
    )
    sent = jnp.zeros((devices, 128), f32)
    for term in split(slotted):
        sent = sent + lax.dot_general(
            owner_hot, term, (((1,), (1,)), ((), ())), preferred_element_type=f32
        )
    total = jnp.zeros((devices, 128), f32)
    for da in (-1, 0, 1):
        for dz in (-1, 0, 1):
            which = (da + 1) * 3 + dz + 1
            back = (-(da * n_axial + dz)) % devices
            moved = pltpu.roll(sent, back, 0) if back else sent
            total = total + (pltpu.roll(moved, CAP * which, 1) if which else moved)
    for o in range(devices):
        message[o, :, :] = total[o : o + 1]
    for a in range(CA):
        layer_copy(a).wait()


def link(first, second):
    joined = first + second
    good = joined > 0
    return jnp.where(
        good,
        (2.0 / HEAT_CAPACITY) * first * second / jnp.where(good, joined, 1.0),
        0.0,
    )


def sweep(source, link_a, link_z, link_r, keep, a, row, lane):
    rows = pl.ds(row, 8)
    pair = [source[a, half, rows, :] for half in HALVES]
    lr = [link_r[a, half, rows, :] for half in HALVES]
    up = shifted(pair, -1, lane)
    down = shifted([x * y for x, y in zip(pair, lr)], 1, lane)
    out = []
    for half in HALVES:
        total = keep[a, half, rows, :] * pair[half]
        total = total + link_a[a, half, rows, :] * source[a + 1, half, rows, :]
        total = total + link_a[a - 1, half, rows, :] * source[a - 1, half, rows, :]
        total = (
            total + link_z[a, half, rows, :] * source[a, half, pl.ds(row + 1, 8), :]
        )
        total = (
            total
            + link_z[a, half, pl.ds(row - 1, 8), :]
            * source[a, half, pl.ds(row - 1, 8), :]
        )
        out.append(total + lr[half] * up[half] + down[half])
    return out


def solid_kernel(
    n_axial,
    temp,
    mat,
    near_s,
    far_s,
    near_e,
    far_e,
    cells,
    swept,
    link_a,
    link_z,
    link_r,
    keep,
    all_cells,
    ext,
    cond,
    other,
):
    lane = lax.broadcasted_iota(jnp.int32, (8, 128), 1)

    def own_layer(a, carry):
        for half in HALVES:
            for part in (0, 1):
                rows = pl.ds(8 * part, 8)
                to = pl.ds(8 + 8 * part, 8)
                ext[a + 3, half, to, :] = temp[a, rows, lanes(half)]
                cond[a + 3, half, to, :] = conductivity(mat[a, rows, lanes(half)])
        return carry

    lax.fori_loop(0, SA, own_layer, 0, unroll=4)

    def azim_rim(lower, upper):
        for half in HALVES:
            for n in range(3):
                for source, a in ((lower, 2 - n), (upper, 19 + n)):
                    ext[a, half, pl.ds(8, 16), :] = source[half, pl.ds(16 * n, 16), :]
                    cond[a, half, pl.ds(8, 16), :] = source[
                        half, pl.ds(SOLID_COND + 16 * n, 16), :
                    ]
        all_cells[1] = lower[0, pl.ds(SOLID_CELLS, 8), :]
        all_cells[7] = upper[0, pl.ds(SOLID_CELLS, 8), :]

    by_parity("azim", azim_rim, near_s, far_s)
    below, above = ends(n_axial)

    def axial_rim(lower, upper):
        for half in HALVES:
            for depth in range(3):
                for n in range(20 - 2 * depth):
                    a = 1 + depth + n
                    at = SKIP[depth] + n
                    for source, row, there in (
                        (lower, 7 - depth, below),
                        (upper, 24 + depth, above),
                    ):
                        ext[a, half, pl.ds(row, 1), :] = source[half, pl.ds(at, 1), :]
                        cond[a, half, pl.ds(row, 1), :] = (
                            source[half, pl.ds(END_COND + at, 1), :] * there
                        )
        outside = jnp.full((CAP, 128), SA * SZ * NR, f32)
        for source, dz, there in ((lower, 0, below), (upper, 2, above)):
            for which, half, row in ((0, 1, 0), (3, 0, 0), (6, 0, 8)):
                all_cells[which + dz] = jnp.where(
                    there > 0, source[half, pl.ds(END_CELLS + row, 8), :], outside
                )

    by_parity("axial", axial_rim, near_e, far_e)
    all_cells[4] = cells[...].astype(f32)

    def links(a, carry):
        for row in (5, 13, 21):
            rows = pl.ds(row, 8)
            pair = [cond[a, half, rows, :] for half in HALVES]
            up = shifted(pair, -1, lane)
            up = [up[0], jnp.where(lane == 127, 0.0, up[1])]
            for half in HALVES:
                link_a[a, half, rows, :] = link(pair[half], cond[a + 1, half, rows, :])
                link_z[a, half, rows, :] = link(
                    pair[half], cond[a, half, pl.ds(row + 1, 8), :]
                )
                link_r[a, half, rows, :] = link(pair[half], up[half])
        return carry

    lax.fori_loop(0, SA + 5, links, 0, unroll=3)

    def keeps(a, carry):
        for row in (6, 14, 22):
            rows = pl.ds(row, 8)
            pair = [link_r[a, half, rows, :] for half in HALVES]
            down = shifted(pair, 1, lane)
            for half in HALVES:
                keep[a, half, rows, :] = 1.0 - (
                    link_a[a, half, rows, :]
                    + link_a[a - 1, half, rows, :]
                    + link_z[a, half, rows, :]
                    + link_z[a, half, pl.ds(row - 1, 8), :]
                    + pair[half]
                    + down[half]
                )
        return carry

    lax.fori_loop(1, SA + 5, keeps, 0, unroll=4)

    def once(source, target, first, last, at):
        def layer(a, carry):
            for row in at:
                out = sweep(source, link_a, link_z, link_r, keep, a, row, lane)
                for half in HALVES:
                    target[a, half, pl.ds(row, 8), :] = out[half]
            return carry

        lax.fori_loop(first, last, layer, 0, unroll=2)

    once(ext, other, 1, SA + 5, (6, 14, 22))
    once(other, ext, 2, SA + 4, (7, 15, 23))

    def final(a, carry):
        for part in (0, 1):
            out = sweep(ext, link_a, link_z, link_r, keep, a + 3, 8 + 8 * part, lane)
            for half in HALVES:
                swept[a, pl.ds(8 * part, 8), lanes(half)] = out[half]
        return carry

    lax.fori_loop(0, SA, final, 0, unroll=4)


def deposit_kernel(
    swept_far,
    link_a_far,
    link_z_far,
    link_r_far,
    keep_far,
    arrived,
    all_cells,
    solid_out,
    heat,
    other,
    came,
    swept,
    link_a,
    link_z,
    link_r,
    keep,
    brought,
):
    copies = [
        pltpu.make_async_copy(source, target, brought.at[n])
        for n, (source, target) in enumerate(
            (
                (swept_far, swept),
                (link_a_far, link_a),
                (link_z_far, link_z),
                (link_r_far, link_r),
                (keep_far, keep),
            )
        )
    ]
    for copy in copies:
        copy.start()
    lane = lax.broadcasted_iota(jnp.int32, (8, 128), 1)
    senders = arrived.shape[0]
    for s in range(senders):
        came[pl.ds(s, 1), :] = arrived[s]

    def clear(a, carry):
        for half in HALVES:
            heat[a, half] = jnp.zeros((ROWS, 128), f32)
        return carry

    lax.fori_loop(0, SA + 6, clear, 0, unroll=2)

    values = jnp.transpose(came[...]) * (1.0 / HEAT_CAPACITY)

    def place(which, rows, row_of):
        cell = all_cells[which].astype(jnp.int32)
        value = values[CAP * which : CAP * (which + 1)]
        one, two = split(value)
        at_row = row_of(lax.broadcasted_iota(jnp.int32, (rows, senders), 0))
        at_col = lax.broadcasted_iota(jnp.int32, (NR, senders), 0)
        left, right = [[], []], []
        for c in range(CAP):
            hit = at_row == (cell[c : c + 1] // NR)
            for to, term in zip(left, (one, two)):
                to.append(
                    jnp.where(hit, term[c : c + 1].astype(f32), 0.0).astype(bf16)
                )
            right.append((at_col == cell[c : c + 1] % NR).astype(f32).astype(bf16))
        both = lax.dot_general(
            jnp.concatenate([jnp.concatenate(to, axis=1) for to in left], axis=0),
            jnp.concatenate(right, axis=1),
            (((1,), (1,)), ((), ())),
            preferred_element_type=f32,
        )
        return both[:rows] + both[rows:]

    own = place(4, SA * SZ, lambda j: j)
    for a in range(SA):
        for half in HALVES:
            heat[a + 3, half, pl.ds(8, 16), :] = own[
                16 * a : 16 * a + 16, 128 * half : 128 * half + 128
            ]
    low = place(1, 32, lambda j: j + 14 * SZ)
    high = place(7, 32, lambda j: j)
    for n in range(2):
        for half in HALVES:
            cut = slice(128 * half, 128 * half + 128)
            heat[1 + n, half, pl.ds(8, 16), :] = low[16 * n : 16 * n + 16, cut]
            heat[19 + n, half, pl.ds(8, 16), :] = high[16 * n : 16 * n + 16, cut]
    low = place(3, 32, lambda j: (j // 2) * SZ + 14 + j % 2)
    high = place(5, 32, lambda j: (j // 2) * SZ + j % 2)
    for a in range(SA):
        for half in HALVES:
            cut = slice(128 * half, 128 * half + 128)
            heat[a + 3, half, pl.ds(6, 2), :] = low[2 * a : 2 * a + 2, cut]
            heat[a + 3, half, pl.ds(24, 2), :] = high[2 * a : 2 * a + 2, cut]
    for which, cell_row, a, row in (
        (0, 255, 2, 7),
        (2, 240, 2, 24),
        (6, 15, 19, 7),
        (8, 0, 19, 24),
    ):
        one = place(which, 8, lambda j: jnp.where(j == 0, cell_row, -1))
        for half in HALVES:
            heat[a, half, pl.ds(row, 1), :] = one[0:1, 128 * half : 128 * half + 128]

    for copy in copies:
        copy.wait()

    def middle(a, carry):
        for row in (7, 15, 23):
            out = sweep(heat, link_a, link_z, link_r, keep, a, row, lane)
            for half in HALVES:
                other[a, half, pl.ds(row, 8), :] = (
                    out[half] + heat[a, half, pl.ds(row, 8), :]
                )
        return carry

    lax.fori_loop(2, SA + 4, middle, 0, unroll=2)

    def final(a, carry):
        for part in (0, 1):
            rows = pl.ds(8 * part, 8)
            out = sweep(other, link_a, link_z, link_r, keep, a + 3, 8 + 8 * part, lane)
            for half in HALVES:
                solid_out[a, rows, lanes(half)] = (
                    out[half]
                    + heat[a + 3, half, pl.ds(8 + 8 * part, 8), :]
                    + swept[a, rows, lanes(half)]
                )
        return carry

    lax.fori_loop(0, SA, final, 0, unroll=4)


def call(
    kernel, ins, outs, scratch=(), limit=16, moved=0, far_ins=0, far_outs=0, held=()
):
    here, there = (pl.BlockSpec(memory_space=m) for m in (VMEM, pltpu.HBM))
    kernel_call = pl.pallas_call(
        kernel,
        out_shape=[
            VMEM(s, f32) if n in held else jax.ShapeDtypeStruct(s, f32)
            for n, s in enumerate(outs)
        ],
        in_specs=[there] * far_ins + [here] * (ins - far_ins),
        out_specs=[there] * far_outs + [here] * (len(outs) - far_outs),
        scratch_shapes=list(scratch),
        compiler_params=pltpu.CompilerParams(vmem_limit_bytes=limit * 1024 * 1024),
        cost_estimate=pl.CostEstimate(
            flops=0, bytes_accessed=moved, transcendentals=0
        ),
    )

    def run(*args):
        far = [pltpu.with_memory_space_constraint(x, pltpu.HBM) for x in args[:far_ins]]
        return kernel_call(*far, *args[far_ins:])

    return run


def swap(values, axis, far):
    count = lax.axis_size(axis)
    pairs = [(i, (((i + 1) ^ 1) - 1) % count if far else i ^ 1) for i in range(count)]
    return lax.ppermute(values, axis, pairs)


def per_device(
    n_azim,
    n_axial,
    populations,
    fluid_flags,
    wall_cell,
    wall_drive,
    wall_owner,
    wall_slot,
    receive_cell,
    materials,
    solid_temp,
):
    devices = n_azim * n_axial
    cells = receive_cell.reshape(devices, CAP).T
    azim_msg = (2, AZIM_ROWS, 128)
    axial_msg = (2, AXIAL_ROWS, 128)
    solid_msg = (2, SOLID_ROWS, 128)
    end_msg = (2, END_ROWS, 128)
    fluid = (Q, CA, CZ, NR)
    solid = (SA, SZ, NR)
    fluid_ext = (Q, CA, 2, ROWS, 128)
    solid_ext = (SA + 6, 2, ROWS, 128)
    post, near_z, far_z, token = call(
        first_kernel,
        2,
        [fluid, axial_msg, axial_msg, (8, 128)],
        [
            VMEM(fluid, f32),
            VMEM((CA, CZ, NR), jnp.int32),
            VMEM(axial_msg, f32),
            VMEM(axial_msg, f32),
            pltpu.SemaphoreType.DMA((CA + 1,)),
        ],
        moved=8 << 20,
        far_ins=2,
    )(populations, fluid_flags)
    near_z = swap(near_z, "axial", False)
    far_z = swap(far_z, "axial", True)
    near_s, far_s = call(
        solid_azim_kernel,
        4,
        [solid_msg, solid_msg],
        [
            VMEM((2, 3, SZ, NR), f32),
            VMEM((2, 3, SZ, NR), jnp.int32),
            pltpu.SemaphoreType.DMA((4,)),
        ],
        moved=2 << 20,
        far_ins=2,
    )(solid_temp, materials, cells, token)
    near_s = swap(near_s, "azim", False)
    far_s = swap(far_s, "azim", True)
    near_z, far_z, near_s, far_s = lax.optimization_barrier(
        (near_z, far_z, near_s, far_s)
    )
    ext, opened, near_a, far_a, token = call(
        functools.partial(rim_kernel, n_axial),
        4,
        [fluid_ext, (3, CA, 2, ROWS, 128), azim_msg, azim_msg, (8, 128)],
        [VMEM(azim_msg, f32), VMEM(azim_msg, f32)],
        moved=8 << 20,
        held=(0, 1),
    )(post, fluid_flags, near_z, far_z)
    near_a = swap(near_a, "azim", False)
    far_a = swap(far_a, "azim", True)
    near_e, far_e = call(
        solid_axial_kernel,
        6,
        [end_msg, end_msg],
        [
            VMEM(solid, f32),
            VMEM(solid, jnp.int32),
            VMEM(end_msg, f32),
            VMEM(end_msg, f32),
            pltpu.SemaphoreType.DMA((2,)),
        ],
        moved=2 << 20,
        far_ins=2,
    )(solid_temp, materials, cells, near_s, far_s, token)
    near_e = swap(near_e, "axial", False)
    far_e = swap(far_e, "axial", True)
    rows = wall_cell.shape[0]
    fluid_out, message = call(
        functools.partial(fluid_kernel, n_azim, n_axial),
        8,
        [fluid, (devices, 1, 128)],
        [
            VMEM((3, CA + 2, 2, ROWS, 128), f32),
            VMEM((Q, CA + 2, 2, ROWS, 128), f32),
            VMEM((2, 13, 2, ROWS, 128), f32),
            VMEM((CA * CZ, NR), f32),
            VMEM(fluid, f32),
            pltpu.SemaphoreType.DMA((CA,)),
        ],
        limit=28,
        moved=16 << 20,
        far_outs=1,
    )(
        pltpu.with_memory_space_constraint(ext, VMEM),
        pltpu.with_memory_space_constraint(opened, VMEM),
        near_a,
        far_a,
        wall_cell.reshape(1, rows),
        wall_drive.reshape(1, rows),
        wall_owner.reshape(1, rows),
        wall_slot.reshape(1, rows),
    )
    arrived = lax.all_to_all(
        message, ("azim", "axial"), split_axis=0, concat_axis=0, tiled=True
    )
    *swept, all_cells = call(
        functools.partial(solid_kernel, n_axial),
        7,
        [solid] + [solid_ext] * 4 + [(9, CAP, devices)],
        [VMEM(solid_ext, f32)] * 3,
        moved=8 << 20,
    )(solid_temp, materials, near_s, far_s, near_e, far_e, cells)
    (solid_out,) = call(
        deposit_kernel,
        7,
        [solid],
        [
            VMEM(solid_ext, f32),
            VMEM(solid_ext, f32),
            VMEM((devices, 128), f32),
            VMEM(solid, f32),
        ]
        + [VMEM(solid_ext, f32)] * 4
        + [pltpu.SemaphoreType.DMA((5,))],
        moved=8 << 20,
        far_ins=5,
    )(*swept, arrived, all_cells)
    return fluid_out, solid_out


def solution(mesh):
    both = ("azim", "axial")
    in_specs = (
        P(None, "azim", "axial", None),
        P("azim", "axial", None),
        P(both),
        P(both),
        P(both),
        P(both),
        P(both),
        P("azim", "axial", None),
        P("azim", "axial", None),
    )
    out_specs = (P(None, "azim", "axial", None), P("azim", "axial", None))
    return jax.shard_map(
        functools.partial(per_device, mesh.shape["azim"], mesh.shape["axial"]),
        mesh=mesh,
        in_specs=in_specs,
        out_specs=out_specs,
        check_vma=False,
    )
```

```python
import functools

import jax
import jax.numpy as jnp
from jax import lax
from jax.experimental import pallas as pl
from jax.experimental.pallas import tpu as pltpu
from jax.sharding import PartitionSpec as P

CAP = 8
STEP_A = [0, 1, -1, 0, 0, 0, 0, 1, -1, 1, -1, 1, -1, 1, -1, 0, 0, 0, 0]
STEP_Z = [0, 0, 0, 1, -1, 0, 0, 1, -1, -1, 1, 0, 0, 0, 0, 1, -1, 1, -1]
STEP_R = [0, 0, 0, 0, 0, 1, -1, 0, 0, 0, 0, 1, -1, -1, 1, 1, -1, -1, 1]
OPPOSITE = [0, 2, 1, 4, 3, 6, 5, 8, 7, 10, 9, 12, 11, 14, 13, 16, 15, 18, 17]
AZIM_UP = [i for i in range(19) if STEP_A[i] == 1]
AZIM_DOWN = [i for i in range(19) if STEP_A[i] == -1]
AXIAL_UP = [i for i in range(19) if STEP_Z[i] == 1]
AXIAL_DOWN = [i for i in range(19) if STEP_Z[i] == -1]
RELAXATION = 1.25
SPEED_REF = 0.05
HEAT_CAPACITY = 6.5

Q = 19
CA, CZ, NR = 8, 16, 256
SA, SZ = 16, 16
HALVES = (0, 1)
ROWS = 32

PER_PLACE = 26
AXIAL_ROWS = CA * PER_PLACE
STREAMED_ROW = 100
SUMS_ROW = 190
FLAG_ROW = 244
AZIM_ROWS = 264
SOLID_COND = 48
SOLID_CELLS = 96
SOLID_ROWS = 104
SKIP = (0, 20, 38)
END_COND = 54
END_CELLS = 112
END_ROWS = 128

GROUP = 5

VMEM = pltpu.VMEM
f32 = jnp.float32
bf16 = jnp.bfloat16


def lanes(half):
    return pl.ds(128 * half, 128)


def moments(f):
    rho = f[0]
    for i in range(1, Q):
        rho = rho + f[i]
    d = [f[i] - f[i + 1] for i in range(1, Q, 2)]
    mom_a = d[0] + d[3] + d[4] + d[5] + d[6]
    mom_z = d[1] + d[3] - d[4] + d[7] + d[8]
    mom_r = d[2] + d[5] - d[6] + d[7] - d[8]
    return rho, mom_a, mom_z, mom_r


def collide_part(sums, f, flag, which):
    rho, mom_a, mom_z, mom_r = sums
    open_cell = flag > 0
    inv = 1.0 / jnp.where(open_cell, rho, 1.0)
    omega = jnp.where(open_cell, RELAXATION, 0.0)
    keep = 1.0 - omega
    ua, uz, ur = mom_a * inv, mom_z * inv, mom_r * inv
    base = 1.0 - 1.5 * (ua * ua + uz * uz + ur * ur)
    scale = omega * rho
    face, edge = scale * (1.0 / 18.0), scale * (1.0 / 36.0)
    post = {}
    if 0 in which:
        post[0] = keep * f[0] + scale * (1.0 / 3.0) * base
    for n, proj in enumerate(
        (ua, uz, ur, ua + uz, ua - uz, ua + ur, ua - ur, uz + ur, uz - ur)
    ):
        weight = face if n < 3 else edge
        one, two = 2 * n + 1, 2 * n + 2
        if one in which or two in which:
            even = weight * (base + 4.5 * proj * proj)
            odd = weight * (3.0 * proj)
        if one in which:
            post[one] = keep * f[one] + (even + odd)
        if two in which:
            post[two] = keep * f[two] + (even - odd)
    return post


def collide(f, flag):
    return collide_part(moments(f), f, flag, range(Q))


def conductivity(material):
    return jnp.where(
        material == 0,
        1.0,
        jnp.where(material == 1, 0.55, jnp.where(material == 2, 0.2, 0.8)),
    ).astype(f32)


def by_parity(axis, body, near, far):
    odd = lax.rem(lax.axis_index(axis), 2) == 1

    @pl.when(odd)
    def _():
        body(near, far)

    @pl.when(jnp.logical_not(odd))
    def _():
        body(far, near)


def first_kernel(
    f_far, flags_far, post, air, near, far, token, f, flags, low, high, come
):
    flags_copy = pltpu.make_async_copy(flags_far, flags, come.at[CA])

    def layer_copy(a):
        return pltpu.make_async_copy(f_far.at[:, a], f.at[:, a], come.at[a])

    flags_copy.start()
    for a in range(CA):
        layer_copy(a).start()
    token[...] = jnp.zeros((8, 128), f32)
    flags_copy.wait()

    def layer(a, carry):
        layer_copy(a).wait()
        for half in HALVES:
            for part in (0, 1):
                rows = pl.ds(8 * part, 8)
                flag = flags[a, rows, lanes(half)].astype(f32)
                out = collide([f[i, a, rows, lanes(half)] for i in range(Q)], flag)
                for i in range(Q):
                    post[i, a, half, rows, :] = out[i]
                air[a, half, rows, :] = flag
                place = a * PER_PLACE
                target, inner, edge, near_edge = (
                    (low, AXIAL_DOWN, 0, 1) if part == 0 else (high, AXIAL_UP, 7, 6)
                )

                def put(row, value, at):
                    target[half, pl.ds(place + row, 1), :] = value[at : at + 1]

                for i in range(Q):
                    put(i, out[i], edge)
                for n, i in enumerate(inner):
                    put(Q + n, out[i], near_edge)
                put(24, flag, edge)
                put(25, flag, near_edge)
        return carry

    lax.fori_loop(0, CA, layer, 0)

    def hand_over(down, up):
        down[...] = low[...]
        up[...] = high[...]

    by_parity("axial", hand_over, near, far)


def solid_azim_kernel(
    temp_far, mat_far, cells, token, near, far, packed, temp, mat, come
):
    packed[...] = jnp.zeros((8, 128), f32)
    copies = []
    for n, layers in enumerate((pl.ds(0, 3), pl.ds(SA - 3, 3))):
        for k, (source, target) in enumerate(((temp_far, temp), (mat_far, mat))):
            copy = pltpu.make_async_copy(
                source.at[layers], target.at[n], come.at[2 * n + k]
            )
            copy.start()
            copies.append(copy)
    for copy in copies:
        copy.wait()

    def fill(down, up):
        for side, target in enumerate((down, up)):
            for half in HALVES:
                for n in range(3):
                    a = n if side == 0 else 2 - n
                    target[half, pl.ds(16 * n, 16), :] = temp[side, a, :, lanes(half)]
                    target[half, pl.ds(SOLID_COND + 16 * n, 16), :] = conductivity(
                        mat[side, a, :, lanes(half)]
                    )
            target[0, pl.ds(SOLID_CELLS, 8), :] = cells[...].astype(f32)

    by_parity("azim", fill, near, far)


def solid_axial_kernel(
    temp_far,
    mat_far,
    cells,
    near_s,
    far_s,
    token,
    near,
    far,
    temp,
    mat,
    low,
    high,
    come,
):
    copies = [
        pltpu.make_async_copy(source, target, come.at[n])
        for n, (source, target) in enumerate(((temp_far, temp), (mat_far, mat)))
    ]
    for copy in copies:
        copy.start()

    def azim_ends(lower, upper):
        for target, edge, step in ((low, 0, 1), (high, SZ - 1, -1)):
            for half in HALVES:
                for depth in range(2):
                    z = edge + step * depth
                    for n in range(2 - depth):
                        for source, at in (
                            (lower, 1 - depth - n),
                            (upper, 18 - depth + n),
                        ):
                            for kind, here in ((0, 0), (END_COND, SOLID_COND)):
                                target[half, pl.ds(kind + SKIP[depth] + at, 1), :] = (
                                    source[half, pl.ds(here + 16 * n + z, 1), :]
                                )
            target[0, pl.ds(END_CELLS, 8), :] = cells[...].astype(f32)
            target[1, pl.ds(END_CELLS, 8), :] = lower[0, pl.ds(SOLID_CELLS, 8), :]
            target[0, pl.ds(END_CELLS + 8, 8), :] = upper[0, pl.ds(SOLID_CELLS, 8), :]

    by_parity("azim", azim_ends, near_s, far_s)
    for copy in copies:
        copy.wait()

    def layer(a, carry):
        for half in HALVES:
            for part, target in ((0, low), (1, high)):
                rows = pl.ds(8 * part, 8)
                t = temp[a, rows, lanes(half)]
                c = conductivity(mat[a, rows, lanes(half)])
                for depth in range(3):
                    at = depth if part == 0 else 7 - depth
                    row = SKIP[depth] + 2 - depth + a
                    target[half, pl.ds(row, 1), :] = t[at : at + 1]
                    target[half, pl.ds(END_COND + row, 1), :] = c[at : at + 1]
        return carry

    lax.fori_loop(0, SA, layer, 0, unroll=4)

    def hand_over(down, up):
        down[...] = low[...]
        up[...] = high[...]

    by_parity("axial", hand_over, near, far)


def ends(n_axial):
    z = lax.axis_index("axial")
    return (
        jnp.where(z > 0, 1.0, 0.0).astype(f32),
        jnp.where(z < n_axial - 1, 1.0, 0.0).astype(f32),
    )


def shifted(pair, step, lane):
    if step == 0:
        return pair
    turn = 1 if step == 1 else 127
    at = 0 if step == 1 else 127
    a, b = (pltpu.roll(x, turn, 1) for x in pair)
    return [jnp.where(lane == at, b, a), jnp.where(lane == at, a, b)]


def split(x):
    one = x.astype(bf16)
    return one, (x - one.astype(f32)).astype(bf16)


def stream(
    source,
    opened,
    at_a,
    flag_a,
    row,
    lane,
    which=None,
    sides=None,
    rim=None,
    beyond=False,
):
    rows = pl.ds(row, 8)
    out = [[], []]
    for i in range(Q) if which is None else which:
        own = OPPOSITE[i]
        from_rows = pl.ds(row - STEP_Z[i], 8)

        def before(half):
            if rim and i in rim:
                return sides[rim[i][0], rim[i][1], half, from_rows, :]
            if beyond:
                return source[i, at_a, half, from_rows, :]
            return source[i, at_a - STEP_A[i], half, from_rows, :]

        def back(half):
            if beyond:
                return sides[rim[own][0], rim[own][1], half, rows, :]
            return source[own, at_a, half, rows, :]

        moved = shifted([before(half) for half in HALVES], STEP_R[i], lane)
        for half in HALVES:
            if i == 0:
                out[half].append(moved[half])
                continue
            from_a = flag_a if beyond else flag_a - STEP_A[i]
            mask = opened[STEP_R[i] % 3, from_a, half, from_rows, :]
            out[half].append(jnp.where(mask > 0, moved[half], back(half)))
    return out


def rim_kernel(
    n_axial,
    post,
    air,
    near_z,
    far_z,
    packed,
    ext,
    opened,
    near,
    far,
    low,
    high,
):
    lane = lax.broadcasted_iota(jnp.int32, (8, 128), 1)
    below, above = ends(n_axial)

    def own_layer(a, carry):
        to = pl.ds(8, 16)
        for half in HALVES:
            for i in range(Q):
                ext[i, a, half, to, :] = post[i, a, half]
            opened[0, a, half, to, :] = air[a, half]
        return carry

    lax.fori_loop(0, CA, own_layer, 0)

    def axial_rim(lower, upper):
        def layer(a, carry):
            place = a * PER_PLACE
            for half in HALVES:
                for source, first, last, moving, there in (
                    (lower, 7, 6, AXIAL_UP, below),
                    (upper, 24, 25, AXIAL_DOWN, above),
                ):

                    def get(row):
                        return source[half, pl.ds(place + row, 1), :]

                    for i in range(Q):
                        ext[i, a, half, pl.ds(first, 1), :] = get(i)
                    for n, i in enumerate(moving):
                        ext[i, a, half, pl.ds(last, 1), :] = get(Q + n)
                    opened[0, a, half, pl.ds(first, 1), :] = get(24) * there
                    opened[0, a, half, pl.ds(last, 1), :] = get(25) * there
            return carry

        lax.fori_loop(0, CA, layer, 0, unroll=2)
    by_parity("axial", axial_rim, near_z, far_z)

    def turn(a, carry):
        turn_flags(opened, a, lane)
        return carry

    lax.fori_loop(0, CA, turn, 0, unroll=2)

    for target, layer, moving, step in (
        (low, 0, AZIM_DOWN, -1),
        (high, CA - 1, AZIM_UP, 1),
    ):
        for half in HALVES:
            for n, i in enumerate(moving):
                target[half, pl.ds(20 * n, 20), :] = ext[
                    i, layer, half, pl.ds(6, 20), :
                ]
            target[half, pl.ds(FLAG_ROW, 20), :] = opened[
                0, layer, half, pl.ds(6, 20), :
            ]
        which = [i for i in range(Q) if STEP_A[i] in (0, step)]
        for row in (7, 15, 17):
            moved = stream(ext, opened, layer, layer, row, lane, which)
            for half in HALVES:
                new = dict(zip(which, moved[half]))
                at = row - 7
                for n, i in enumerate(moving):
                    target[half, pl.ds(STREAMED_ROW + 18 * n + at, 8), :] = new[i]
                still = [i for i in which if STEP_A[i] == 0]
                for n, table in enumerate(([1] * Q, STEP_Z, STEP_R)):
                    total = None
                    for i in still:
                        if table[i]:
                            term = new[i] * table[i]
                            total = term if total is None else total + term
                    target[half, pl.ds(SUMS_ROW + 18 * n + at, 8), :] = total

    def hand_over(down, up):
        down[...] = low[...]
        up[...] = high[...]

    by_parity("azim", hand_over, near, far)


def turn_flags(opened, a, lane):
    for part in range(4):
        rows = pl.ds(8 * part, 8)
        pair = [opened[0, a, half, rows, :] for half in HALVES]
        up = shifted(pair, 1, lane)
        down = shifted(pair, -1, lane)
        opened[1, a, 0, rows, :] = jnp.where(lane == 0, 0.0, up[0])
        opened[1, a, 1, rows, :] = up[1]
        opened[2, a, 0, rows, :] = down[0]
        opened[2, a, 1, rows, :] = jnp.where(lane == 127, 0.0, down[1])


def step_two(second, opened, a, flag_a, lane, speeds, target, at):
    for part in (0, 1):
        moved = stream(second, opened, a + 1, flag_a, 8 + 8 * part, lane)
        for half in HALVES:
            for i in range(Q):
                target[i, at, pl.ds(8 * part, 8), lanes(half)] = moved[half][i]
            rho, mom_a, mom_z, mom_r = moments(moved[half])
            inv = 1.0 / rho
            ua, uz, ur = mom_a * inv, mom_z * inv, mom_r * inv
            speeds[pl.ds(a * CZ + 8 * part, 8), lanes(half)] = jnp.sqrt(
                ua * ua + uz * uz + ur * ur + 1e-06
            )


def inner_kernel(
    ext, opened, fluid_far, second, speeds, token, fluid_out, layers_out
):
    token[...] = jnp.zeros((8, 128), f32)
    lane = lax.broadcasted_iota(jnp.int32, (8, 128), 1)

    def first_step(a, carry):
        for row in (7, 15, 17):
            moved = stream(ext, opened, a, a, row, lane)
            for half in HALVES:
                out = collide(moved[half], opened[0, a, half, pl.ds(row, 8), :])
                for i in range(Q):
                    second[i, a + 1, half, pl.ds(row, 8), :] = out[i]
        return carry

    lax.fori_loop(1, CA - 1, first_step, 0)

    def layer_copy(n):
        return pltpu.make_async_copy(
            fluid_out.at[:, n], fluid_far.at[:, n + 2], layers_out.at[n]
        )

    def second_step(n, carry):
        step_two(second, opened, n + 2, n + 2, lane, speeds, fluid_out, n)
        layer_copy(n).start()
        return carry

    lax.fori_loop(0, CA - 4, second_step, 0)
    for n in range(CA - 4):
        layer_copy(n).wait()


def outer_kernel(
    n_azim,
    n_axial,
    fluid_so_far,
    second_so_far,
    inner_speeds,
    ext,
    own_opened,
    near_a,
    far_a,
    cell,
    drive,
    owner,
    slot,
    fluid_far,
    second,
    message,
    opened,
    sides,
    speeds,
    fluid_out,
    layers_out,
):
    lane = lax.broadcasted_iota(jnp.int32, (8, 128), 1)
    inside = pl.ds(2 * CZ, (CA - 4) * CZ)
    speeds[inside, :] = inner_speeds[inside, :]

    def own_flags(a, carry):
        for k in range(3):
            for half in HALVES:
                opened[k, a + 1, half] = own_opened[k, a, half]
        return carry

    lax.fori_loop(0, CA, own_flags, 0, unroll=2)

    def azim_rim(lower, upper):
        for side, (source, a) in enumerate(((lower, 0), (upper, CA + 1))):
            for half in HALVES:
                for n in range(5):
                    sides[side, n, half, pl.ds(6, 20), :] = source[
                        half, pl.ds(20 * n, 20), :
                    ]
                for n in range(8):
                    sides[side, 5 + n, half, pl.ds(7, 18), :] = source[
                        half, pl.ds(STREAMED_ROW + 18 * n, 18), :
                    ]
                opened[0, a, half, pl.ds(6, 20), :] = source[
                    half, pl.ds(FLAG_ROW, 20), :
                ]

    by_parity("azim", azim_rim, near_a, far_a)
    turn_flags(opened, 0, lane)
    turn_flags(opened, CA + 1, lane)

    def finish(a, row, moved):
        for half in HALVES:
            out = collide(moved[half], opened[0, a + 1, half, pl.ds(row, 8), :])
            for i in range(Q):
                second[i, a + 1, half, pl.ds(row, 8), :] = out[i]

    def layer_copy(n, a):
        return pltpu.make_async_copy(
            fluid_out.at[:, n], fluid_far.at[:, a], layers_out.at[n]
        )

    for side, (a, inward, outward) in enumerate(
        ((0, AZIM_UP, AZIM_DOWN), (CA - 1, AZIM_DOWN, AZIM_UP))
    ):
        rim = {i: (side, n) for n, i in enumerate(inward)}
        beyond = 0 if side == 0 else CA + 1

        def edge_step(n, carry):
            row = 7 + 8 * n
            finish(a, row, stream(ext, opened, a, a + 1, row, lane, None, sides, rim))
            far_in = stream(
                ext, opened, a, a + 1, row, lane, outward, sides, rim, beyond=True
            )
            for half in HALVES:
                rows = pl.ds(row, 8)

                def at(n):
                    return sides[side, n, half, rows, :]

                new = {i: at(5 + n) for n, i in enumerate(inward)}
                new.update(zip(outward, far_in[half]))
                sums = [at(10), None, at(11), at(12)]
                for k, table in enumerate(([1] * Q, STEP_A, STEP_Z, STEP_R)):
                    for i in inward + outward:
                        if table[i]:
                            term = new[i] * table[i]
                            sums[k] = term if sums[k] is None else sums[k] + term
                out = collide_part(
                    sums, new, opened[0, beyond, half, rows, :], inward
                )
                for i in inward:
                    second[i, beyond, half, rows, :] = out[i]
            return carry

        lax.fori_loop(0, 3, edge_step, 0)

        def second_step(n, carry):
            layer = n + side * (CA - 2)
            at = n + 2 * side
            step_two(second, opened, layer, layer + 1, lane, speeds, fluid_out, at)
            layer_copy(at, layer).start()
            return carry

        lax.fori_loop(0, 2, second_step, 0)


    rows_here = cell.shape[1]
    place = cell[...]
    row_hot = (
        lax.broadcasted_iota(jnp.int32, (CA * CZ, rows_here), 0) == place // NR
    ).astype(f32).astype(bf16)
    turned = jnp.transpose(speeds[...])
    picked = jnp.zeros((NR, rows_here), f32)
    for term in split(turned):
        picked = picked + jnp.dot(term, row_hot, preferred_element_type=f32)
    column = lax.broadcasted_iota(jnp.int32, (NR, rows_here), 0) == place % NR
    speed = jnp.sum(jnp.where(column, picked, 0.0), axis=0, keepdims=True)
    flux = drive[...] * (0.2 + speed / SPEED_REF)
    devices = n_azim * n_axial
    owner_hot = (
        lax.broadcasted_iota(jnp.int32, (devices, rows_here), 0) == owner[...]
    ).astype(f32).astype(bf16)
    slotted = jnp.where(
        lax.broadcasted_iota(jnp.int32, (128, rows_here), 0) == slot[...], flux, 0.0
    )
    sent = jnp.zeros((devices, 128), f32)
    for term in split(slotted):
        sent = sent + lax.dot_general(
            owner_hot, term, (((1,), (1,)), ((), ())), preferred_element_type=f32
        )
    total = jnp.zeros((devices, 128), f32)
    for da in (-1, 0, 1):
        for dz in (-1, 0, 1):
            which = (da + 1) * 3 + dz + 1
            back = (-(da * n_axial + dz)) % devices
            moved = pltpu.roll(sent, back, 0) if back else sent
            total = total + (pltpu.roll(moved, CAP * which, 1) if which else moved)
    for o in range(devices):
        message[o, :, :] = total[o : o + 1]
    for n, a in enumerate((0, 1, CA - 2, CA - 1)):
        layer_copy(n, a).wait()


def link(first, second):
    joined = first + second
    good = joined > 0
    return jnp.where(
        good,
        (2.0 / HEAT_CAPACITY) * first * second / jnp.where(good, joined, 1.0),
        0.0,
    )


def sweep(source, link_a, link_z, link_r, keep, a, row, lane):
    rows = pl.ds(row, 8)
    pair = [source[a, half, rows, :] for half in HALVES]
    lr = [link_r[a, half, rows, :] for half in HALVES]
    up = shifted(pair, -1, lane)
    down = shifted([x * y for x, y in zip(pair, lr)], 1, lane)
    out = []
    for half in HALVES:
        total = keep[a, half, rows, :] * pair[half]
        total = total + link_a[a, half, rows, :] * source[a + 1, half, rows, :]
        total = total + link_a[a - 1, half, rows, :] * source[a - 1, half, rows, :]
        total = (
            total + link_z[a, half, rows, :] * source[a, half, pl.ds(row + 1, 8), :]
        )
        total = (
            total
            + link_z[a, half, pl.ds(row - 1, 8), :]
            * source[a, half, pl.ds(row - 1, 8), :]
        )
        out.append(total + lr[half] * up[half] + down[half])
    return out


def solid_kernel(
    n_axial,
    temp_far,
    mat_far,
    near_s,
    far_s,
    near_e,
    far_e,
    cells,
    swept,
    links_out,
    all_cells,
    link_a,
    link_z,
    link_r,
    keep,
    ext,
    cond,
    other,
    temp,
    mat,
    come,
):
    copies = [
        pltpu.make_async_copy(source, target, come.at[n])
        for n, (source, target) in enumerate(((temp_far, temp), (mat_far, mat)))
    ]
    for copy in copies:
        copy.start()
    for copy in copies:
        copy.wait()
    lane = lax.broadcasted_iota(jnp.int32, (8, 128), 1)

    def own_layer(a, carry):
        for half in HALVES:
            for part in (0, 1):
                rows = pl.ds(8 * part, 8)
                to = pl.ds(8 + 8 * part, 8)
                ext[a + 3, half, to, :] = temp[a, rows, lanes(half)]
                cond[a + 3, half, to, :] = conductivity(mat[a, rows, lanes(half)])
        return carry

    lax.fori_loop(0, SA, own_layer, 0, unroll=4)

    def azim_rim(lower, upper):
        for half in HALVES:
            for n in range(3):
                for source, a in ((lower, 2 - n), (upper, 19 + n)):
                    ext[a, half, pl.ds(8, 16), :] = source[half, pl.ds(16 * n, 16), :]
                    cond[a, half, pl.ds(8, 16), :] = source[
                        half, pl.ds(SOLID_COND + 16 * n, 16), :
                    ]
        all_cells[1] = lower[0, pl.ds(SOLID_CELLS, 8), :]
        all_cells[7] = upper[0, pl.ds(SOLID_CELLS, 8), :]

    by_parity("azim", azim_rim, near_s, far_s)
    below, above = ends(n_axial)

    def axial_rim(lower, upper):
        for half in HALVES:
            for depth in range(3):
                for n in range(20 - 2 * depth):
                    a = 1 + depth + n
                    at = SKIP[depth] + n
                    for source, row, there in (
                        (lower, 7 - depth, below),
                        (upper, 24 + depth, above),
                    ):
                        ext[a, half, pl.ds(row, 1), :] = source[half, pl.ds(at, 1), :]
                        cond[a, half, pl.ds(row, 1), :] = (
                            source[half, pl.ds(END_COND + at, 1), :] * there
                        )
        outside = jnp.full((CAP, 128), SA * SZ * NR, f32)
        for source, dz, there in ((lower, 0, below), (upper, 2, above)):
            for which, half, row in ((0, 1, 0), (3, 0, 0), (6, 0, 8)):
                all_cells[which + dz] = jnp.where(
                    there > 0, source[half, pl.ds(END_CELLS + row, 8), :], outside
                )

    by_parity("axial", axial_rim, near_e, far_e)
    all_cells[4] = cells[...].astype(f32)

    def links(a, carry):
        for row in (5, 13, 21):
            rows = pl.ds(row, 8)
            pair = [cond[a, half, rows, :] for half in HALVES]
            up = shifted(pair, -1, lane)
            up = [up[0], jnp.where(lane == 127, 0.0, up[1])]
            for half in HALVES:
                link_a[a, half, rows, :] = link(pair[half], cond[a + 1, half, rows, :])
                link_z[a, half, rows, :] = link(
                    pair[half], cond[a, half, pl.ds(row + 1, 8), :]
                )
                link_r[a, half, rows, :] = link(pair[half], up[half])
        return carry

    lax.fori_loop(0, SA + 5, links, 0, unroll=3)

    def keeps(a, carry):
        for row in (6, 14, 22):
            rows = pl.ds(row, 8)
            pair = [link_r[a, half, rows, :] for half in HALVES]
            down = shifted(pair, 1, lane)
            for half in HALVES:
                keep[a, half, rows, :] = 1.0 - (
                    link_a[a, half, rows, :]
                    + link_a[a - 1, half, rows, :]
                    + link_z[a, half, rows, :]
                    + link_z[a, half, pl.ds(row - 1, 8), :]
                    + pair[half]
                    + down[half]
                )
        return carry

    lax.fori_loop(1, SA + 5, keeps, 0, unroll=4)

    def trim(a, carry):
        for half in HALVES:
            for n, kind in enumerate((link_a, link_z, link_r)):
                links_out[n, a, half] = kind[a + 1, half, pl.ds(6, 24), :]
        return carry

    lax.fori_loop(0, SA + 4, trim, 0, unroll=2)

    def once(source, target, first, last, at):
        def layer(a, carry):
            for row in at:
                out = sweep(source, link_a, link_z, link_r, keep, a, row, lane)
                for half in HALVES:
                    target[a, half, pl.ds(row, 8), :] = out[half]
            return carry

        lax.fori_loop(first, last, layer, 0, unroll=2)

    once(ext, other, 1, SA + 5, (6, 14, 22))
    once(other, ext, 2, SA + 4, (7, 15, 23))

    def final(a, carry):
        for part in (0, 1):
            out = sweep(ext, link_a, link_z, link_r, keep, a + 3, 8 + 8 * part, lane)
            for half in HALVES:
                swept[a, pl.ds(8 * part, 8), lanes(half)] = out[half]
        return carry

    lax.fori_loop(0, SA, final, 0, unroll=4)


def deposit_kernel(
    swept_far,
    links_far,
    arrived,
    all_cells,
    solid_out,
    heat,
    other,
    came,
    swept,
    links,
    brought,
):
    groups = [
        pltpu.make_async_copy(
            links_far.at[:, pl.ds(GROUP * n, GROUP)],
            links.at[:, pl.ds(GROUP * n, GROUP)],
            brought.at[n],
        )
        for n in range((SA + 4) // GROUP)
    ]
    swept_copy = pltpu.make_async_copy(swept_far, swept, brought.at[len(groups)])
    for copy in groups:
        copy.start()
    swept_copy.start()
    lane = lax.broadcasted_iota(jnp.int32, (8, 128), 1)
    senders = arrived.shape[0]
    for s in range(senders):
        came[pl.ds(s, 1), :] = arrived[s]

    def clear(a, carry):
        for half in HALVES:
            heat[a, half] = jnp.zeros((24, 128), f32)
        return carry

    lax.fori_loop(0, SA + 4, clear, 0, unroll=2)
    values = jnp.transpose(came[...]) * (1.0 / HEAT_CAPACITY)

    def place(which, rows, row_of):
        cell = all_cells[which].astype(jnp.int32)
        value = values[CAP * which : CAP * (which + 1)]
        one, two = split(value)
        at_row = row_of(lax.broadcasted_iota(jnp.int32, (rows, senders), 0))
        at_col = lax.broadcasted_iota(jnp.int32, (NR, senders), 0)
        left, right = [[], []], []
        for c in range(CAP):
            hit = at_row == (cell[c : c + 1] // NR)
            for to, term in zip(left, (one, two)):
                to.append(
                    jnp.where(hit, term[c : c + 1].astype(f32), 0.0).astype(bf16)
                )
            right.append((at_col == cell[c : c + 1] % NR).astype(f32).astype(bf16))
        both = lax.dot_general(
            jnp.concatenate([jnp.concatenate(to, axis=1) for to in left], axis=0),
            jnp.concatenate(right, axis=1),
            (((1,), (1,)), ((), ())),
            preferred_element_type=f32,
        )
        return both[:rows] + both[rows:]

    own = place(4, SA * SZ, lambda j: j)
    for a in range(SA):
        for half in HALVES:
            heat[a + 2, half, pl.ds(2, 16), :] = own[
                16 * a : 16 * a + 16, 128 * half : 128 * half + 128
            ]
    low = place(1, 32, lambda j: j + 14 * SZ)
    high = place(7, 32, lambda j: j)
    for n in range(2):
        for half in HALVES:
            cut = slice(128 * half, 128 * half + 128)
            heat[n, half, pl.ds(2, 16), :] = low[16 * n : 16 * n + 16, cut]
            heat[18 + n, half, pl.ds(2, 16), :] = high[16 * n : 16 * n + 16, cut]
    low = place(3, 32, lambda j: (j // 2) * SZ + 14 + j % 2)
    high = place(5, 32, lambda j: (j // 2) * SZ + j % 2)
    for a in range(SA):
        for half in HALVES:
            cut = slice(128 * half, 128 * half + 128)
            heat[a + 2, half, pl.ds(0, 2), :] = low[2 * a : 2 * a + 2, cut]
            heat[a + 2, half, pl.ds(18, 2), :] = high[2 * a : 2 * a + 2, cut]
    for which, cell_row, a, row in (
        (0, 255, 1, 1),
        (2, 240, 1, 18),
        (6, 15, 18, 1),
        (8, 0, 18, 18),
    ):
        one = place(which, 8, lambda j: jnp.where(j == 0, cell_row, -1))
        for half in HALVES:
            heat[a, half, pl.ds(row, 1), :] = one[0:1, 128 * half : 128 * half + 128]

    def spread(source, a, row):
        rows, before, after = (pl.ds(row + n, 8) for n in (0, -1, 1))
        pair = [source[a, half, rows, :] for half in HALVES]
        up = shifted(pair, -1, lane)
        flow = [links[2, a, half, rows, :] * (up[half] - pair[half]) for half in HALVES]
        back = shifted(flow, 1, lane)
        out = []
        for half in HALVES:
            here = pair[half]
            out.append(
                here
                + links[0, a, half, rows, :] * (source[a + 1, half, rows, :] - here)
                + links[0, a - 1, half, rows, :] * (source[a - 1, half, rows, :] - here)
                + links[1, a, half, rows, :] * (source[a, half, after, :] - here)
                + links[1, a, half, before, :] * (source[a, half, before, :] - here)
                + (flow[half] - back[half])
                + heat[a, half, rows, :]
            )
        return out

    def middle(a, carry):
        for row in (1, 9, 11):
            out = spread(heat, a, row)
            for half in HALVES:
                other[a, half, pl.ds(row, 8), :] = out[half]
        return carry

    for n, copy in enumerate(groups):
        copy.wait()
        first = max(GROUP * n, 1)
        last = min(GROUP * (n + 1), SA + 3)
        lax.fori_loop(first, last, middle, 0, unroll=last - first)
    swept_copy.wait()

    def final(a, carry):
        for part in (0, 1):
            rows = pl.ds(8 * part, 8)
            out = spread(other, a + 2, 2 + 8 * part)
            for half in HALVES:
                solid_out[a, rows, lanes(half)] = (
                    out[half] + swept[a, rows, lanes(half)]
                )
        return carry

    lax.fori_loop(0, SA, final, 0, unroll=4)


def call(
    kernel, ins, outs, scratch=(), limit=16, moved=0, far_ins=0, far_outs=0, held=(), aliases={}
):
    here, there = (pl.BlockSpec(memory_space=m) for m in (VMEM, pltpu.HBM))
    kernel_call = pl.pallas_call(
        kernel,
        out_shape=[
            VMEM(s, f32) if n in held else jax.ShapeDtypeStruct(s, f32)
            for n, s in enumerate(outs)
        ],
        in_specs=[there] * far_ins + [here] * (ins - far_ins),
        out_specs=[there] * far_outs + [here] * (len(outs) - far_outs),
        scratch_shapes=list(scratch),
        input_output_aliases=aliases,
        compiler_params=pltpu.CompilerParams(vmem_limit_bytes=limit * 1024 * 1024),
        cost_estimate=pl.CostEstimate(
            flops=0, bytes_accessed=moved, transcendentals=0
        ),
    )

    def run(*args):
        far = [pltpu.with_memory_space_constraint(x, pltpu.HBM) for x in args[:far_ins]]
        return kernel_call(*far, *args[far_ins:])

    return run


def swap(values, axis, far):
    count = lax.axis_size(axis)
    pairs = [(i, (((i + 1) ^ 1) - 1) % count if far else i ^ 1) for i in range(count)]
    return lax.ppermute(values, axis, pairs)


def per_device(
    n_azim,
    n_axial,
    populations,
    fluid_flags,
    wall_cell,
    wall_drive,
    wall_owner,
    wall_slot,
    receive_cell,
    materials,
    solid_temp,
):
    devices = n_azim * n_axial
    cells = receive_cell.reshape(devices, CAP).T
    azim_msg = (2, AZIM_ROWS, 128)
    axial_msg = (2, AXIAL_ROWS, 128)
    solid_msg = (2, SOLID_ROWS, 128)
    end_msg = (2, END_ROWS, 128)
    fluid = (Q, CA, CZ, NR)
    solid = (SA, SZ, NR)
    fluid_ext = (Q, CA, 2, ROWS, 128)
    solid_ext = (SA + 6, 2, ROWS, 128)
    opened_ext = (3, CA, 2, ROWS, 128)
    post, air, near_z, far_z, token = call(
        first_kernel,
        2,
        [(Q, CA, 2, CZ, 128), (CA, 2, CZ, 128), axial_msg, axial_msg, (8, 128)],
        [
            VMEM(fluid, f32),
            VMEM((CA, CZ, NR), jnp.int32),
            VMEM(axial_msg, f32),
            VMEM(axial_msg, f32),
            pltpu.SemaphoreType.DMA((CA + 1,)),
        ],
        moved=8 << 20,
        far_ins=2,
        held=(0, 1, 2, 3),
    )(populations, fluid_flags)
    near_z = swap(near_z, "axial", False)
    far_z = swap(far_z, "axial", True)
    near_s, far_s, packed = call(
        solid_azim_kernel,
        4,
        [solid_msg, solid_msg, (8, 128)],
        [
            VMEM((2, 3, SZ, NR), f32),
            VMEM((2, 3, SZ, NR), jnp.int32),
            pltpu.SemaphoreType.DMA((4,)),
        ],
        moved=2 << 20,
        far_ins=2,
    )(solid_temp, materials, cells, token)
    near_s = swap(near_s, "azim", False)
    far_s = swap(far_s, "azim", True)
    near_z, far_z, near_s, far_s = lax.optimization_barrier(
        (near_z, far_z, near_s, far_s)
    )
    ext, opened, near_a, far_a = call(
        functools.partial(rim_kernel, n_axial),
        5,
        [fluid_ext, opened_ext, azim_msg, azim_msg],
        [VMEM(azim_msg, f32), VMEM(azim_msg, f32)],
        moved=8 << 20,
        held=(0, 1),
    )(post, air, near_z, far_z, packed)
    near_a = swap(near_a, "azim", False)
    far_a = swap(far_a, "azim", True)
    rows = wall_cell.shape[0]
    ext, opened = (pltpu.with_memory_space_constraint(x, VMEM) for x in (ext, opened))
    fluid_out, second, speeds, token = call(
        inner_kernel,
        2,
        [fluid, (Q, CA + 2, 2, ROWS, 128), (CA * CZ, NR), (8, 128)],
        [VMEM((Q, CA - 4, CZ, NR), f32), pltpu.SemaphoreType.DMA((CA - 4,))],
        moved=12 << 20,
        far_outs=1,
        held=(1, 2),
    )(ext, opened)
    near_e, far_e = call(
        solid_axial_kernel,
        6,
        [end_msg, end_msg],
        [
            VMEM(solid, f32),
            VMEM(solid, jnp.int32),
            VMEM(end_msg, f32),
            VMEM(end_msg, f32),
            pltpu.SemaphoreType.DMA((2,)),
        ],
        moved=2 << 20,
        far_ins=2,
    )(solid_temp, materials, cells, near_s, far_s, token)
    near_e = swap(near_e, "axial", False)
    far_e = swap(far_e, "axial", True)
    fluid_out, _, message = call(
        functools.partial(outer_kernel, n_azim, n_axial),
        11,
        [fluid, (Q, CA + 2, 2, ROWS, 128), (devices, 1, 128)],
        [
            VMEM((3, CA + 2, 2, ROWS, 128), f32),
            VMEM((2, 13, 2, ROWS, 128), f32),
            VMEM((CA * CZ, NR), f32),
            VMEM((Q, 4, CZ, NR), f32),
            pltpu.SemaphoreType.DMA((4,)),
        ],
        moved=8 << 20,
        far_ins=1,
        far_outs=1,
        held=(1,),
        aliases={0: 0, 1: 1},
    )(
        fluid_out,
        pltpu.with_memory_space_constraint(second, VMEM),
        pltpu.with_memory_space_constraint(speeds, VMEM),
        ext,
        opened,
        near_a,
        far_a,
        wall_cell.reshape(1, rows),
        wall_drive.reshape(1, rows),
        wall_owner.reshape(1, rows),
        wall_slot.reshape(1, rows),
    )
    arrived = lax.all_to_all(
        message, ("azim", "axial"), split_axis=0, concat_axis=0, tiled=True
    )
    link_shape = (3, SA + 4, 2, 24, 128)
    swept, links, all_cells = call(
        functools.partial(solid_kernel, n_axial),
        7,
        [solid, link_shape, (9, CAP, devices)],
        [VMEM(solid_ext, f32)] * 7
        + [
            VMEM(solid, f32),
            VMEM(solid, jnp.int32),
            pltpu.SemaphoreType.DMA((2,)),
        ],
        moved=8 << 20,
        far_ins=2,
    )(solid_temp, materials, near_s, far_s, near_e, far_e, cells)
    (solid_out,) = call(
        deposit_kernel,
        4,
        [solid],
        [
            VMEM(link_shape[1:], f32),
            VMEM(link_shape[1:], f32),
            VMEM((devices, 128), f32),
            VMEM(solid, f32),
            VMEM(link_shape, f32),
            pltpu.SemaphoreType.DMA((5,)),
        ],
        moved=8 << 20,
        far_ins=2,
    )(swept, links, arrived, all_cells)
    return fluid_out, solid_out


def solution(mesh):
    both = ("azim", "axial")
    in_specs = (
        P(None, "azim", "axial", None),
        P("azim", "axial", None),
        P(both),
        P(both),
        P(both),
        P(both),
        P(both),
        P("azim", "axial", None),
        P("azim", "axial", None),
    )
    out_specs = (P(None, "azim", "axial", None), P("azim", "axial", None))
    return jax.shard_map(
        functools.partial(per_device, mesh.shape["azim"], mesh.shape["axial"]),
        mesh=mesh,
        in_specs=in_specs,
        out_specs=out_specs,
        check_vma=False,
    )
```

```python
import functools

import jax
import jax.numpy as jnp
from jax import lax
from jax.experimental import pallas as pl
from jax.experimental.pallas import tpu as pltpu
from jax.sharding import PartitionSpec as P

CAP = 8
STEP_A = [0, 1, -1, 0, 0, 0, 0, 1, -1, 1, -1, 1, -1, 1, -1, 0, 0, 0, 0]
STEP_Z = [0, 0, 0, 1, -1, 0, 0, 1, -1, -1, 1, 0, 0, 0, 0, 1, -1, 1, -1]
STEP_R = [0, 0, 0, 0, 0, 1, -1, 0, 0, 0, 0, 1, -1, -1, 1, 1, -1, -1, 1]
OPPOSITE = [0, 2, 1, 4, 3, 6, 5, 8, 7, 10, 9, 12, 11, 14, 13, 16, 15, 18, 17]
AZIM_UP = [i for i in range(19) if STEP_A[i] == 1]
AZIM_DOWN = [i for i in range(19) if STEP_A[i] == -1]
AXIAL_UP = [i for i in range(19) if STEP_Z[i] == 1]
AXIAL_DOWN = [i for i in range(19) if STEP_Z[i] == -1]
RELAXATION = 1.25
SPEED_REF = 0.05
HEAT_CAPACITY = 6.5

Q = 19
CA, CZ, NR = 8, 16, 256
SA, SZ = 16, 16
HALVES = (0, 1)
ROWS = 32

PER_PLACE = 26
AXIAL_ROWS = CA * PER_PLACE
STREAMED_ROW = 100
SUMS_ROW = 190
FLAG_ROW = 244
AZIM_ROWS = 264
SOLID_COND = 48
SOLID_CELLS = 96
SOLID_ROWS = 104
SKIP = (0, 20, 38)
END_COND = 54
END_CELLS = 112
END_ROWS = 128

GROUP = 5

VMEM = pltpu.VMEM
f32 = jnp.float32
bf16 = jnp.bfloat16


def lanes(half):
    return pl.ds(128 * half, 128)


def moments(f):
    rho = f[0]
    for i in range(1, Q):
        rho = rho + f[i]
    d = [f[i] - f[i + 1] for i in range(1, Q, 2)]
    mom_a = d[0] + d[3] + d[4] + d[5] + d[6]
    mom_z = d[1] + d[3] - d[4] + d[7] + d[8]
    mom_r = d[2] + d[5] - d[6] + d[7] - d[8]
    return rho, mom_a, mom_z, mom_r


def collide_part(sums, f, flag, which):
    rho, mom_a, mom_z, mom_r = sums
    open_cell = flag > 0
    inv = 1.0 / jnp.where(open_cell, rho, 1.0)
    omega = jnp.where(open_cell, RELAXATION, 0.0)
    keep = 1.0 - omega
    ua, uz, ur = mom_a * inv, mom_z * inv, mom_r * inv
    base = 1.0 - 1.5 * (ua * ua + uz * uz + ur * ur)
    scale = omega * rho
    face, edge = scale * (1.0 / 18.0), scale * (1.0 / 36.0)
    post = {}
    if 0 in which:
        post[0] = keep * f[0] + scale * (1.0 / 3.0) * base
    for n, proj in enumerate(
        (ua, uz, ur, ua + uz, ua - uz, ua + ur, ua - ur, uz + ur, uz - ur)
    ):
        weight = face if n < 3 else edge
        one, two = 2 * n + 1, 2 * n + 2
        if one in which or two in which:
            even = weight * (base + 4.5 * proj * proj)
            odd = weight * (3.0 * proj)
        if one in which:
            post[one] = keep * f[one] + (even + odd)
        if two in which:
            post[two] = keep * f[two] + (even - odd)
    return post


def collide(f, flag):
    return collide_part(moments(f), f, flag, range(Q))


def conductivity(material):
    return jnp.where(
        material == 0,
        1.0,
        jnp.where(material == 1, 0.55, jnp.where(material == 2, 0.2, 0.8)),
    ).astype(f32)


def by_parity(axis, body, near, far):
    odd = lax.rem(lax.axis_index(axis), 2) == 1

    @pl.when(odd)
    def _():
        body(near, far)

    @pl.when(jnp.logical_not(odd))
    def _():
        body(far, near)


def first_kernel(
    f_far, flags_far, post, air, near, far, token, f, flags, low, high, come
):
    flags_copy = pltpu.make_async_copy(flags_far, flags, come.at[CA])

    def layer_copy(a):
        return pltpu.make_async_copy(f_far.at[:, a], f.at[:, a], come.at[a])

    flags_copy.start()
    for a in range(CA):
        layer_copy(a).start()
    token[...] = jnp.zeros((8, 128), f32)
    flags_copy.wait()

    def layer(a, carry):
        layer_copy(a).wait()
        for half in HALVES:
            for part in (0, 1):
                rows = pl.ds(8 * part, 8)
                flag = flags[a, rows, lanes(half)].astype(f32)
                out = collide([f[i, a, rows, lanes(half)] for i in range(Q)], flag)
                for i in range(Q):
                    post[i, a, half, rows, :] = out[i]
                air[a, half, rows, :] = flag
                place = a * PER_PLACE
                target, inner, edge, near_edge = (
                    (low, AXIAL_DOWN, 0, 1) if part == 0 else (high, AXIAL_UP, 7, 6)
                )

                def put(row, value, at):
                    target[half, pl.ds(place + row, 1), :] = value[at : at + 1]

                for i in range(Q):
                    put(i, out[i], edge)
                for n, i in enumerate(inner):
                    put(Q + n, out[i], near_edge)
                put(24, flag, edge)
                put(25, flag, near_edge)
        return carry

    lax.fori_loop(0, CA, layer, 0)

    def hand_over(down, up):
        down[...] = low[...]
        up[...] = high[...]

    by_parity("axial", hand_over, near, far)


def solid_azim_kernel(
    temp_far, mat_far, cells, token, near, far, packed, temp, mat, come
):
    packed[...] = jnp.zeros((8, 128), f32)
    copies = []
    for n, layers in enumerate((pl.ds(0, 3), pl.ds(SA - 3, 3))):
        for k, (source, target) in enumerate(((temp_far, temp), (mat_far, mat))):
            copy = pltpu.make_async_copy(
                source.at[layers], target.at[n], come.at[2 * n + k]
            )
            copy.start()
            copies.append(copy)
    for copy in copies:
        copy.wait()

    def fill(down, up):
        for side, target in enumerate((down, up)):
            for half in HALVES:
                for n in range(3):
                    a = n if side == 0 else 2 - n
                    target[half, pl.ds(16 * n, 16), :] = temp[side, a, :, lanes(half)]
                    target[half, pl.ds(SOLID_COND + 16 * n, 16), :] = conductivity(
                        mat[side, a, :, lanes(half)]
                    )
            target[0, pl.ds(SOLID_CELLS, 8), :] = cells[...].astype(f32)

    by_parity("azim", fill, near, far)


def solid_axial_kernel(
    temp_far,
    mat_far,
    cells,
    near_s,
    far_s,
    token,
    near,
    far,
    temp,
    mat,
    low,
    high,
    come,
):
    copies = [
        pltpu.make_async_copy(source, target, come.at[n])
        for n, (source, target) in enumerate(((temp_far, temp), (mat_far, mat)))
    ]
    for copy in copies:
        copy.start()

    def azim_ends(lower, upper):
        for target, edge, step in ((low, 0, 1), (high, SZ - 1, -1)):
            for half in HALVES:
                for depth in range(2):
                    z = edge + step * depth
                    for n in range(2 - depth):
                        for source, at in (
                            (lower, 1 - depth - n),
                            (upper, 18 - depth + n),
                        ):
                            for kind, here in ((0, 0), (END_COND, SOLID_COND)):
                                target[half, pl.ds(kind + SKIP[depth] + at, 1), :] = (
                                    source[half, pl.ds(here + 16 * n + z, 1), :]
                                )
            target[0, pl.ds(END_CELLS, 8), :] = cells[...].astype(f32)
            target[1, pl.ds(END_CELLS, 8), :] = lower[0, pl.ds(SOLID_CELLS, 8), :]
            target[0, pl.ds(END_CELLS + 8, 8), :] = upper[0, pl.ds(SOLID_CELLS, 8), :]

    by_parity("azim", azim_ends, near_s, far_s)
    for copy in copies:
        copy.wait()

    def layer(a, carry):
        for half in HALVES:
            for part, target in ((0, low), (1, high)):
                rows = pl.ds(8 * part, 8)
                t = temp[a, rows, lanes(half)]
                c = conductivity(mat[a, rows, lanes(half)])
                for depth in range(3):
                    at = depth if part == 0 else 7 - depth
                    row = SKIP[depth] + 2 - depth + a
                    target[half, pl.ds(row, 1), :] = t[at : at + 1]
                    target[half, pl.ds(END_COND + row, 1), :] = c[at : at + 1]
        return carry

    lax.fori_loop(0, SA, layer, 0, unroll=4)

    def hand_over(down, up):
        down[...] = low[...]
        up[...] = high[...]

    by_parity("axial", hand_over, near, far)


def ends(n_axial):
    z = lax.axis_index("axial")
    return (
        jnp.where(z > 0, 1.0, 0.0).astype(f32),
        jnp.where(z < n_axial - 1, 1.0, 0.0).astype(f32),
    )


def shifted(pair, step, lane):
    if step == 0:
        return pair
    turn = 1 if step == 1 else 127
    at = 0 if step == 1 else 127
    a, b = (pltpu.roll(x, turn, 1) for x in pair)
    return [jnp.where(lane == at, b, a), jnp.where(lane == at, a, b)]


def split(x):
    one = x.astype(bf16)
    return one, (x - one.astype(f32)).astype(bf16)


def stream(
    source,
    opened,
    at_a,
    flag_a,
    row,
    lane,
    which=None,
    sides=None,
    rim=None,
    beyond=False,
):
    rows = pl.ds(row, 8)
    out = [[], []]
    for i in range(Q) if which is None else which:
        own = OPPOSITE[i]
        from_rows = pl.ds(row - STEP_Z[i], 8)

        def before(half):
            if rim and i in rim:
                return sides[rim[i][0], rim[i][1], half, from_rows, :]
            if beyond:
                return source[i, at_a, half, from_rows, :]
            return source[i, at_a - STEP_A[i], half, from_rows, :]

        def back(half):
            if beyond:
                return sides[rim[own][0], rim[own][1], half, rows, :]
            return source[own, at_a, half, rows, :]

        moved = shifted([before(half) for half in HALVES], STEP_R[i], lane)
        for half in HALVES:
            if i == 0:
                out[half].append(moved[half])
                continue
            from_a = flag_a if beyond else flag_a - STEP_A[i]
            mask = opened[STEP_R[i] % 3, from_a, half, from_rows, :]
            out[half].append(jnp.where(mask > 0, moved[half], back(half)))
    return out


def rim_kernel(
    n_axial,
    post,
    air,
    near_z,
    far_z,
    packed,
    ext,
    opened,
    near,
    far,
    low,
    high,
):
    lane = lax.broadcasted_iota(jnp.int32, (8, 128), 1)
    below, above = ends(n_axial)

    def own_layer(a, carry):
        to = pl.ds(8, 16)
        for half in HALVES:
            for i in range(Q):
                ext[i, a, half, to, :] = post[i, a, half]
            opened[0, a, half, to, :] = air[a, half]
        return carry

    lax.fori_loop(0, CA, own_layer, 0)

    def axial_rim(lower, upper):
        def layer(a, carry):
            place = a * PER_PLACE
            for half in HALVES:
                for source, first, last, moving, there in (
                    (lower, 7, 6, AXIAL_UP, below),
                    (upper, 24, 25, AXIAL_DOWN, above),
                ):

                    def get(row):
                        return source[half, pl.ds(place + row, 1), :]

                    for i in range(Q):
                        ext[i, a, half, pl.ds(first, 1), :] = get(i)
                    for n, i in enumerate(moving):
                        ext[i, a, half, pl.ds(last, 1), :] = get(Q + n)
                    opened[0, a, half, pl.ds(first, 1), :] = get(24) * there
                    opened[0, a, half, pl.ds(last, 1), :] = get(25) * there
            return carry

        lax.fori_loop(0, CA, layer, 0, unroll=2)
    by_parity("axial", axial_rim, near_z, far_z)

    def turn(a, carry):
        turn_flags(opened, a, lane)
        return carry

    lax.fori_loop(0, CA, turn, 0, unroll=2)

    for target, layer, moving, step in (
        (low, 0, AZIM_DOWN, -1),
        (high, CA - 1, AZIM_UP, 1),
    ):
        for half in HALVES:
            for n, i in enumerate(moving):
                target[half, pl.ds(20 * n, 20), :] = ext[
                    i, layer, half, pl.ds(6, 20), :
                ]
            target[half, pl.ds(FLAG_ROW, 20), :] = opened[
                0, layer, half, pl.ds(6, 20), :
            ]
        which = [i for i in range(Q) if STEP_A[i] in (0, step)]
        for row in (7, 15, 17):
            moved = stream(ext, opened, layer, layer, row, lane, which)
            for half in HALVES:
                new = dict(zip(which, moved[half]))
                at = row - 7
                for n, i in enumerate(moving):
                    target[half, pl.ds(STREAMED_ROW + 18 * n + at, 8), :] = new[i]
                still = [i for i in which if STEP_A[i] == 0]
                for n, table in enumerate(([1] * Q, STEP_Z, STEP_R)):
                    total = None
                    for i in still:
                        if table[i]:
                            term = new[i] * table[i]
                            total = term if total is None else total + term
                    target[half, pl.ds(SUMS_ROW + 18 * n + at, 8), :] = total

    def hand_over(down, up):
        down[...] = low[...]
        up[...] = high[...]

    by_parity("azim", hand_over, near, far)


def turn_flags(opened, a, lane):
    for part in range(4):
        rows = pl.ds(8 * part, 8)
        pair = [opened[0, a, half, rows, :] for half in HALVES]
        up = shifted(pair, 1, lane)
        down = shifted(pair, -1, lane)
        opened[1, a, 0, rows, :] = jnp.where(lane == 0, 0.0, up[0])
        opened[1, a, 1, rows, :] = up[1]
        opened[2, a, 0, rows, :] = down[0]
        opened[2, a, 1, rows, :] = jnp.where(lane == 127, 0.0, down[1])


def step_two(second, opened, a, flag_a, lane, speeds, target, at):
    for part in (0, 1):
        moved = stream(second, opened, a + 1, flag_a, 8 + 8 * part, lane)
        for half in HALVES:
            for i in range(Q):
                target[i, at, pl.ds(8 * part, 8), lanes(half)] = moved[half][i]
            rho, mom_a, mom_z, mom_r = moments(moved[half])
            inv = 1.0 / rho
            ua, uz, ur = mom_a * inv, mom_z * inv, mom_r * inv
            speeds[pl.ds(a * CZ + 8 * part, 8), lanes(half)] = jnp.sqrt(
                ua * ua + uz * uz + ur * ur + 1e-06
            )


def inner_kernel(
    ext, opened, fluid_far, second, speeds, token, fluid_out, layers_out
):
    token[...] = jnp.zeros((8, 128), f32)
    lane = lax.broadcasted_iota(jnp.int32, (8, 128), 1)

    def first_step(a, carry):
        for row in (7, 15, 17):
            moved = stream(ext, opened, a, a, row, lane)
            for half in HALVES:
                out = collide(moved[half], opened[0, a, half, pl.ds(row, 8), :])
                for i in range(Q):
                    second[i, a + 1, half, pl.ds(row, 8), :] = out[i]
        return carry

    lax.fori_loop(1, CA - 1, first_step, 0)

    def layer_copy(n):
        return pltpu.make_async_copy(
            fluid_out.at[:, n], fluid_far.at[:, n + 2], layers_out.at[n]
        )

    def second_step(n, carry):
        step_two(second, opened, n + 2, n + 2, lane, speeds, fluid_out, n)
        layer_copy(n).start()
        return carry

    lax.fori_loop(0, CA - 4, second_step, 0)
    for n in range(CA - 4):
        layer_copy(n).wait()


def outer_kernel(
    n_azim,
    n_axial,
    fluid_so_far,
    second_so_far,
    inner_speeds,
    ext,
    own_opened,
    near_a,
    far_a,
    cell,
    drive,
    owner,
    slot,
    fluid_far,
    second,
    message,
    opened,
    sides,
    speeds,
    fluid_out,
    layers_out,
):
    lane = lax.broadcasted_iota(jnp.int32, (8, 128), 1)
    inside = pl.ds(2 * CZ, (CA - 4) * CZ)
    speeds[inside, :] = inner_speeds[inside, :]

    def own_flags(a, carry):
        for k in range(3):
            for half in HALVES:
                opened[k, a + 1, half] = own_opened[k, a, half]
        return carry

    lax.fori_loop(0, CA, own_flags, 0, unroll=2)

    def azim_rim(lower, upper):
        for side, (source, a) in enumerate(((lower, 0), (upper, CA + 1))):
            for half in HALVES:
                for n in range(5):
                    sides[side, n, half, pl.ds(6, 20), :] = source[
                        half, pl.ds(20 * n, 20), :
                    ]
                for n in range(8):
                    sides[side, 5 + n, half, pl.ds(7, 18), :] = source[
                        half, pl.ds(STREAMED_ROW + 18 * n, 18), :
                    ]
                opened[0, a, half, pl.ds(6, 20), :] = source[
                    half, pl.ds(FLAG_ROW, 20), :
                ]

    by_parity("azim", azim_rim, near_a, far_a)
    turn_flags(opened, 0, lane)
    turn_flags(opened, CA + 1, lane)

    def finish(a, row, moved):
        for half in HALVES:
            out = collide(moved[half], opened[0, a + 1, half, pl.ds(row, 8), :])
            for i in range(Q):
                second[i, a + 1, half, pl.ds(row, 8), :] = out[i]

    def layer_copy(n, a):
        return pltpu.make_async_copy(
            fluid_out.at[:, n], fluid_far.at[:, a], layers_out.at[n]
        )

    for side, (a, inward, outward) in enumerate(
        ((0, AZIM_UP, AZIM_DOWN), (CA - 1, AZIM_DOWN, AZIM_UP))
    ):
        rim = {i: (side, n) for n, i in enumerate(inward)}
        beyond = 0 if side == 0 else CA + 1

        def edge_step(n, carry):
            row = 7 + 8 * n
            finish(a, row, stream(ext, opened, a, a + 1, row, lane, None, sides, rim))
            far_in = stream(
                ext, opened, a, a + 1, row, lane, outward, sides, rim, beyond=True
            )
            for half in HALVES:
                rows = pl.ds(row, 8)

                def at(n):
                    return sides[side, n, half, rows, :]

                new = {i: at(5 + n) for n, i in enumerate(inward)}
                new.update(zip(outward, far_in[half]))
                sums = [at(10), None, at(11), at(12)]
                for k, table in enumerate(([1] * Q, STEP_A, STEP_Z, STEP_R)):
                    for i in inward + outward:
                        if table[i]:
                            term = new[i] * table[i]
                            sums[k] = term if sums[k] is None else sums[k] + term
                out = collide_part(
                    sums, new, opened[0, beyond, half, rows, :], inward
                )
                for i in inward:
                    second[i, beyond, half, rows, :] = out[i]
            return carry

        lax.fori_loop(0, 3, edge_step, 0)

        def second_step(n, carry):
            layer = n + side * (CA - 2)
            at = n + 2 * side
            step_two(second, opened, layer, layer + 1, lane, speeds, fluid_out, at)
            layer_copy(at, layer).start()
            return carry

        lax.fori_loop(0, 2, second_step, 0)


    rows_here = cell.shape[1]
    place = cell[...]
    row_hot = (
        lax.broadcasted_iota(jnp.int32, (CA * CZ, rows_here), 0) == place // NR
    ).astype(f32).astype(bf16)
    turned = jnp.transpose(speeds[...])
    picked = jnp.zeros((NR, rows_here), f32)
    for term in split(turned):
        picked = picked + jnp.dot(term, row_hot, preferred_element_type=f32)
    column = lax.broadcasted_iota(jnp.int32, (NR, rows_here), 0) == place % NR
    speed = jnp.sum(jnp.where(column, picked, 0.0), axis=0, keepdims=True)
    flux = drive[...] * (0.2 + speed / SPEED_REF)
    devices = n_azim * n_axial
    owner_hot = (
        lax.broadcasted_iota(jnp.int32, (devices, rows_here), 0) == owner[...]
    ).astype(f32).astype(bf16)
    slotted = jnp.where(
        lax.broadcasted_iota(jnp.int32, (128, rows_here), 0) == slot[...], flux, 0.0
    )
    sent = jnp.zeros((devices, 128), f32)
    for term in split(slotted):
        sent = sent + lax.dot_general(
            owner_hot, term, (((1,), (1,)), ((), ())), preferred_element_type=f32
        )
    total = jnp.zeros((devices, 128), f32)
    for da in (-1, 0, 1):
        for dz in (-1, 0, 1):
            which = (da + 1) * 3 + dz + 1
            back = (-(da * n_axial + dz)) % devices
            moved = pltpu.roll(sent, back, 0) if back else sent
            total = total + (pltpu.roll(moved, CAP * which, 1) if which else moved)
    for o in range(devices):
        message[o, :, :] = total[o : o + 1]
    for n, a in enumerate((0, 1, CA - 2, CA - 1)):
        layer_copy(n, a).wait()


def link(first, second):
    joined = first + second
    good = joined > 0
    return jnp.where(
        good,
        (2.0 / HEAT_CAPACITY) * first * second / jnp.where(good, joined, 1.0),
        0.0,
    )


def sweep(source, link_a, link_z, link_r, keep, a, row, lane):
    rows = pl.ds(row, 8)
    pair = [source[a, half, rows, :] for half in HALVES]
    lr = [link_r[a, half, rows, :] for half in HALVES]
    up = shifted(pair, -1, lane)
    down = shifted([x * y for x, y in zip(pair, lr)], 1, lane)
    out = []
    for half in HALVES:
        total = keep[a, half, rows, :] * pair[half]
        total = total + link_a[a, half, rows, :] * source[a + 1, half, rows, :]
        total = total + link_a[a - 1, half, rows, :] * source[a - 1, half, rows, :]
        total = (
            total + link_z[a, half, rows, :] * source[a, half, pl.ds(row + 1, 8), :]
        )
        total = (
            total
            + link_z[a, half, pl.ds(row - 1, 8), :]
            * source[a, half, pl.ds(row - 1, 8), :]
        )
        out.append(total + lr[half] * up[half] + down[half])
    return out


def solid_kernel(
    n_axial,
    temp_far,
    mat_far,
    near_s,
    far_s,
    near_e,
    far_e,
    cells,
    swept,
    links_out,
    all_cells,
    link_a,
    link_z,
    link_r,
    keep,
    ext,
    cond,
    other,
    temp,
    mat,
    come,
):
    copies = [
        pltpu.make_async_copy(source, target, come.at[n])
        for n, (source, target) in enumerate(((temp_far, temp), (mat_far, mat)))
    ]
    for copy in copies:
        copy.start()
    for copy in copies:
        copy.wait()
    lane = lax.broadcasted_iota(jnp.int32, (8, 128), 1)

    def own_layer(a, carry):
        for half in HALVES:
            for part in (0, 1):
                rows = pl.ds(8 * part, 8)
                to = pl.ds(8 + 8 * part, 8)
                ext[a + 3, half, to, :] = temp[a, rows, lanes(half)]
                cond[a + 3, half, to, :] = conductivity(mat[a, rows, lanes(half)])
        return carry

    lax.fori_loop(0, SA, own_layer, 0, unroll=4)

    def azim_rim(lower, upper):
        for half in HALVES:
            for n in range(3):
                for source, a in ((lower, 2 - n), (upper, 19 + n)):
                    ext[a, half, pl.ds(8, 16), :] = source[half, pl.ds(16 * n, 16), :]
                    cond[a, half, pl.ds(8, 16), :] = source[
                        half, pl.ds(SOLID_COND + 16 * n, 16), :
                    ]
        all_cells[1] = lower[0, pl.ds(SOLID_CELLS, 8), :]
        all_cells[7] = upper[0, pl.ds(SOLID_CELLS, 8), :]

    by_parity("azim", azim_rim, near_s, far_s)
    below, above = ends(n_axial)

    def axial_rim(lower, upper):
        for half in HALVES:
            for depth in range(3):
                for n in range(20 - 2 * depth):
                    a = 1 + depth + n
                    at = SKIP[depth] + n
                    for source, row, there in (
                        (lower, 7 - depth, below),
                        (upper, 24 + depth, above),
                    ):
                        ext[a, half, pl.ds(row, 1), :] = source[half, pl.ds(at, 1), :]
                        cond[a, half, pl.ds(row, 1), :] = (
                            source[half, pl.ds(END_COND + at, 1), :] * there
                        )
        outside = jnp.full((CAP, 128), SA * SZ * NR, f32)
        for source, dz, there in ((lower, 0, below), (upper, 2, above)):
            for which, half, row in ((0, 1, 0), (3, 0, 0), (6, 0, 8)):
                all_cells[which + dz] = jnp.where(
                    there > 0, source[half, pl.ds(END_CELLS + row, 8), :], outside
                )

    by_parity("axial", axial_rim, near_e, far_e)
    all_cells[4] = cells[...].astype(f32)

    def links(a, carry):
        for row in (5, 13, 21):
            rows = pl.ds(row, 8)
            pair = [cond[a, half, rows, :] for half in HALVES]
            up = shifted(pair, -1, lane)
            up = [up[0], jnp.where(lane == 127, 0.0, up[1])]
            for half in HALVES:
                link_a[a, half, rows, :] = link(pair[half], cond[a + 1, half, rows, :])
                link_z[a, half, rows, :] = link(
                    pair[half], cond[a, half, pl.ds(row + 1, 8), :]
                )
                link_r[a, half, rows, :] = link(pair[half], up[half])
        return carry

    lax.fori_loop(0, SA + 5, links, 0, unroll=3)

    def keeps(a, carry):
        for row in (6, 14, 22):
            rows = pl.ds(row, 8)
            pair = [link_r[a, half, rows, :] for half in HALVES]
            down = shifted(pair, 1, lane)
            for half in HALVES:
                keep[a, half, rows, :] = 1.0 - (
                    link_a[a, half, rows, :]
                    + link_a[a - 1, half, rows, :]
                    + link_z[a, half, rows, :]
                    + link_z[a, half, pl.ds(row - 1, 8), :]
                    + pair[half]
                    + down[half]
                )
        return carry

    lax.fori_loop(1, SA + 5, keeps, 0, unroll=4)

    def trim(a, carry):
        for half in HALVES:
            for n, kind in enumerate((link_a, link_z, link_r)):
                links_out[n, a, half] = kind[a + 1, half, pl.ds(6, 24), :]
        return carry

    lax.fori_loop(0, SA + 4, trim, 0, unroll=2)

    def once(source, target, first, last, at):
        def layer(a, carry):
            for row in at:
                out = sweep(source, link_a, link_z, link_r, keep, a, row, lane)
                for half in HALVES:
                    target[a, half, pl.ds(row, 8), :] = out[half]
            return carry

        lax.fori_loop(first, last, layer, 0, unroll=2)

    once(ext, other, 1, SA + 5, (6, 14, 22))
    once(other, ext, 2, SA + 4, (7, 15, 23))

    def final(a, carry):
        for part in (0, 1):
            out = sweep(ext, link_a, link_z, link_r, keep, a + 3, 8 + 8 * part, lane)
            for half in HALVES:
                swept[a, pl.ds(8 * part, 8), lanes(half)] = out[half]
        return carry

    lax.fori_loop(0, SA, final, 0, unroll=4)


def deposit_kernel(
    swept_far,
    links_far,
    arrived,
    all_cells,
    solid_far,
    heat,
    other,
    came,
    swept,
    links,
    solid_out,
    brought,
    taken,
):
    groups = [
        pltpu.make_async_copy(
            links_far.at[:, pl.ds(GROUP * n, GROUP)],
            links.at[:, pl.ds(GROUP * n, GROUP)],
            brought.at[n],
        )
        for n in range((SA + 4) // GROUP)
    ]
    swept_copy = pltpu.make_async_copy(swept_far, swept, brought.at[len(groups)])
    for copy in groups:
        copy.start()
    swept_copy.start()
    lane = lax.broadcasted_iota(jnp.int32, (8, 128), 1)
    senders = arrived.shape[0]
    for s in range(senders):
        came[pl.ds(s, 1), :] = arrived[s]

    def clear(a, carry):
        for half in HALVES:
            heat[a, half] = jnp.zeros((24, 128), f32)
        return carry

    lax.fori_loop(0, SA + 4, clear, 0, unroll=2)
    values = jnp.transpose(came[...]) * (1.0 / HEAT_CAPACITY)

    def place(which, rows, row_of):
        cell = all_cells[which].astype(jnp.int32)
        value = values[CAP * which : CAP * (which + 1)]
        one, two = split(value)
        at_row = row_of(lax.broadcasted_iota(jnp.int32, (rows, senders), 0))
        at_col = lax.broadcasted_iota(jnp.int32, (NR, senders), 0)
        left, right = [[], []], []
        for c in range(CAP):
            hit = at_row == (cell[c : c + 1] // NR)
            for to, term in zip(left, (one, two)):
                to.append(
                    jnp.where(hit, term[c : c + 1].astype(f32), 0.0).astype(bf16)
                )
            right.append((at_col == cell[c : c + 1] % NR).astype(f32).astype(bf16))
        both = lax.dot_general(
            jnp.concatenate([jnp.concatenate(to, axis=1) for to in left], axis=0),
            jnp.concatenate(right, axis=1),
            (((1,), (1,)), ((), ())),
            preferred_element_type=f32,
        )
        return both[:rows] + both[rows:]

    own = place(4, SA * SZ, lambda j: j)
    for a in range(SA):
        for half in HALVES:
            heat[a + 2, half, pl.ds(2, 16), :] = own[
                16 * a : 16 * a + 16, 128 * half : 128 * half + 128
            ]
    low = place(1, 32, lambda j: j + 14 * SZ)
    high = place(7, 32, lambda j: j)
    for n in range(2):
        for half in HALVES:
            cut = slice(128 * half, 128 * half + 128)
            heat[n, half, pl.ds(2, 16), :] = low[16 * n : 16 * n + 16, cut]
            heat[18 + n, half, pl.ds(2, 16), :] = high[16 * n : 16 * n + 16, cut]
    low = place(3, 32, lambda j: (j // 2) * SZ + 14 + j % 2)
    high = place(5, 32, lambda j: (j // 2) * SZ + j % 2)
    for a in range(SA):
        for half in HALVES:
            cut = slice(128 * half, 128 * half + 128)
            heat[a + 2, half, pl.ds(0, 2), :] = low[2 * a : 2 * a + 2, cut]
            heat[a + 2, half, pl.ds(18, 2), :] = high[2 * a : 2 * a + 2, cut]
    for which, cell_row, a, row in (
        (0, 255, 1, 1),
        (2, 240, 1, 18),
        (6, 15, 18, 1),
        (8, 0, 18, 18),
    ):
        one = place(which, 8, lambda j: jnp.where(j == 0, cell_row, -1))
        for half in HALVES:
            heat[a, half, pl.ds(row, 1), :] = one[0:1, 128 * half : 128 * half + 128]

    def spread(source, a, row):
        rows, before, after = (pl.ds(row + n, 8) for n in (0, -1, 1))
        pair = [source[a, half, rows, :] for half in HALVES]
        up = shifted(pair, -1, lane)
        flow = [links[2, a, half, rows, :] * (up[half] - pair[half]) for half in HALVES]
        back = shifted(flow, 1, lane)
        out = []
        for half in HALVES:
            here = pair[half]
            out.append(
                here
                + links[0, a, half, rows, :] * (source[a + 1, half, rows, :] - here)
                + links[0, a - 1, half, rows, :] * (source[a - 1, half, rows, :] - here)
                + links[1, a, half, rows, :] * (source[a, half, after, :] - here)
                + links[1, a, half, before, :] * (source[a, half, before, :] - here)
                + (flow[half] - back[half])
                + heat[a, half, rows, :]
            )
        return out

    def middle(a, carry):
        for row in (1, 9, 11):
            out = spread(heat, a, row)
            for half in HALVES:
                other[a, half, pl.ds(row, 8), :] = out[half]
        return carry

    for n, copy in enumerate(groups):
        copy.wait()
        first = max(GROUP * n, 1)
        last = min(GROUP * (n + 1), SA + 3)
        lax.fori_loop(first, last, middle, 0, unroll=last - first)
    swept_copy.wait()

    def final(a, carry):
        for part in (0, 1):
            rows = pl.ds(8 * part, 8)
            out = spread(other, a + 2, 2 + 8 * part)
            for half in HALVES:
                solid_out[a, rows, lanes(half)] = (
                    out[half] + swept[a, rows, lanes(half)]
                )
        return carry

    quarters = []
    for n in range(4):
        at = pl.ds(4 * n, 4)
        lax.fori_loop(4 * n, 4 * n + 4, final, 0, unroll=4)
        quarters.append(
            pltpu.make_async_copy(solid_out.at[at], solid_far.at[at], taken.at[n])
        )
        quarters[-1].start()
    for copy in quarters:
        copy.wait()


def call(
    kernel, ins, outs, scratch=(), limit=16, moved=0, far_ins=0, far_outs=0, held=(), aliases={}
):
    here, there = (pl.BlockSpec(memory_space=m) for m in (VMEM, pltpu.HBM))
    kernel_call = pl.pallas_call(
        kernel,
        out_shape=[
            VMEM(s, f32) if n in held else jax.ShapeDtypeStruct(s, f32)
            for n, s in enumerate(outs)
        ],
        in_specs=[there] * far_ins + [here] * (ins - far_ins),
        out_specs=[there] * far_outs + [here] * (len(outs) - far_outs),
        scratch_shapes=list(scratch),
        input_output_aliases=aliases,
        compiler_params=pltpu.CompilerParams(vmem_limit_bytes=limit * 1024 * 1024),
        cost_estimate=pl.CostEstimate(
            flops=0, bytes_accessed=moved, transcendentals=0
        ),
    )

    def run(*args):
        far = [pltpu.with_memory_space_constraint(x, pltpu.HBM) for x in args[:far_ins]]
        return kernel_call(*far, *args[far_ins:])

    return run


def swap(values, axis, far):
    count = lax.axis_size(axis)
    pairs = [(i, (((i + 1) ^ 1) - 1) % count if far else i ^ 1) for i in range(count)]
    if axis == "axial" and far:
        pairs[0], pairs[-1] = (0, 0), (count - 1, count - 1)
    return lax.ppermute(values, axis, pairs)


def per_device(
    n_azim,
    n_axial,
    populations,
    fluid_flags,
    wall_cell,
    wall_drive,
    wall_owner,
    wall_slot,
    receive_cell,
    materials,
    solid_temp,
):
    devices = n_azim * n_axial
    cells = receive_cell.reshape(devices, CAP).T
    azim_msg = (2, AZIM_ROWS, 128)
    axial_msg = (2, AXIAL_ROWS, 128)
    solid_msg = (2, SOLID_ROWS, 128)
    end_msg = (2, END_ROWS, 128)
    fluid = (Q, CA, CZ, NR)
    solid = (SA, SZ, NR)
    fluid_ext = (Q, CA, 2, ROWS, 128)
    solid_ext = (SA + 6, 2, ROWS, 128)
    opened_ext = (3, CA, 2, ROWS, 128)
    post, air, near_z, far_z, token = call(
        first_kernel,
        2,
        [(Q, CA, 2, CZ, 128), (CA, 2, CZ, 128), axial_msg, axial_msg, (8, 128)],
        [
            VMEM(fluid, f32),
            VMEM((CA, CZ, NR), jnp.int32),
            VMEM(axial_msg, f32),
            VMEM(axial_msg, f32),
            pltpu.SemaphoreType.DMA((CA + 1,)),
        ],
        moved=8 << 20,
        far_ins=2,
        held=(0, 1, 2, 3),
    )(populations, fluid_flags)
    near_z = swap(near_z, "axial", False)
    far_z = swap(far_z, "axial", True)
    near_s, far_s, packed = call(
        solid_azim_kernel,
        4,
        [solid_msg, solid_msg, (8, 128)],
        [
            VMEM((2, 3, SZ, NR), f32),
            VMEM((2, 3, SZ, NR), jnp.int32),
            pltpu.SemaphoreType.DMA((4,)),
        ],
        moved=2 << 20,
        far_ins=2,
    )(solid_temp, materials, cells, token)
    near_s = swap(near_s, "azim", False)
    far_s = swap(far_s, "azim", True)
    near_z, far_z, near_s, far_s = lax.optimization_barrier(
        (near_z, far_z, near_s, far_s)
    )
    ext, opened, near_a, far_a = call(
        functools.partial(rim_kernel, n_axial),
        5,
        [fluid_ext, opened_ext, azim_msg, azim_msg],
        [VMEM(azim_msg, f32), VMEM(azim_msg, f32)],
        moved=8 << 20,
        held=(0, 1),
    )(post, air, near_z, far_z, packed)
    near_a = swap(near_a, "azim", False)
    far_a = swap(far_a, "azim", True)
    rows = wall_cell.shape[0]
    ext, opened = (pltpu.with_memory_space_constraint(x, VMEM) for x in (ext, opened))
    fluid_out, second, speeds, token = call(
        inner_kernel,
        2,
        [fluid, (Q, CA + 2, 2, ROWS, 128), (CA * CZ, NR), (8, 128)],
        [VMEM((Q, CA - 4, CZ, NR), f32), pltpu.SemaphoreType.DMA((CA - 4,))],
        moved=12 << 20,
        far_outs=1,
        held=(1, 2),
    )(ext, opened)
    near_e, far_e = call(
        solid_axial_kernel,
        6,
        [end_msg, end_msg],
        [
            VMEM(solid, f32),
            VMEM(solid, jnp.int32),
            VMEM(end_msg, f32),
            VMEM(end_msg, f32),
            pltpu.SemaphoreType.DMA((2,)),
        ],
        moved=2 << 20,
        far_ins=2,
    )(solid_temp, materials, cells, near_s, far_s, token)
    near_e = swap(near_e, "axial", False)
    far_e = swap(far_e, "axial", True)
    fluid_out, _, message = call(
        functools.partial(outer_kernel, n_azim, n_axial),
        11,
        [fluid, (Q, CA + 2, 2, ROWS, 128), (devices, 1, 128)],
        [
            VMEM((3, CA + 2, 2, ROWS, 128), f32),
            VMEM((2, 13, 2, ROWS, 128), f32),
            VMEM((CA * CZ, NR), f32),
            VMEM((Q, 4, CZ, NR), f32),
            pltpu.SemaphoreType.DMA((4,)),
        ],
        moved=8 << 20,
        far_ins=1,
        far_outs=1,
        held=(1,),
        aliases={0: 0, 1: 1},
    )(
        fluid_out,
        pltpu.with_memory_space_constraint(second, VMEM),
        pltpu.with_memory_space_constraint(speeds, VMEM),
        ext,
        opened,
        near_a,
        far_a,
        wall_cell.reshape(1, rows),
        wall_drive.reshape(1, rows),
        wall_owner.reshape(1, rows),
        wall_slot.reshape(1, rows),
    )
    arrived = lax.all_to_all(
        message, ("azim", "axial"), split_axis=0, concat_axis=0, tiled=True
    )
    link_shape = (3, SA + 4, 2, 24, 128)
    swept, links, all_cells = call(
        functools.partial(solid_kernel, n_axial),
        7,
        [solid, link_shape, (9, CAP, devices)],
        [VMEM(solid_ext, f32)] * 7
        + [
            VMEM(solid, f32),
            VMEM(solid, jnp.int32),
            pltpu.SemaphoreType.DMA((2,)),
        ],
        moved=8 << 20,
        far_ins=2,
    )(solid_temp, materials, near_s, far_s, near_e, far_e, cells)
    (solid_out,) = call(
        deposit_kernel,
        4,
        [solid],
        [
            VMEM(link_shape[1:], f32),
            VMEM(link_shape[1:], f32),
            VMEM((devices, 128), f32),
            VMEM(solid, f32),
            VMEM(link_shape, f32),
            VMEM(solid, f32),
            pltpu.SemaphoreType.DMA((5,)),
            pltpu.SemaphoreType.DMA((4,)),
        ],
        moved=8 << 20,
        far_ins=2,
        far_outs=1,
    )(swept, links, arrived, all_cells)
    return fluid_out, solid_out


def solution(mesh):
    both = ("azim", "axial")
    in_specs = (
        P(None, "azim", "axial", None),
        P("azim", "axial", None),
        P(both),
        P(both),
        P(both),
        P(both),
        P(both),
        P("azim", "axial", None),
        P("azim", "axial", None),
    )
    out_specs = (P(None, "azim", "axial", None), P("azim", "axial", None))
    return jax.shard_map(
        functools.partial(per_device, mesh.shape["azim"], mesh.shape["axial"]),
        mesh=mesh,
        in_specs=in_specs,
        out_specs=out_specs,
        check_vma=False,
    )
```

```python
import functools

import jax
import jax.numpy as jnp
from jax import lax
from jax.experimental import pallas as pl
from jax.experimental.pallas import tpu as pltpu
from jax.sharding import PartitionSpec as P

CAP = 8
STEP_A = [0, 1, -1, 0, 0, 0, 0, 1, -1, 1, -1, 1, -1, 1, -1, 0, 0, 0, 0]
STEP_Z = [0, 0, 0, 1, -1, 0, 0, 1, -1, -1, 1, 0, 0, 0, 0, 1, -1, 1, -1]
STEP_R = [0, 0, 0, 0, 0, 1, -1, 0, 0, 0, 0, 1, -1, -1, 1, 1, -1, -1, 1]
OPPOSITE = [0, 2, 1, 4, 3, 6, 5, 8, 7, 10, 9, 12, 11, 14, 13, 16, 15, 18, 17]
AZIM_UP = [i for i in range(19) if STEP_A[i] == 1]
AZIM_DOWN = [i for i in range(19) if STEP_A[i] == -1]
AXIAL_UP = [i for i in range(19) if STEP_Z[i] == 1]
AXIAL_DOWN = [i for i in range(19) if STEP_Z[i] == -1]
RELAXATION = 1.25
SPEED_REF = 0.05
HEAT_CAPACITY = 6.5

Q = 19
CA, CZ, NR = 8, 16, 256
SA, SZ = 16, 16
HALVES = (0, 1)
ROWS = 32

PER_PLACE = 26
AXIAL_ROWS = CA * PER_PLACE
STREAMED_ROW = 100
SUMS_ROW = 190
FLAG_ROW = 244
AZIM_ROWS = 264
SOLID_COND = 48
SOLID_CELLS = 96
SOLID_ROWS = 104
SKIP = (0, 20, 38)
END_COND = 54
END_CELLS = 112
END_ROWS = 128

GROUP = 5

VMEM = pltpu.VMEM
f32 = jnp.float32
bf16 = jnp.bfloat16


def lanes(half):
    return pl.ds(128 * half, 128)


def moments(f):
    rho = f[0]
    for i in range(1, Q):
        rho = rho + f[i]
    d = [f[i] - f[i + 1] for i in range(1, Q, 2)]
    mom_a = d[0] + d[3] + d[4] + d[5] + d[6]
    mom_z = d[1] + d[3] - d[4] + d[7] + d[8]
    mom_r = d[2] + d[5] - d[6] + d[7] - d[8]
    return rho, mom_a, mom_z, mom_r


def collide_part(sums, f, flag, which):
    rho, mom_a, mom_z, mom_r = sums
    open_cell = flag > 0
    inv = 1.0 / jnp.where(open_cell, rho, 1.0)
    omega = jnp.where(open_cell, RELAXATION, 0.0)
    keep = 1.0 - omega
    ua, uz, ur = mom_a * inv, mom_z * inv, mom_r * inv
    base = 1.0 - 1.5 * (ua * ua + uz * uz + ur * ur)
    scale = omega * rho
    face, edge = scale * (1.0 / 18.0), scale * (1.0 / 36.0)
    post = {}
    if 0 in which:
        post[0] = keep * f[0] + scale * (1.0 / 3.0) * base
    for n, proj in enumerate(
        (ua, uz, ur, ua + uz, ua - uz, ua + ur, ua - ur, uz + ur, uz - ur)
    ):
        weight = face if n < 3 else edge
        one, two = 2 * n + 1, 2 * n + 2
        if one in which or two in which:
            even = weight * (base + 4.5 * proj * proj)
            odd = weight * (3.0 * proj)
        if one in which:
            post[one] = keep * f[one] + (even + odd)
        if two in which:
            post[two] = keep * f[two] + (even - odd)
    return post


def collide(f, flag):
    return collide_part(moments(f), f, flag, range(Q))


def conductivity(material):
    return jnp.where(
        material == 0,
        1.0,
        jnp.where(material == 1, 0.55, jnp.where(material == 2, 0.2, 0.8)),
    ).astype(f32)


def by_parity(axis, body, near, far):
    odd = lax.rem(lax.axis_index(axis), 2) == 1

    @pl.when(odd)
    def _():
        body(near, far)

    @pl.when(jnp.logical_not(odd))
    def _():
        body(far, near)


def first_kernel(
    f_far, flags_far, post, air, near, far, token, f, flags, low, high, come
):
    flags_copy = pltpu.make_async_copy(flags_far, flags, come.at[CA])

    def layer_copy(a):
        return pltpu.make_async_copy(f_far.at[:, a], f.at[:, a], come.at[a])

    flags_copy.start()
    for a in range(CA):
        layer_copy(a).start()
    token[...] = jnp.zeros((8, 128), f32)
    flags_copy.wait()

    def layer(a, carry):
        layer_copy(a).wait()
        for half in HALVES:
            for part in (0, 1):
                rows = pl.ds(8 * part, 8)
                flag = flags[a, rows, lanes(half)].astype(f32)
                out = collide([f[i, a, rows, lanes(half)] for i in range(Q)], flag)
                for i in range(Q):
                    post[i, a, half, rows, :] = out[i]
                air[a, half, rows, :] = flag
                place = a * PER_PLACE
                target, inner, edge, near_edge = (
                    (low, AXIAL_DOWN, 0, 1) if part == 0 else (high, AXIAL_UP, 7, 6)
                )

                def put(row, value, at):
                    target[half, pl.ds(place + row, 1), :] = value[at : at + 1]

                for i in range(Q):
                    put(i, out[i], edge)
                for n, i in enumerate(inner):
                    put(Q + n, out[i], near_edge)
                put(24, flag, edge)
                put(25, flag, near_edge)
        return carry

    lax.fori_loop(0, CA, layer, 0)

    def hand_over(down, up):
        down[...] = low[...]
        up[...] = high[...]

    by_parity("axial", hand_over, near, far)


def solid_azim_kernel(
    temp_far, mat_far, cells, token, near, far, packed, temp, mat, come
):
    packed[...] = jnp.zeros((8, 128), f32)
    copies = []
    for n, layers in enumerate((pl.ds(0, 3), pl.ds(SA - 3, 3))):
        for k, (source, target) in enumerate(((temp_far, temp), (mat_far, mat))):
            copy = pltpu.make_async_copy(
                source.at[layers], target.at[n], come.at[2 * n + k]
            )
            copy.start()
            copies.append(copy)
    for copy in copies:
        copy.wait()

    def fill(down, up):
        for side, target in enumerate((down, up)):
            for half in HALVES:
                for n in range(3):
                    a = n if side == 0 else 2 - n
                    target[half, pl.ds(16 * n, 16), :] = temp[side, a, :, lanes(half)]
                    target[half, pl.ds(SOLID_COND + 16 * n, 16), :] = conductivity(
                        mat[side, a, :, lanes(half)]
                    )
            target[0, pl.ds(SOLID_CELLS, 8), :] = cells[...].astype(f32)

    by_parity("azim", fill, near, far)


def solid_axial_kernel(
    temp_far,
    mat_far,
    cells,
    near_s,
    far_s,
    token,
    near,
    far,
    temp,
    mat,
    low,
    high,
    come,
):
    copies = [
        pltpu.make_async_copy(source, target, come.at[n])
        for n, (source, target) in enumerate(((temp_far, temp), (mat_far, mat)))
    ]
    for copy in copies:
        copy.start()

    def azim_ends(lower, upper):
        for target, edge, step in ((low, 0, 1), (high, SZ - 1, -1)):
            for half in HALVES:
                for depth in range(2):
                    z = edge + step * depth
                    for n in range(2 - depth):
                        for source, at in (
                            (lower, 1 - depth - n),
                            (upper, 18 - depth + n),
                        ):
                            for kind, here in ((0, 0), (END_COND, SOLID_COND)):
                                target[half, pl.ds(kind + SKIP[depth] + at, 1), :] = (
                                    source[half, pl.ds(here + 16 * n + z, 1), :]
                                )
            target[0, pl.ds(END_CELLS, 8), :] = cells[...].astype(f32)
            target[1, pl.ds(END_CELLS, 8), :] = lower[0, pl.ds(SOLID_CELLS, 8), :]
            target[0, pl.ds(END_CELLS + 8, 8), :] = upper[0, pl.ds(SOLID_CELLS, 8), :]

    by_parity("azim", azim_ends, near_s, far_s)
    for copy in copies:
        copy.wait()

    def layer(a, carry):
        for half in HALVES:
            for part, target in ((0, low), (1, high)):
                rows = pl.ds(8 * part, 8)
                t = temp[a, rows, lanes(half)]
                c = conductivity(mat[a, rows, lanes(half)])
                for depth in range(3):
                    at = depth if part == 0 else 7 - depth
                    row = SKIP[depth] + 2 - depth + a
                    target[half, pl.ds(row, 1), :] = t[at : at + 1]
                    target[half, pl.ds(END_COND + row, 1), :] = c[at : at + 1]
        return carry

    lax.fori_loop(0, SA, layer, 0, unroll=4)

    def hand_over(down, up):
        down[...] = low[...]
        up[...] = high[...]

    by_parity("axial", hand_over, near, far)


def ends(n_axial):
    z = lax.axis_index("axial")
    return (
        jnp.where(z > 0, 1.0, 0.0).astype(f32),
        jnp.where(z < n_axial - 1, 1.0, 0.0).astype(f32),
    )


def shifted(pair, step, lane):
    if step == 0:
        return pair
    turn = 1 if step == 1 else 127
    at = 0 if step == 1 else 127
    a, b = (pltpu.roll(x, turn, 1) for x in pair)
    return [jnp.where(lane == at, b, a), jnp.where(lane == at, a, b)]


def split(x):
    one = x.astype(bf16)
    return one, (x - one.astype(f32)).astype(bf16)


def stream(
    source,
    opened,
    at_a,
    flag_a,
    row,
    lane,
    which=None,
    sides=None,
    rim=None,
    beyond=False,
):
    rows = pl.ds(row, 8)
    out = [[], []]
    for i in range(Q) if which is None else which:
        own = OPPOSITE[i]
        from_rows = pl.ds(row - STEP_Z[i], 8)

        def before(half):
            if rim and i in rim:
                return sides[rim[i][0], rim[i][1], half, from_rows, :]
            if beyond:
                return source[i, at_a, half, from_rows, :]
            return source[i, at_a - STEP_A[i], half, from_rows, :]

        def back(half):
            if beyond:
                return sides[rim[own][0], rim[own][1], half, rows, :]
            return source[own, at_a, half, rows, :]

        moved = shifted([before(half) for half in HALVES], STEP_R[i], lane)
        for half in HALVES:
            if i == 0:
                out[half].append(moved[half])
                continue
            from_a = flag_a if beyond else flag_a - STEP_A[i]
            mask = opened[STEP_R[i] % 3, from_a, half, from_rows, :]
            out[half].append(jnp.where(mask > 0, moved[half], back(half)))
    return out


def rim_kernel(
    n_axial,
    post,
    air,
    near_z,
    far_z,
    packed,
    ext,
    opened,
    near,
    far,
    low,
    high,
):
    lane = lax.broadcasted_iota(jnp.int32, (8, 128), 1)
    below, above = ends(n_axial)

    def own_layer(a, carry):
        to = pl.ds(8, 16)
        for half in HALVES:
            for i in range(Q):
                ext[i, a, half, to, :] = post[i, a, half]
            opened[0, a, half, to, :] = air[a, half]
        return carry

    lax.fori_loop(0, CA, own_layer, 0, unroll=4)

    def axial_rim(lower, upper):
        def layer(a, carry):
            place = a * PER_PLACE
            for half in HALVES:
                for source, first, last, moving, there in (
                    (lower, 7, 6, AXIAL_UP, below),
                    (upper, 24, 25, AXIAL_DOWN, above),
                ):

                    def get(row):
                        return source[half, pl.ds(place + row, 1), :]

                    for i in range(Q):
                        ext[i, a, half, pl.ds(first, 1), :] = get(i)
                    for n, i in enumerate(moving):
                        ext[i, a, half, pl.ds(last, 1), :] = get(Q + n)
                    opened[0, a, half, pl.ds(first, 1), :] = get(24) * there
                    opened[0, a, half, pl.ds(last, 1), :] = get(25) * there
            return carry

        lax.fori_loop(0, CA, layer, 0, unroll=4)
    by_parity("axial", axial_rim, near_z, far_z)

    def turn(a, carry):
        turn_flags(opened, a, lane)
        return carry

    lax.fori_loop(0, CA, turn, 0, unroll=8)

    for target, layer, moving, step in (
        (low, 0, AZIM_DOWN, -1),
        (high, CA - 1, AZIM_UP, 1),
    ):
        for half in HALVES:
            for n, i in enumerate(moving):
                target[half, pl.ds(20 * n, 20), :] = ext[
                    i, layer, half, pl.ds(6, 20), :
                ]
            target[half, pl.ds(FLAG_ROW, 20), :] = opened[
                0, layer, half, pl.ds(6, 20), :
            ]
        which = [i for i in range(Q) if STEP_A[i] in (0, step)]
        for row in (7, 15, 17):
            moved = stream(ext, opened, layer, layer, row, lane, which)
            for half in HALVES:
                new = dict(zip(which, moved[half]))
                at = row - 7
                for n, i in enumerate(moving):
                    target[half, pl.ds(STREAMED_ROW + 18 * n + at, 8), :] = new[i]
                still = [i for i in which if STEP_A[i] == 0]
                for n, table in enumerate(([1] * Q, STEP_Z, STEP_R)):
                    total = None
                    for i in still:
                        if table[i]:
                            term = new[i] * table[i]
                            total = term if total is None else total + term
                    target[half, pl.ds(SUMS_ROW + 18 * n + at, 8), :] = total

    def hand_over(down, up):
        down[...] = low[...]
        up[...] = high[...]

    by_parity("azim", hand_over, near, far)


def turn_flags(opened, a, lane):
    for part in range(4):
        rows = pl.ds(8 * part, 8)
        pair = [opened[0, a, half, rows, :] for half in HALVES]
        up = shifted(pair, 1, lane)
        down = shifted(pair, -1, lane)
        opened[1, a, 0, rows, :] = jnp.where(lane == 0, 0.0, up[0])
        opened[1, a, 1, rows, :] = up[1]
        opened[2, a, 0, rows, :] = down[0]
        opened[2, a, 1, rows, :] = jnp.where(lane == 127, 0.0, down[1])


def step_two(second, opened, a, flag_a, lane, speeds, target, at):
    for part in (0, 1):
        moved = stream(second, opened, a + 1, flag_a, 8 + 8 * part, lane)
        for half in HALVES:
            for i in range(Q):
                target[i, at, pl.ds(8 * part, 8), lanes(half)] = moved[half][i]
            rho, mom_a, mom_z, mom_r = moments(moved[half])
            inv = 1.0 / rho
            ua, uz, ur = mom_a * inv, mom_z * inv, mom_r * inv
            speeds[pl.ds(a * CZ + 8 * part, 8), lanes(half)] = jnp.sqrt(
                ua * ua + uz * uz + ur * ur + 1e-06
            )


def inner_kernel(
    ext, opened, fluid_far, second, speeds, token, fluid_out, layers_out
):
    token[...] = jnp.zeros((8, 128), f32)
    lane = lax.broadcasted_iota(jnp.int32, (8, 128), 1)

    def first_step(a, carry):
        for row in (7, 15, 17):
            moved = stream(ext, opened, a, a, row, lane)
            for half in HALVES:
                out = collide(moved[half], opened[0, a, half, pl.ds(row, 8), :])
                for i in range(Q):
                    second[i, a + 1, half, pl.ds(row, 8), :] = out[i]
        return carry

    lax.fori_loop(1, CA - 1, first_step, 0)

    def layer_copy(n):
        return pltpu.make_async_copy(
            fluid_out.at[:, n], fluid_far.at[:, n + 2], layers_out.at[n]
        )

    def second_step(n, carry):
        step_two(second, opened, n + 2, n + 2, lane, speeds, fluid_out, n)
        layer_copy(n).start()
        return carry

    lax.fori_loop(0, CA - 4, second_step, 0)
    for n in range(CA - 4):
        layer_copy(n).wait()


def outer_kernel(
    n_azim,
    n_axial,
    fluid_so_far,
    second_so_far,
    inner_speeds,
    ext,
    own_opened,
    near_a,
    far_a,
    cell,
    drive,
    owner,
    slot,
    fluid_far,
    second,
    message,
    opened,
    sides,
    speeds,
    fluid_out,
    layers_out,
):
    lane = lax.broadcasted_iota(jnp.int32, (8, 128), 1)
    inside = pl.ds(2 * CZ, (CA - 4) * CZ)
    speeds[inside, :] = inner_speeds[inside, :]

    def own_flags(a, carry):
        for k in range(3):
            for half in HALVES:
                opened[k, a + 1, half] = own_opened[k, a, half]
        return carry

    lax.fori_loop(0, CA, own_flags, 0, unroll=8)

    def azim_rim(lower, upper):
        for side, (source, a) in enumerate(((lower, 0), (upper, CA + 1))):
            for half in HALVES:
                for n in range(5):
                    sides[side, n, half, pl.ds(6, 20), :] = source[
                        half, pl.ds(20 * n, 20), :
                    ]
                for n in range(8):
                    sides[side, 5 + n, half, pl.ds(7, 18), :] = source[
                        half, pl.ds(STREAMED_ROW + 18 * n, 18), :
                    ]
                opened[0, a, half, pl.ds(6, 20), :] = source[
                    half, pl.ds(FLAG_ROW, 20), :
                ]

    by_parity("azim", azim_rim, near_a, far_a)
    turn_flags(opened, 0, lane)
    turn_flags(opened, CA + 1, lane)

    def finish(a, row, moved):
        for half in HALVES:
            out = collide(moved[half], opened[0, a + 1, half, pl.ds(row, 8), :])
            for i in range(Q):
                second[i, a + 1, half, pl.ds(row, 8), :] = out[i]

    def layer_copy(n, a):
        return pltpu.make_async_copy(
            fluid_out.at[:, n], fluid_far.at[:, a], layers_out.at[n]
        )

    for side, (a, inward, outward) in enumerate(
        ((0, AZIM_UP, AZIM_DOWN), (CA - 1, AZIM_DOWN, AZIM_UP))
    ):
        rim = {i: (side, n) for n, i in enumerate(inward)}
        beyond = 0 if side == 0 else CA + 1

        def edge_step(n, carry):
            row = 7 + 8 * n
            finish(a, row, stream(ext, opened, a, a + 1, row, lane, None, sides, rim))
            far_in = stream(
                ext, opened, a, a + 1, row, lane, outward, sides, rim, beyond=True
            )
            for half in HALVES:
                rows = pl.ds(row, 8)

                def at(n):
                    return sides[side, n, half, rows, :]

                new = {i: at(5 + n) for n, i in enumerate(inward)}
                new.update(zip(outward, far_in[half]))
                sums = [at(10), None, at(11), at(12)]
                for k, table in enumerate(([1] * Q, STEP_A, STEP_Z, STEP_R)):
                    for i in inward + outward:
                        if table[i]:
                            term = new[i] * table[i]
                            sums[k] = term if sums[k] is None else sums[k] + term
                out = collide_part(
                    sums, new, opened[0, beyond, half, rows, :], inward
                )
                for i in inward:
                    second[i, beyond, half, rows, :] = out[i]
            return carry

        lax.fori_loop(0, 3, edge_step, 0)

        def second_step(n, carry):
            layer = n + side * (CA - 2)
            at = n + 2 * side
            step_two(second, opened, layer, layer + 1, lane, speeds, fluid_out, at)
            layer_copy(at, layer).start()
            return carry

        lax.fori_loop(0, 2, second_step, 0, unroll=2)


    rows_here = cell.shape[1]
    place = cell[...]
    row_hot = (
        lax.broadcasted_iota(jnp.int32, (CA * CZ, rows_here), 0) == place // NR
    ).astype(f32).astype(bf16)
    turned = jnp.transpose(speeds[...])
    picked = jnp.zeros((NR, rows_here), f32)
    for term in split(turned):
        picked = picked + jnp.dot(term, row_hot, preferred_element_type=f32)
    column = lax.broadcasted_iota(jnp.int32, (NR, rows_here), 0) == place % NR
    speed = jnp.sum(jnp.where(column, picked, 0.0), axis=0, keepdims=True)
    flux = drive[...] * (0.2 + speed / SPEED_REF)
    devices = n_azim * n_axial
    owner_hot = (
        lax.broadcasted_iota(jnp.int32, (devices, rows_here), 0) == owner[...]
    ).astype(f32).astype(bf16)
    slotted = jnp.where(
        lax.broadcasted_iota(jnp.int32, (128, rows_here), 0) == slot[...], flux, 0.0
    )
    sent = jnp.zeros((devices, 128), f32)
    for term in split(slotted):
        sent = sent + lax.dot_general(
            owner_hot, term, (((1,), (1,)), ((), ())), preferred_element_type=f32
        )
    total = jnp.zeros((devices, 128), f32)
    for da in (-1, 0, 1):
        for dz in (-1, 0, 1):
            which = (da + 1) * 3 + dz + 1
            back = (-(da * n_axial + dz)) % devices
            moved = pltpu.roll(sent, back, 0) if back else sent
            total = total + (pltpu.roll(moved, CAP * which, 1) if which else moved)
    for o in range(devices):
        message[o, :, :] = total[o : o + 1]
    for n, a in enumerate((0, 1, CA - 2, CA - 1)):
        layer_copy(n, a).wait()


def link(first, second):
    joined = first + second
    good = joined > 0
    return jnp.where(
        good,
        (2.0 / HEAT_CAPACITY) * first * second / jnp.where(good, joined, 1.0),
        0.0,
    )


def sweep(source, link_a, link_z, link_r, keep, a, row, lane):
    rows = pl.ds(row, 8)
    pair = [source[a, half, rows, :] for half in HALVES]
    lr = [link_r[a, half, rows, :] for half in HALVES]
    up = shifted(pair, -1, lane)
    down = shifted([x * y for x, y in zip(pair, lr)], 1, lane)
    out = []
    for half in HALVES:
        total = keep[a, half, rows, :] * pair[half]
        total = total + link_a[a, half, rows, :] * source[a + 1, half, rows, :]
        total = total + link_a[a - 1, half, rows, :] * source[a - 1, half, rows, :]
        total = (
            total + link_z[a, half, rows, :] * source[a, half, pl.ds(row + 1, 8), :]
        )
        total = (
            total
            + link_z[a, half, pl.ds(row - 1, 8), :]
            * source[a, half, pl.ds(row - 1, 8), :]
        )
        out.append(total + lr[half] * up[half] + down[half])
    return out


def solid_kernel(
    n_axial,
    temp_far,
    mat_far,
    near_s,
    far_s,
    near_e,
    far_e,
    cells,
    swept,
    links_out,
    all_cells,
    link_a,
    link_z,
    link_r,
    keep,
    ext,
    cond,
    other,
    temp,
    mat,
    come,
):
    copies = [
        pltpu.make_async_copy(source, target, come.at[n])
        for n, (source, target) in enumerate(((temp_far, temp), (mat_far, mat)))
    ]
    for copy in copies:
        copy.start()
    for copy in copies:
        copy.wait()
    lane = lax.broadcasted_iota(jnp.int32, (8, 128), 1)

    def own_layer(a, carry):
        for half in HALVES:
            for part in (0, 1):
                rows = pl.ds(8 * part, 8)
                to = pl.ds(8 + 8 * part, 8)
                ext[a + 3, half, to, :] = temp[a, rows, lanes(half)]
                cond[a + 3, half, to, :] = conductivity(mat[a, rows, lanes(half)])
        return carry

    lax.fori_loop(0, SA, own_layer, 0, unroll=4)

    def azim_rim(lower, upper):
        for half in HALVES:
            for n in range(3):
                for source, a in ((lower, 2 - n), (upper, 19 + n)):
                    ext[a, half, pl.ds(8, 16), :] = source[half, pl.ds(16 * n, 16), :]
                    cond[a, half, pl.ds(8, 16), :] = source[
                        half, pl.ds(SOLID_COND + 16 * n, 16), :
                    ]
        all_cells[1] = lower[0, pl.ds(SOLID_CELLS, 8), :]
        all_cells[7] = upper[0, pl.ds(SOLID_CELLS, 8), :]

    by_parity("azim", azim_rim, near_s, far_s)
    below, above = ends(n_axial)

    def axial_rim(lower, upper):
        for half in HALVES:
            for depth in range(3):
                for n in range(20 - 2 * depth):
                    a = 1 + depth + n
                    at = SKIP[depth] + n
                    for source, row, there in (
                        (lower, 7 - depth, below),
                        (upper, 24 + depth, above),
                    ):
                        ext[a, half, pl.ds(row, 1), :] = source[half, pl.ds(at, 1), :]
                        cond[a, half, pl.ds(row, 1), :] = (
                            source[half, pl.ds(END_COND + at, 1), :] * there
                        )
        outside = jnp.full((CAP, 128), SA * SZ * NR, f32)
        for source, dz, there in ((lower, 0, below), (upper, 2, above)):
            for which, half, row in ((0, 1, 0), (3, 0, 0), (6, 0, 8)):
                all_cells[which + dz] = jnp.where(
                    there > 0, source[half, pl.ds(END_CELLS + row, 8), :], outside
                )

    by_parity("axial", axial_rim, near_e, far_e)
    all_cells[4] = cells[...].astype(f32)

    def links(a, carry):
        for row in (5, 13, 21):
            rows = pl.ds(row, 8)
            pair = [cond[a, half, rows, :] for half in HALVES]
            up = shifted(pair, -1, lane)
            up = [up[0], jnp.where(lane == 127, 0.0, up[1])]
            for half in HALVES:
                link_a[a, half, rows, :] = link(pair[half], cond[a + 1, half, rows, :])
                link_z[a, half, rows, :] = link(
                    pair[half], cond[a, half, pl.ds(row + 1, 8), :]
                )
                link_r[a, half, rows, :] = link(pair[half], up[half])
        return carry

    lax.fori_loop(0, SA + 5, links, 0, unroll=3)

    def keeps(a, carry):
        for row in (6, 14, 22):
            rows = pl.ds(row, 8)
            pair = [link_r[a, half, rows, :] for half in HALVES]
            down = shifted(pair, 1, lane)
            for half in HALVES:
                keep[a, half, rows, :] = 1.0 - (
                    link_a[a, half, rows, :]
                    + link_a[a - 1, half, rows, :]
                    + link_z[a, half, rows, :]
                    + link_z[a, half, pl.ds(row - 1, 8), :]
                    + pair[half]
                    + down[half]
                )
        return carry

    lax.fori_loop(1, SA + 5, keeps, 0, unroll=4)

    def trim(a, carry):
        for half in HALVES:
            for n, kind in enumerate((link_a, link_z, link_r)):
                links_out[n, a, half] = kind[a + 1, half, pl.ds(6, 24), :]
        return carry

    lax.fori_loop(0, SA + 4, trim, 0, unroll=2)

    def once(source, target, first, last, at):
        def layer(a, carry):
            for row in at:
                out = sweep(source, link_a, link_z, link_r, keep, a, row, lane)
                for half in HALVES:
                    target[a, half, pl.ds(row, 8), :] = out[half]
            return carry

        lax.fori_loop(first, last, layer, 0, unroll=2)

    once(ext, other, 1, SA + 5, (6, 14, 22))
    once(other, ext, 2, SA + 4, (7, 15, 23))

    def final(a, carry):
        for part in (0, 1):
            out = sweep(ext, link_a, link_z, link_r, keep, a + 3, 8 + 8 * part, lane)
            for half in HALVES:
                swept[a, pl.ds(8 * part, 8), lanes(half)] = out[half]
        return carry

    lax.fori_loop(0, SA, final, 0, unroll=4)


def deposit_kernel(
    swept_far,
    links_far,
    arrived,
    all_cells,
    solid_far,
    heat,
    other,
    came,
    swept,
    links,
    solid_out,
    brought,
    taken,
):
    groups = [
        pltpu.make_async_copy(
            links_far.at[:, pl.ds(GROUP * n, GROUP)],
            links.at[:, pl.ds(GROUP * n, GROUP)],
            brought.at[n],
        )
        for n in range((SA + 4) // GROUP)
    ]
    swept_copy = pltpu.make_async_copy(swept_far, swept, brought.at[len(groups)])
    for copy in groups:
        copy.start()
    swept_copy.start()
    lane = lax.broadcasted_iota(jnp.int32, (8, 128), 1)
    senders = arrived.shape[0]
    for s in range(senders):
        came[pl.ds(s, 1), :] = arrived[s]

    def clear(a, carry):
        for half in HALVES:
            heat[a, half] = jnp.zeros((24, 128), f32)
        return carry

    lax.fori_loop(0, SA + 4, clear, 0, unroll=2)
    values = jnp.transpose(came[...]) * (1.0 / HEAT_CAPACITY)

    def place(which, rows, row_of):
        cell = all_cells[which].astype(jnp.int32)
        value = values[CAP * which : CAP * (which + 1)]
        one, two = split(value)
        at_row = row_of(lax.broadcasted_iota(jnp.int32, (rows, senders), 0))
        at_col = lax.broadcasted_iota(jnp.int32, (NR, senders), 0)
        left, right = [[], []], []
        for c in range(CAP):
            hit = at_row == (cell[c : c + 1] // NR)
            for to, term in zip(left, (one, two)):
                to.append(
                    jnp.where(hit, term[c : c + 1].astype(f32), 0.0).astype(bf16)
                )
            right.append((at_col == cell[c : c + 1] % NR).astype(f32).astype(bf16))
        both = lax.dot_general(
            jnp.concatenate([jnp.concatenate(to, axis=1) for to in left], axis=0),
            jnp.concatenate(right, axis=1),
            (((1,), (1,)), ((), ())),
            preferred_element_type=f32,
        )
        return both[:rows] + both[rows:]

    own = place(4, SA * SZ, lambda j: j)
    for a in range(SA):
        for half in HALVES:
            heat[a + 2, half, pl.ds(2, 16), :] = own[
                16 * a : 16 * a + 16, 128 * half : 128 * half + 128
            ]
    low = place(1, 32, lambda j: j + 14 * SZ)
    high = place(7, 32, lambda j: j)
    for n in range(2):
        for half in HALVES:
            cut = slice(128 * half, 128 * half + 128)
            heat[n, half, pl.ds(2, 16), :] = low[16 * n : 16 * n + 16, cut]
            heat[18 + n, half, pl.ds(2, 16), :] = high[16 * n : 16 * n + 16, cut]
    low = place(3, 32, lambda j: (j // 2) * SZ + 14 + j % 2)
    high = place(5, 32, lambda j: (j // 2) * SZ + j % 2)
    for a in range(SA):
        for half in HALVES:
            cut = slice(128 * half, 128 * half + 128)
            heat[a + 2, half, pl.ds(0, 2), :] = low[2 * a : 2 * a + 2, cut]
            heat[a + 2, half, pl.ds(18, 2), :] = high[2 * a : 2 * a + 2, cut]
    for which, cell_row, a, row in (
        (0, 255, 1, 1),
        (2, 240, 1, 18),
        (6, 15, 18, 1),
        (8, 0, 18, 18),
    ):
        one = place(which, 8, lambda j: jnp.where(j == 0, cell_row, -1))
        for half in HALVES:
            heat[a, half, pl.ds(row, 1), :] = one[0:1, 128 * half : 128 * half + 128]

    def spread(source, a, row):
        rows, before, after = (pl.ds(row + n, 8) for n in (0, -1, 1))
        pair = [source[a, half, rows, :] for half in HALVES]
        up = shifted(pair, -1, lane)
        flow = [links[2, a, half, rows, :] * (up[half] - pair[half]) for half in HALVES]
        back = shifted(flow, 1, lane)
        out = []
        for half in HALVES:
            here = pair[half]
            out.append(
                here
                + links[0, a, half, rows, :] * (source[a + 1, half, rows, :] - here)
                + links[0, a - 1, half, rows, :] * (source[a - 1, half, rows, :] - here)
                + links[1, a, half, rows, :] * (source[a, half, after, :] - here)
                + links[1, a, half, before, :] * (source[a, half, before, :] - here)
                + (flow[half] - back[half])
                + heat[a, half, rows, :]
            )
        return out

    def middle(a, carry):
        for row in (1, 9, 11):
            out = spread(heat, a, row)
            for half in HALVES:
                other[a, half, pl.ds(row, 8), :] = out[half]
        return carry

    for n, copy in enumerate(groups):
        copy.wait()
        first = max(GROUP * n, 1)
        last = min(GROUP * (n + 1), SA + 3)
        lax.fori_loop(first, last, middle, 0, unroll=last - first)
    swept_copy.wait()

    def final(a, carry):
        for part in (0, 1):
            rows = pl.ds(8 * part, 8)
            out = spread(other, a + 2, 2 + 8 * part)
            for half in HALVES:
                solid_out[a, rows, lanes(half)] = (
                    out[half] + swept[a, rows, lanes(half)]
                )
        return carry

    quarters = []
    for n in range(4):
        at = pl.ds(4 * n, 4)
        lax.fori_loop(4 * n, 4 * n + 4, final, 0, unroll=4)
        quarters.append(
            pltpu.make_async_copy(solid_out.at[at], solid_far.at[at], taken.at[n])
        )
        quarters[-1].start()
    for copy in quarters:
        copy.wait()


def call(
    kernel, ins, outs, scratch=(), limit=16, moved=0, far_ins=0, far_outs=0, held=(), aliases={}
):
    here, there = (pl.BlockSpec(memory_space=m) for m in (VMEM, pltpu.HBM))
    kernel_call = pl.pallas_call(
        kernel,
        out_shape=[
            VMEM(s, f32) if n in held else jax.ShapeDtypeStruct(s, f32)
            for n, s in enumerate(outs)
        ],
        in_specs=[there] * far_ins + [here] * (ins - far_ins),
        out_specs=[there] * far_outs + [here] * (len(outs) - far_outs),
        scratch_shapes=list(scratch),
        input_output_aliases=aliases,
        compiler_params=pltpu.CompilerParams(vmem_limit_bytes=limit * 1024 * 1024),
        cost_estimate=pl.CostEstimate(
            flops=0, bytes_accessed=moved, transcendentals=0
        ),
    )

    def run(*args):
        far = [pltpu.with_memory_space_constraint(x, pltpu.HBM) for x in args[:far_ins]]
        return kernel_call(*far, *args[far_ins:])

    return run


def swap(values, axis, far):
    count = lax.axis_size(axis)
    pairs = [(i, (((i + 1) ^ 1) - 1) % count if far else i ^ 1) for i in range(count)]
    if axis == "axial" and far:
        pairs[0], pairs[-1] = (0, 0), (count - 1, count - 1)
    return lax.ppermute(values, axis, pairs)


def per_device(
    n_azim,
    n_axial,
    populations,
    fluid_flags,
    wall_cell,
    wall_drive,
    wall_owner,
    wall_slot,
    receive_cell,
    materials,
    solid_temp,
):
    devices = n_azim * n_axial
    cells = receive_cell.reshape(devices, CAP).T
    azim_msg = (2, AZIM_ROWS, 128)
    axial_msg = (2, AXIAL_ROWS, 128)
    solid_msg = (2, SOLID_ROWS, 128)
    end_msg = (2, END_ROWS, 128)
    fluid = (Q, CA, CZ, NR)
    solid = (SA, SZ, NR)
    fluid_ext = (Q, CA, 2, ROWS, 128)
    solid_ext = (SA + 6, 2, ROWS, 128)
    opened_ext = (3, CA, 2, ROWS, 128)
    post, air, near_z, far_z, token = call(
        first_kernel,
        2,
        [(Q, CA, 2, CZ, 128), (CA, 2, CZ, 128), axial_msg, axial_msg, (8, 128)],
        [
            VMEM(fluid, f32),
            VMEM((CA, CZ, NR), jnp.int32),
            VMEM(axial_msg, f32),
            VMEM(axial_msg, f32),
            pltpu.SemaphoreType.DMA((CA + 1,)),
        ],
        moved=8 << 20,
        far_ins=2,
        held=(0, 1, 2, 3),
    )(populations, fluid_flags)
    near_z = swap(near_z, "axial", False)
    far_z = swap(far_z, "axial", True)
    near_s, far_s, packed = call(
        solid_azim_kernel,
        4,
        [solid_msg, solid_msg, (8, 128)],
        [
            VMEM((2, 3, SZ, NR), f32),
            VMEM((2, 3, SZ, NR), jnp.int32),
            pltpu.SemaphoreType.DMA((4,)),
        ],
        moved=2 << 20,
        far_ins=2,
    )(solid_temp, materials, cells, token)
    near_s = swap(near_s, "azim", False)
    far_s = swap(far_s, "azim", True)
    near_z, far_z, near_s, far_s = lax.optimization_barrier(
        (near_z, far_z, near_s, far_s)
    )
    ext, opened, near_a, far_a = call(
        functools.partial(rim_kernel, n_axial),
        5,
        [fluid_ext, opened_ext, azim_msg, azim_msg],
        [VMEM(azim_msg, f32), VMEM(azim_msg, f32)],
        moved=8 << 20,
        held=(0, 1),
    )(post, air, near_z, far_z, packed)
    near_a = swap(near_a, "azim", False)
    far_a = swap(far_a, "azim", True)
    rows = wall_cell.shape[0]
    ext, opened = (pltpu.with_memory_space_constraint(x, VMEM) for x in (ext, opened))
    fluid_out, second, speeds, token = call(
        inner_kernel,
        2,
        [fluid, (Q, CA + 2, 2, ROWS, 128), (CA * CZ, NR), (8, 128)],
        [VMEM((Q, CA - 4, CZ, NR), f32), pltpu.SemaphoreType.DMA((CA - 4,))],
        moved=12 << 20,
        far_outs=1,
        held=(1, 2),
    )(ext, opened)
    near_e, far_e = call(
        solid_axial_kernel,
        6,
        [end_msg, end_msg],
        [
            VMEM(solid, f32),
            VMEM(solid, jnp.int32),
            VMEM(end_msg, f32),
            VMEM(end_msg, f32),
            pltpu.SemaphoreType.DMA((2,)),
        ],
        moved=2 << 20,
        far_ins=2,
    )(solid_temp, materials, cells, near_s, far_s, token)
    near_e = swap(near_e, "axial", False)
    far_e = swap(far_e, "axial", True)
    fluid_out, _, message = call(
        functools.partial(outer_kernel, n_azim, n_axial),
        11,
        [fluid, (Q, CA + 2, 2, ROWS, 128), (devices, 1, 128)],
        [
            VMEM((3, CA + 2, 2, ROWS, 128), f32),
            VMEM((2, 13, 2, ROWS, 128), f32),
            VMEM((CA * CZ, NR), f32),
            VMEM((Q, 4, CZ, NR), f32),
            pltpu.SemaphoreType.DMA((4,)),
        ],
        moved=8 << 20,
        far_ins=1,
        far_outs=1,
        held=(1,),
        aliases={0: 0, 1: 1},
    )(
        fluid_out,
        pltpu.with_memory_space_constraint(second, VMEM),
        pltpu.with_memory_space_constraint(speeds, VMEM),
        ext,
        opened,
        near_a,
        far_a,
        wall_cell.reshape(1, rows),
        wall_drive.reshape(1, rows),
        wall_owner.reshape(1, rows),
        wall_slot.reshape(1, rows),
    )
    arrived = lax.all_to_all(
        message, ("azim", "axial"), split_axis=0, concat_axis=0, tiled=True
    )
    link_shape = (3, SA + 4, 2, 24, 128)
    swept, links, all_cells = call(
        functools.partial(solid_kernel, n_axial),
        7,
        [solid, link_shape, (9, CAP, devices)],
        [VMEM(solid_ext, f32)] * 7
        + [
            VMEM(solid, f32),
            VMEM(solid, jnp.int32),
            pltpu.SemaphoreType.DMA((2,)),
        ],
        moved=8 << 20,
        far_ins=2,
    )(solid_temp, materials, near_s, far_s, near_e, far_e, cells)
    (solid_out,) = call(
        deposit_kernel,
        4,
        [solid],
        [
            VMEM(link_shape[1:], f32),
            VMEM(link_shape[1:], f32),
            VMEM((devices, 128), f32),
            VMEM(solid, f32),
            VMEM(link_shape, f32),
            VMEM(solid, f32),
            pltpu.SemaphoreType.DMA((5,)),
            pltpu.SemaphoreType.DMA((4,)),
        ],
        moved=8 << 20,
        far_ins=2,
        far_outs=1,
    )(swept, links, arrived, all_cells)
    return fluid_out, solid_out


def solution(mesh):
    both = ("azim", "axial")
    in_specs = (
        P(None, "azim", "axial", None),
        P("azim", "axial", None),
        P(both),
        P(both),
        P(both),
        P(both),
        P(both),
        P("azim", "axial", None),
        P("azim", "axial", None),
    )
    out_specs = (P(None, "azim", "axial", None), P("azim", "axial", None))
    return jax.shard_map(
        functools.partial(per_device, mesh.shape["azim"], mesh.shape["axial"]),
        mesh=mesh,
        in_specs=in_specs,
        out_specs=out_specs,
        check_vma=False,
    )
```
